128 devices in a mesh: dp: 8 (over z, core), expert: 16 (over y, x).
Axes of the slice: x: 4, y: 4, z: 4, core: 2. Of those that a mesh axis runs over, the one named last changes fastest.
Arguments:
- tokens: bfloat16 [128, 2, 64, 1280], P(('dp', 'expert')), may hold values from -6 to 6
- expert_ids: int32 [128, 2, 64], P(('dp', 'expert')), may hold values from 0 to 31, as said below
- slots: int32 [128, 2, 64], P(('dp', 'expert')), may hold values from 0 to 5, as said below
- ln_gain: float32 [1280], replicated, may hold values from 0.5 to 1.5
- w_in: bfloat16 [32, 1280, 5120], P('expert', None, 'dp'), may hold values from -0.15625 to 0.15625
- w_out: bfloat16 [32, 5120, 1280], P('expert', 'dp'), may hold values from -0.078125 to 0.078125
Outputs:
- grad_tokens: bfloat16 [128, 2, 64, 1280], P(('dp', 'expert'))
- grad_w_in: float32 [32, 1280, 5120], P('expert', None, 'dp')
- grad_w_out: float32 [32, 5120, 1280], P('expert', 'dp')
The draws below stay inside these ranges and needn't reach their ends.
Inputs may be any that keep to these rules, and one draw needn't show every extreme that they name: `expert_ids`: within each block of 128 tokens of one device, no expert is named more than 6 times, and in every draw one expert is named exactly 6 times in every block. Within each block, the tokens of one expert have distinct slots.
All inputs are finite; a program needn't handle non-finite values.
Results may differ from the reference program's by a relative error of at most 0.019.
Values may be sent and summed in bfloat16 or wider, within the bound.
No kernel may reach another device: no remote copies, remote signals or barrier semaphores. Data moves between devices by JAX's collectives and lax.ppermute only.
A program may use at most 128 MiB of HBM per device.

```python
import math
import jax
import jax.numpy as jnp
from jax import lax

D = 1280
H = 5120
TOK = 64
PAIRS_DEV = 1
EXPERT_TOTAL = 32
PAIRS = 128
CAP = 6
N_DP = 8


def route_table(key):
    block_count = PAIRS // PAIRS_DEV
    row_count = 2 * PAIRS_DEV * TOK
    others = (EXPERT_TOTAL - 1) * CAP
    key_favoured, key_boost, key_jitter, key_shuffle = jax.random.split(key, 4)
    hot_expert_id = jax.random.randint(key_favoured, (), 0, EXPERT_TOTAL)
    slot_position = jnp.arange(others, dtype=jnp.int32)
    second_expert = slot_position // CAP
    second_expert = second_expert + (second_expert >= hot_expert_id).astype(jnp.int32)
    other_slot = slot_position % CAP
    expert_boost = jax.random.randint(key_boost, (EXPERT_TOTAL,), 0, 1024)
    row_jitter = jax.random.randint(key_jitter, (block_count, others), 0, 1024)
    slot_rating = (row_jitter + expert_boost[second_expert][None, :]) * 4096 + slot_position[None, :]
    top_values, picked = lax.top_k(slot_rating, row_count - CAP)
    hot_column = jnp.full((block_count, CAP), hot_expert_id, jnp.int32)
    hot_slots = jnp.broadcast_to(jnp.arange(CAP, dtype=jnp.int32)[None, :], (block_count, CAP))
    all_expert = jnp.concatenate([hot_column, second_expert[picked]], axis=1)
    all_slot = jnp.concatenate([hot_slots, other_slot[picked]], axis=1)
    row_order = jax.vmap(lambda sub_key: jax.random.permutation(sub_key, row_count))(jax.random.split(key_shuffle, block_count))
    expert_table = jnp.take_along_axis(all_expert, row_order, axis=1).reshape(PAIRS, 2, TOK)
    slot_table = jnp.take_along_axis(all_slot, row_order, axis=1).reshape(PAIRS, 2, TOK)
    return (expert_table.astype(jnp.int32), slot_table.astype(jnp.int32))


def draw_expert_ids(key, part):
    expert_table, slot_table = route_table(key)
    return expert_table


def draw_slots(key, part):
    expert_table, slot_table = route_table(key)
    return slot_table


def draw_tokens(key, part):
    key = jax.random.fold_in(key, 7)
    key_base = jax.random.fold_in(key, 0)
    values = jnp.clip(jax.random.normal(key_base, (PAIRS, 2, TOK, D), jnp.float32), -6.0, 6.0)
    return values.astype(jnp.bfloat16)


def steps_of(stream_key, dims, shards, least, largest):
    loudness, own = 1.0, jax.random.fold_in(stream_key, 6)
    for position, parts in shards:
        heights = jnp.exp(jax.random.uniform(jax.random.fold_in(own, position), (parts,), jnp.float32, least / len(shards), largest / len(shards)))
        loudness = loudness * jnp.repeat(heights, dims[position] // parts).reshape([-1 if axis == position else 1 for axis in range(len(dims))])
    return loudness


def noise(own_key, shape, deviation, limit, shards=(), held_as=jnp.bfloat16):
    drawn = jax.random.normal(own_key, shape, jnp.float32) * deviation
    if len(shards) > 0:
        drawn = steps_of(own_key, shape, shards, -0.22, 0.18) * drawn
    return jnp.clip(drawn, min=-limit, max=limit).astype(held_as)


def setup_inputs(seed: int = 0) -> dict:
    splits = jax.random.split(jax.random.key(seed), 7)
    tokens = draw_tokens(jax.random.fold_in(splits[6], 71), 0)
    expert_ids = draw_expert_ids(jax.random.fold_in(splits[6], 71), 0)
    slots = draw_slots(jax.random.fold_in(splits[6], 71), 0)
    ln_gain = jnp.clip(1.0 + 0.1 * jax.random.normal(splits[3], (D,), jnp.float32), 0.5, 1.5)
    w_in = noise(splits[4], (EXPERT_TOTAL, D, H), D ** -0.5, 0.15625, ((0, 16), (2, 8)))
    w_out = noise(splits[5], (EXPERT_TOTAL, H, D), H ** -0.5, 0.078125, ((0, 16), (1, 8)))
    return dict(tokens=tokens, expert_ids=expert_ids, slots=slots, ln_gain=ln_gain, w_in=w_in, w_out=w_out)


norm_eps = 1e-06
objective_scale = 32.0

def layer_norm(values, gain_vector):
    centred = values - lax.optimization_barrier(jnp.mean(values, axis=-1, keepdims=True))
    spread = lax.optimization_barrier(jnp.mean(centred * centred, axis=-1, keepdims=True))
    return centred * lax.rsqrt(spread + norm_eps) * gain_vector

def gelu_tanh(values):
    return jax.nn.gelu(values, approximate=True)

def block_sum(block_terms):
    rounded = lax.optimization_barrier(block_terms.astype(jnp.bfloat16))
    return lax.optimization_barrier(jnp.sum(rounded.astype(jnp.float32), axis=0)).astype(jnp.bfloat16)

def reference(tokens, expert_ids, slots, ln_gain, w_in, w_out):
    block_count = PAIRS // PAIRS_DEV
    row_count = 2 * PAIRS_DEV * TOK
    hidden_block = H // N_DP
    flat_tokens = tokens.reshape(block_count, row_count, D).astype(jnp.float32)
    chosen = expert_ids.reshape(block_count, row_count).astype(jnp.int32)
    slot_place = slots.reshape(block_count, row_count).astype(jnp.int32)
    anchor = jnp.broadcast_to(jnp.arange(block_count, dtype=jnp.int32)[:, None], (block_count, row_count))
    normed_full, norm_back = jax.vjp(lambda values: layer_norm(values, ln_gain), flat_tokens)
    normed = normed_full.astype(jnp.bfloat16)

    def dispatch(values):
        buffer = jnp.zeros((EXPERT_TOTAL, block_count, CAP, D), jnp.bfloat16).at[chosen, anchor, slot_place].set(values)
        return buffer.reshape(EXPERT_TOTAL, block_count * CAP, D)

    def forward_expert(operands):
        rows_in, weight_in, weight_out = operands
        pre_act = jnp.dot(rows_in, weight_in, preferred_element_type=jnp.float32)
        activation = gelu_tanh(pre_act).astype(jnp.bfloat16)
        split_act = activation.reshape(-1, N_DP, hidden_block).astype(jnp.float32)
        split_out = weight_out.reshape(N_DP, hidden_block, D).astype(jnp.float32)
        return block_sum(jnp.einsum('mkh,khd->kmd', split_act, split_out))
    dispatched = dispatch(normed)
    expert_out = lax.map(forward_expert, (dispatched, w_in, w_out))
    combined = expert_out.reshape(EXPERT_TOTAL, block_count, CAP, D)[chosen, anchor, slot_place]
    mixed_rows = flat_tokens + combined.astype(jnp.float32)
    pooled = lax.optimization_barrier(jnp.mean(mixed_rows.reshape(PAIRS, 2, TOK, D), axis=2))
    image_emb = pooled[:, 0]
    text_emb = pooled[:, 1]
    logit_scale = TOK / math.sqrt(D)
    logits = logit_scale * jnp.dot(image_emb, text_emb.T, precision=lax.Precision.HIGHEST)
    identity = jnp.eye(PAIRS, dtype=jnp.float32)
    grad_logits = objective_scale * (jax.nn.softmax(logits, axis=1) + jax.nn.softmax(logits, axis=0) - 2.0 * identity)
    grad_image = logit_scale * jnp.dot(grad_logits, text_emb, precision=lax.Precision.HIGHEST)
    grad_text = logit_scale * jnp.dot(grad_logits.T, image_emb, precision=lax.Precision.HIGHEST)
    grad_pooled = jnp.stack([grad_image, grad_text], axis=1) / TOK
    grad_mixed = jnp.broadcast_to(grad_pooled[:, :, None, :], (PAIRS, 2, TOK, D)).reshape(block_count, row_count, D)
    grad_sent = grad_mixed.astype(jnp.bfloat16)
    grad_dispatched = dispatch(grad_sent)

    def backward_expert(operands):
        rows_in, grad_rows, weight_in, weight_out = operands
        pre_act = jnp.dot(rows_in, weight_in, preferred_element_type=jnp.float32)
        act_full, gelu_back = jax.vjp(gelu_tanh, pre_act)
        activation = act_full.astype(jnp.bfloat16)
        grad_act = jnp.dot(grad_rows, weight_out.T, preferred_element_type=jnp.float32)
        grad_out_weight = jnp.dot(activation.T, grad_rows, preferred_element_type=jnp.float32)
        grad_pre = gelu_back(grad_act)[0].astype(jnp.bfloat16)
        grad_in_weight = jnp.dot(rows_in.T, grad_pre, preferred_element_type=jnp.float32)
        split_grad = grad_pre.reshape(-1, N_DP, hidden_block).astype(jnp.float32)
        split_in = weight_in.reshape(D, N_DP, hidden_block).astype(jnp.float32)
        grad_rows_back = block_sum(jnp.einsum('mkh,dkh->kmd', split_grad, split_in))
        return (grad_in_weight, grad_out_weight, grad_rows_back)
    grad_w_in, grad_w_out, grad_back = lax.map(backward_expert, (dispatched, grad_dispatched, w_in, w_out))
    grad_normed = grad_back.reshape(EXPERT_TOTAL, block_count, CAP, D)[chosen, anchor, slot_place]
    grad_flat = grad_mixed + norm_back(grad_normed.astype(jnp.float32))[0]
    return (grad_flat.astype(jnp.bfloat16).reshape(PAIRS, 2, TOK, D), grad_w_in, grad_w_out)
```

```python
import math

import jax
import jax.numpy as jnp
from jax import lax
from jax.sharding import PartitionSpec as P

norm_eps = 1e-06
objective_scale = 32.0
bf16 = jnp.bfloat16
f32 = jnp.float32


def layer_norm(values, gain_vector):
    centred = values - jnp.mean(values, axis=-1, keepdims=True)
    spread = jnp.mean(centred * centred, axis=-1, keepdims=True)
    return centred * lax.rsqrt(spread + norm_eps) * gain_vector


def gelu_tanh(values):
    return jax.nn.gelu(values, approximate=True)


def mm(spec, a, b, out=f32):
    return jnp.einsum(spec, a, b, preferred_element_type=f32).astype(out)


def body(tokens, expert_ids, slots, ln_gain, w_in, w_out):
    tok_count = tokens.shape[2]
    width = tokens.shape[3]
    row_count = 2 * tok_count
    groups = lax.axis_size("expert")
    datas = lax.axis_size("dp")
    local = w_in.shape[0]
    total = local * groups
    cap = max(2, 3 * row_count // (2 * total))
    pairs = groups * datas
    everyone = ("dp", "expert")

    flat = tokens.reshape(row_count, width).astype(f32)
    position = expert_ids.reshape(row_count) * cap + slots.reshape(row_count)
    all_pos = lax.all_gather(position[None], everyone, axis=0, tiled=True)

    normed_full, norm_back = jax.vjp(lambda values: layer_norm(values, ln_gain), flat)
    normed = normed_full.astype(bf16)
    place = (jnp.arange(total * cap, dtype=jnp.int32)[:, None] == position[None, :]).astype(bf16)
    sent = mm("rt,td->rd", place, normed, bf16).reshape(groups, local, cap, width)
    routed = lax.all_to_all(sent, "expert", split_axis=0, concat_axis=0, tiled=True)
    routed = routed.transpose(1, 0, 2, 3).reshape(1, local, groups * cap, width)
    rows = lax.all_gather(routed, "dp", axis=0, tiled=True)

    first = lax.axis_index("expert") * (local * cap)
    held = jnp.arange(local * cap, dtype=jnp.int32)[None, :, None] + first
    named = (all_pos[:, None, :] == held).astype(f32).reshape(pairs, local * cap, 2, tok_count)
    kind = jnp.max(named, axis=3).reshape(datas, groups, local, cap, 2)
    eye = jnp.eye(groups, dtype=f32)
    pool = jnp.einsum("sglck,gf->slfkgc", kind, eye)
    pool = pool.reshape(datas, local, groups * 2, groups * cap).astype(bf16)

    hidden_pre = mm("slrd,ldh->slrh", rows, w_in)
    act_full, gelu_back = jax.vjp(gelu_tanh, hidden_pre)
    pooled_act = mm("slqr,slrh->slqh", pool, act_full.astype(bf16), bf16)
    partial = mm("slqh,lhd->sqd", pooled_act, w_out, bf16)
    partial = lax.all_to_all(
        partial.reshape(pairs, 2, width), everyone, split_axis=0, concat_axis=0, tiled=True
    )
    own = jnp.sum(partial.astype(f32), axis=0) + jnp.sum(
        flat.reshape(2, tok_count, width), axis=1
    )
    own = own / tok_count
    emb = lax.all_to_all(
        jnp.broadcast_to(own[None], (pairs, 2, width)),
        everyone,
        split_axis=0,
        concat_axis=0,
        tiled=True,
    )
    image_emb, text_emb = emb[:, 0], emb[:, 1]
    logit_scale = tok_count / math.sqrt(width)
    highest = lax.Precision.HIGHEST
    logits = logit_scale * jnp.dot(image_emb, text_emb.T, precision=highest)
    grad_logits = objective_scale * (
        jax.nn.softmax(logits, axis=1)
        + jax.nn.softmax(logits, axis=0)
        - 2.0 * jnp.eye(pairs, dtype=f32)
    )
    grad_image = logit_scale * jnp.dot(grad_logits, text_emb, precision=highest)
    grad_text = logit_scale * jnp.dot(grad_logits.T, image_emb, precision=highest)
    grad_pooled = jnp.stack([grad_image, grad_text], axis=1) / tok_count
    grad_rows = grad_pooled.astype(bf16).reshape(datas, groups * 2, width)
    me = lax.axis_index(everyone)
    grad_own = lax.dynamic_index_in_dim(grad_pooled, me, axis=0, keepdims=False)

    grad_pool = mm("sqd,lhd->slqh", grad_rows, w_out, bf16)
    grad_act = mm("slqr,slqh->slrh", pool, grad_pool)
    grad_pre = gelu_back(grad_act)[0].astype(bf16)
    grad_partial = mm("slrh,ldh->slrd", grad_pre, w_in, bf16)
    summed = lax.psum_scatter(
        grad_partial.reshape(datas * total * cap, width), "dp", scatter_dimension=0, tiled=True
    )
    grad_w_out = mm("slqh,sqd->lhd", pooled_act, grad_rows)
    grad_w_in = mm("slrd,slrh->ldh", rows, grad_pre)

    back = summed.reshape(local, groups, cap, width).transpose(1, 0, 2, 3)
    back = lax.all_to_all(back, "expert", split_axis=0, concat_axis=0, tiled=True)
    grad_normed = mm("rt,rd->td", place, back.reshape(total * cap, width))
    grad_flat = jnp.repeat(grad_own, tok_count, axis=0) + norm_back(grad_normed)[0]
    return (grad_flat.astype(bf16).reshape(tokens.shape), grad_w_in, grad_w_out)


def solution(mesh):
    placed = (
        P(("dp", "expert"), None, None, None),
        P(("dp", "expert"), None, None),
        P(("dp", "expert"), None, None),
        P(),
        P("expert", None, "dp"),
        P("expert", "dp", None),
    )
    return jax.shard_map(
        body,
        mesh=mesh,
        in_specs=placed,
        out_specs=(
            P(("dp", "expert"), None, None, None),
            P("expert", None, "dp"),
            P("expert", "dp", None),
        ),
        check_vma=False,
    )
```

```python
import functools
import math

import jax
import jax.numpy as jnp
from jax import lax
from jax.experimental import pallas as pl
from jax.experimental.pallas import tpu as pltpu
from jax.sharding import PartitionSpec as P

norm_eps = 1e-06
objective_scale = 32.0
bf16 = jnp.bfloat16
f32 = jnp.float32
i32 = jnp.int32

CAP = 6
HELD = 2
GROUP = HELD * CAP
PAD = 16
PEERS = 16
HALF = PEERS * CAP
KIND_ROWS = 16
POOLED = 2 * PEERS


def nn(a, b):
    return lax.dot_general(a, b, (((1,), (0,)), ((), ())), preferred_element_type=f32)


def nt(a, b, precision=None):
    return lax.dot_general(
        a, b, (((1,), (1,)), ((), ())), precision=precision, preferred_element_type=f32
    )


def tn(a, b, precision=None):
    return lax.dot_general(
        a, b, (((0,), (0,)), ((), ())), precision=precision, preferred_element_type=f32
    )


def iota(shape, dim):
    return lax.broadcasted_iota(i32, shape, dim)


def shape_of(*dims, dtype=bf16):
    return jax.ShapeDtypeStruct(dims, dtype)


def call(kernel, out, args, flops=0, nbytes=0, smem=(), scratch=(), vmem=40):
    specs = [
        pl.BlockSpec(memory_space=pltpu.SMEM if k in smem else pltpu.VMEM)
        for k in range(len(args))
    ]
    many = isinstance(out, (list, tuple))
    out_specs = [pl.BlockSpec(memory_space=pltpu.VMEM) for _ in (out if many else [out])]
    return pl.pallas_call(
        kernel,
        out_shape=out,
        in_specs=specs,
        out_specs=out_specs if many else out_specs[0],
        scratch_shapes=list(scratch),
        compiler_params=pltpu.CompilerParams(vmem_limit_bytes=vmem * 1024 * 1024),
        cost_estimate=pl.CostEstimate(flops=flops, bytes_accessed=nbytes, transcendentals=0),
    )(*args)


def normal_parts(x):
    centred = x - jnp.mean(x, axis=-1, keepdims=True)
    spread = jnp.mean(centred * centred, axis=-1, keepdims=True)
    scale = lax.rsqrt(spread + norm_eps)
    return centred * scale, scale


def slot_table(pos):
    tokens = pos.shape[1]
    row = iota((PEERS * PAD, tokens), 0)
    want = (row // PAD) * GROUP + row % PAD
    return jnp.where((want == pos) & (row % PAD < GROUP), 1.0, 0.0).astype(bf16)


def dispatch_kernel(me_ref, pos_ref, tok_ref, gain_ref, out_ref):
    pos = pos_ref[...]
    tokens = pos.shape[1]
    normed = normal_parts(tok_ref[...].astype(f32))[0] * gain_ref[...]
    normed = normed.astype(bf16)
    sent = nn(slot_table(pos), normed)
    row = iota((PEERS * PAD, tokens), 0)
    goes = jnp.where((row % PAD == GROUP) & (pos // GROUP == row // PAD), 1.0, 0.0).astype(bf16)
    place = pos % GROUP
    column = (place // CAP) * 128 + me_ref[0] * CAP + place % CAP
    lane = iota((2 * 128, tokens), 0)
    kind = jnp.where(iota((2 * 128, tokens), 1) < tokens // 2, 1.0, 2.0)
    kinds = nt(goes, jnp.where(lane == column, kind, 0.0).astype(bf16))
    width = sent.shape[1]
    first = sent[:, : 2 * 128] + kinds
    out_ref[:, :, : 2 * 128] = first.astype(bf16).reshape(PEERS, PAD, 2 * 128)
    out_ref[:, :, 2 * 128 :] = sent[:, 2 * 128 :].astype(bf16).reshape(
        PEERS, PAD, width - 2 * 128
    )


def repack_table(rows, back):
    shape = (PEERS * PAD, rows) if back else (rows, PEERS * PAD)
    r = iota(shape, 1 if back else 0)
    m = iota(shape, 0 if back else 1)
    held, rest = r // HALF, r % HALF
    from_slot = (rest // CAP) * PAD + held * CAP + rest % CAP
    hit = (r < 2 * HALF) & (m == from_slot)
    if not back:
        hit = hit | ((r == 2 * HALF) & (m % PAD == GROUP))
    return jnp.where(hit, 1.0, 0.0).astype(bf16)


def repack_kernel(in_ref, first_ref, second_ref):
    width = in_ref.shape[2]
    rows = 2 * HALF + KIND_ROWS
    out = nn(repack_table(rows, False), in_ref[...].reshape(PEERS * PAD, width)).astype(bf16)
    first_ref[...] = out[:HALF]
    second_ref[...] = out[HALF:]


def forward_kernel(count, *refs):
    firsts, seconds = refs[:count], refs[count : 2 * count]
    w_in, pooled_ref, slope_ref, pool_ref = refs[2 * count :]
    c0 = math.sqrt(2.0 / math.pi)
    c1 = 0.044715
    for k in range(count):
        for held in range(HELD):
            rows = firsts[k][...] if held == 0 else seconds[k][:HALF, :]
            h = nn(rows, w_in[held])
            h2 = h * h
            t = jnp.tanh(c0 * h * (1.0 + c1 * h2))
            half = 0.5 * (1.0 + t)
            act = (h * half).astype(bf16)
            slope = half + 0.5 * h * (1.0 - t * t) * (c0 * (1.0 + 3.0 * c1 * h2))
            kinds = seconds[k][HALF : HALF + KIND_ROWS, held * 128 : held * 128 + 128]
            kinds = kinds.astype(f32)[:1, :HALF]
            q = iota((POOLED, HALF), 0)
            r = iota((POOLED, HALF), 1)
            hit = (q % PEERS == r // CAP) & (kinds == (q // PEERS + 1).astype(f32))
            pool = jnp.where(hit, 1.0, 0.0).astype(bf16)
            pooled_ref[k, held] = nn(pool, act).astype(bf16)
            slope_ref[k, held] = slope.astype(bf16)
            pool_ref[k, held] = pool


def forward(firsts, seconds, w_in):
    count = len(firsts)
    hidden = w_in.shape[2]
    width = w_in.shape[1]
    return call(
        functools.partial(forward_kernel, count),
        [
            shape_of(count, HELD, POOLED, hidden),
            shape_of(count, HELD, HALF, hidden),
            shape_of(count, HELD, POOLED, HALF),
        ],
        [*firsts, *seconds, w_in],
        flops=count * 2 * 2 * HALF * width * hidden,
        nbytes=w_in.size * 2 + count * 2 * HALF * (width + hidden) * 2,
    )


def block_of(refs, k):
    if k < 2:
        return refs[0].at[k]
    if k < 6:
        return refs[1].at[k - 2]
    return refs[2].at[k - 6]


AROUND = (0, 4, 6, 2)


def out_kernel(a_ref, b_ref, c_ref, w_out, own_ref, other_ref):
    refs = (a_ref, b_ref, c_ref)
    for shift, out_ref in ((1, other_ref), (0, own_ref)):
        total = None
        for held in range(HELD):
            rows = jnp.concatenate([block_of(refs, k + shift)[held] for k in AROUND], axis=0)
            part = nn(rows, w_out[held])
            total = part if total is None else total + part
        out_ref[...] = total.astype(bf16).reshape(out_ref.shape)


def join_kernel(z_ref, own_ref, got_ref, out_ref):
    for ahead in range(4):
        to = lax.rem(z_ref[0] + ahead, 4)
        out_ref[to] = (own_ref[ahead].astype(f32) + got_ref[ahead].astype(f32)).astype(bf16)


def loss_kernel(z_ref, image_ref, text_ref, w_out, grad_ref, rows_ref, prod_ref, gi_ref, gt_ref):
    highest = lax.Precision.HIGHEST
    image, text = image_ref[...], text_ref[...]
    pairs, width = image.shape
    scale = PAIR_TOKENS / math.sqrt(width)
    logits = scale * nt(image, text, highest)

    def softmax(axis):
        top = jnp.exp(logits - jnp.max(logits, axis=axis, keepdims=True))
        return top / jnp.sum(top, axis=axis, keepdims=True)

    same = jnp.where(iota((pairs, pairs), 0) == iota((pairs, pairs), 1), 2.0, 0.0)
    grad_logits = objective_scale * (softmax(1) + softmax(0) - same)
    grad_image = (scale / PAIR_TOKENS) * lax.dot_general(
        grad_logits,
        text,
        (((1,), (0,)), ((), ())),
        precision=highest,
        preferred_element_type=f32,
    )
    grad_text = (scale / PAIR_TOKENS) * tn(grad_logits, image, highest)
    grad_ref[0] = grad_image
    grad_ref[1] = grad_text
    gi_ref[...] = grad_image.astype(bf16)
    gt_ref[...] = grad_text.astype(bf16)
    for at, k in enumerate(AROUND):
        for other in range(2):
            first = other * 4 * PEERS + lax.rem(z_ref[0] + at, 4) * PEERS
            span = pl.ds(pl.multiple_of(first, PEERS), PEERS)
            rows_ref[k + other, :PEERS, :] = gi_ref[span, :]
            rows_ref[k + other, PEERS:, :] = gt_ref[span, :]
    rows = rows_ref[...].reshape(8 * POOLED, width)
    for held in range(HELD):
        prod_ref[held] = nt(rows, w_out[held]).astype(bf16)


def backward_kernel(first, count, pool_ref, slope_ref, prod_ref, w_in, pre_ref, *outs):
    for k in range(count):
        for held in range(HELD):
            prod = prod_ref[held, (first + k) * POOLED : (first + k + 1) * POOLED, :]
            grad_act = tn(pool_ref[k, held], prod)
            pre = (grad_act * slope_ref[k, held].astype(f32)).astype(bf16)
            pre_ref[k, held] = pre
            outs[k][held * HALF : (held + 1) * HALF, :] = nt(pre, w_in[held]).astype(bf16)


def backward(first, pool, slope, prod, w_in):
    count = pool.shape[0]
    width, hidden = w_in.shape[1:]
    return call(
        functools.partial(backward_kernel, first, count),
        [shape_of(count, HELD, HALF, hidden)] + [shape_of(2 * HALF, width)] * count,
        [pool, slope, prod, w_in],
        flops=count * 2 * 2 * HALF * width * hidden,
        nbytes=w_in.size * 2 + count * 2 * HALF * (width + hidden) * 2,
    )


def grad_in_kernel(*refs):
    blocks, pres, out_ref, x_ref, p_ref = refs[:16], refs[16:19], refs[19], refs[20], refs[21]
    held = pl.program_id(0)

    def fill(which):
        for k in range(8):
            span = slice(k * HALF, (k + 1) * HALF)
            x_ref[span, :] = blocks[8 * which + k][:HALF, :]
            p_ref[span, :] = block_of(pres, k)[which]

    for which in range(HELD):
        pl.when(held == which)(functools.partial(fill, which))
    out_ref[0] = tn(x_ref[...], p_ref[...])


def grad_in(firsts, seconds, pres, width, hidden):
    whole = pl.BlockSpec(memory_space=pltpu.VMEM)
    return pl.pallas_call(
        grad_in_kernel,
        grid=(HELD,),
        out_shape=shape_of(HELD, width, hidden, dtype=f32),
        in_specs=[whole] * 19,
        out_specs=pl.BlockSpec((1, width, hidden), lambda i: (i, 0, 0)),
        scratch_shapes=[
            pltpu.VMEM((8 * HALF, width), bf16),
            pltpu.VMEM((8 * HALF, hidden), bf16),
        ],
        compiler_params=pltpu.CompilerParams(vmem_limit_bytes=44 * 1024 * 1024),
        cost_estimate=pl.CostEstimate(
            flops=2 * 2 * 8 * HALF * width * hidden, bytes_accessed=17_000_000, transcendentals=0
        ),
    )(*firsts, *seconds, *pres)


def grad_out_kernel(a_ref, b_ref, c_ref, rows_ref, out_ref):
    refs = (a_ref, b_ref, c_ref)
    held = pl.program_id(0)
    width = rows_ref.shape[2]
    pooled = jnp.concatenate([block_of(refs, k)[held] for k in range(8)], axis=0)
    out_ref[0] = tn(pooled, rows_ref[...].reshape(8 * POOLED, width))


def grad_out(pooled, rows, width, hidden):
    whole = pl.BlockSpec(memory_space=pltpu.VMEM)
    return pl.pallas_call(
        grad_out_kernel,
        grid=(HELD,),
        out_shape=shape_of(HELD, hidden, width, dtype=f32),
        in_specs=[whole] * 4,
        out_specs=pl.BlockSpec((1, hidden, width), lambda i: (i, 0, 0)),
        compiler_params=pltpu.CompilerParams(vmem_limit_bytes=32 * 1024 * 1024),
        cost_estimate=pl.CostEstimate(
            flops=2 * 2 * 8 * POOLED * width * hidden, bytes_accessed=9_000_000, transcendentals=0
        ),
    )(*pooled, rows)


def settle_kernel(own_ref, got_ref, la_ref, lb_ref, ra_ref, rb_ref, out_ref):
    width = own_ref.shape[1]
    total = own_ref[...].astype(f32) + got_ref[...].astype(f32)
    first = total[:HALF] + la_ref[...].astype(f32) + ra_ref[...].astype(f32)
    second = total[HALF:] + lb_ref[...].astype(f32) + rb_ref[...].astype(f32)
    table = repack_table(2 * HALF, True)
    rows = jnp.concatenate([first.astype(bf16), second.astype(bf16)], axis=0)
    out_ref[...] = nn(table, rows).astype(bf16).reshape(PEERS, PAD, width)


def tail_kernel(pos_ref, tok_ref, gain_ref, grad_ref, back_ref, out_ref):
    tokens, width = tok_ref.shape
    grad_normed = tn(slot_table(pos_ref[...]), back_ref[...].reshape(PEERS * PAD, width))
    unit, scale = normal_parts(tok_ref[...].astype(f32))
    grad = grad_normed * gain_ref[...]
    grad = scale * (
        grad
        - jnp.mean(grad, axis=-1, keepdims=True)
        - unit * jnp.mean(grad * unit, axis=-1, keepdims=True)
    )
    image = iota((tokens, width), 0) < tokens // 2
    mixed = jnp.where(image, grad_ref[0:1, :], grad_ref[1:2, :])
    out_ref[...] = (mixed + grad).astype(bf16)


PAIR_TOKENS = 64


def body(tokens, expert_ids, slots, ln_gain, w_in, w_out):
    width, hidden = w_in.shape[1:]
    row_count = tokens.shape[1] * tokens.shape[2]
    flat = tokens.reshape(row_count, width)
    gain = ln_gain.reshape(1, width)
    pos = (expert_ids * CAP + slots).reshape(1, row_count)
    data = lax.axis_index("dp")
    group = lax.axis_index("expert")
    z = (data // 2).reshape(1)
    everyone = ("dp", "expert")
    cores = [[d * PEERS + e for d in range(c, 8, 2) for e in range(PEERS)] for c in range(2)]

    def up(x):
        return lax.ppermute(x, "dp", [(i, (i + 2) % 8) for i in range(8)])

    def down(x):
        return lax.ppermute(x, "dp", [(i, (i + 6) % 8) for i in range(8)])

    def swap(x):
        return lax.ppermute(x, "dp", [(i, i ^ 1) for i in range(8)])

    def exchange(x):
        return lax.all_to_all(x, "expert", split_axis=0, concat_axis=0, tiled=True)

    def spread(x):
        return lax.all_to_all(
            x, everyone, split_axis=0, concat_axis=0, tiled=True, axis_index_groups=cores
        )

    sent = call(
        dispatch_kernel,
        shape_of(PEERS, PAD, width),
        [group.reshape(1), pos, flat, gain],
        smem=(0,),
    )
    first, second = call(
        repack_kernel,
        [shape_of(HALF, width), shape_of(HALF + KIND_ROWS, width)],
        [exchange(sent)],
    )

    a, b = [None] * 8, [None] * 8
    a[0], b[0] = first, second
    a[2] = up(first)
    b[4] = down(second)
    b[2] = up(second)
    a[4] = down(first)
    a[6] = up(a[2])
    b[6] = down(b[4])
    for k in (0, 2, 4, 6):
        a[k + 1] = swap(a[k])
        b[k + 1] = swap(b[k])
    made = [forward(a[i:j], b[i:j], w_in) for i, j in ((0, 2), (2, 6), (6, 8))]
    pooled = [m[0] for m in made]
    slope = [m[1] for m in made]
    pool = [m[2] for m in made]

    own, other = call(
        out_kernel,
        [shape_of(4, POOLED, width), shape_of(4, POOLED, width)],
        [*pooled, w_out],
        flops=2 * 8 * POOLED * width * hidden * HELD,
        nbytes=w_out.size * 2,
    )
    joined = call(
        join_kernel, shape_of(4, POOLED, width), [z, own, swap(other)], smem=(0,)
    )
    joined = joined.reshape(4, 2, PEERS, width).transpose(0, 2, 1, 3).reshape(-1, 2, width)
    parts = spread(joined)
    emb = jnp.sum(parts.astype(f32), axis=0) + jnp.sum(
        flat.reshape(2, PAIR_TOKENS, width).astype(f32), axis=1
    )
    emb = spread(jnp.broadcast_to((emb / PAIR_TOKENS)[None], (4 * PEERS, 2, width)))
    emb_other = swap(emb)
    image = jnp.concatenate([emb[:, 0], emb_other[:, 0]], axis=0)
    text = jnp.concatenate([emb[:, 1], emb_other[:, 1]], axis=0)
    grad_pooled, rows, prod = call(
        loss_kernel,
        [
            shape_of(2, 8 * PEERS, width, dtype=f32),
            shape_of(8, POOLED, width),
            shape_of(HELD, 8 * POOLED, hidden),
        ],
        [z, image, text, w_out],
        smem=(0,),
        scratch=[pltpu.VMEM((8 * PEERS, width), bf16), pltpu.VMEM((8 * PEERS, width), bf16)],
        flops=2 * 8 * POOLED * width * hidden * HELD,
        nbytes=w_out.size * 2,
    )
    grad_own = lax.dynamic_index_in_dim(
        grad_pooled, (data // 2) * PEERS + group, axis=1, keepdims=False
    )

    def plus(x, y):
        return (x.astype(f32) + y.astype(f32)).astype(bf16)

    pre_c, p6, p7 = backward(6, pool[2], slope[2], prod, w_in)
    r6 = plus(p6, swap(p7))
    from_below = up(r6[:HALF])
    from_above = down(r6[HALF:])
    pre_b, p2, p3, p4, p5 = backward(2, pool[1], slope[1], prod, w_in)
    r4 = plus(p4, swap(p5))
    r2 = plus(p2, swap(p3))
    low_b = up(r4[HALF:])
    high_a = down(r2[:HALF])
    low_a = up(plus(r4[:HALF], from_below))
    high_b = down(plus(r2[HALF:], from_above))
    pre_a, p0, p1 = backward(0, pool[0], slope[0], prod, w_in)
    got = swap(p1)
    grad_w_in = grad_in(a, b, [pre_a, pre_b, pre_c], width, hidden)
    grad_w_out = grad_out(pooled, rows, width, hidden)

    back = exchange(
        call(
            settle_kernel,
            shape_of(PEERS, PAD, width),
            [p0, got, low_a, low_b, high_a, high_b],
        )
    )
    grad_flat = call(
        tail_kernel, shape_of(row_count, width), [pos, flat, gain, grad_own, back]
    )
    return (grad_flat.reshape(tokens.shape), grad_w_in, grad_w_out)


def solution(mesh):
    placed = (
        P(("dp", "expert"), None, None, None),
        P(("dp", "expert"), None, None),
        P(("dp", "expert"), None, None),
        P(),
        P("expert", None, "dp"),
        P("expert", "dp", None),
    )
    return jax.shard_map(
        body,
        mesh=mesh,
        in_specs=placed,
        out_specs=(
            P(("dp", "expert"), None, None, None),
            P("expert", None, "dp"),
            P("expert", "dp", None),
        ),
        check_vma=False,
    )
```

```python
import functools
import math

import jax
import jax.numpy as jnp
from jax import lax
from jax.experimental import pallas as pl
from jax.experimental.pallas import tpu as pltpu
from jax.sharding import PartitionSpec as P

norm_eps = 1e-06
objective_scale = 32.0
bf16 = jnp.bfloat16
f32 = jnp.float32
i32 = jnp.int32

CAP = 6
HELD = 2
GROUP = HELD * CAP
PAD = 16
PEERS = 16
HALF = PEERS * CAP
KIND_ROWS = 16
POOLED = 2 * PEERS


def nn(a, b):
    return lax.dot_general(a, b, (((1,), (0,)), ((), ())), preferred_element_type=f32)


def nt(a, b, precision=None):
    return lax.dot_general(
        a, b, (((1,), (1,)), ((), ())), precision=precision, preferred_element_type=f32
    )


def tn(a, b, precision=None):
    return lax.dot_general(
        a, b, (((0,), (0,)), ((), ())), precision=precision, preferred_element_type=f32
    )


def iota(shape, dim):
    return lax.broadcasted_iota(i32, shape, dim)


def shape_of(*dims, dtype=bf16):
    return jax.ShapeDtypeStruct(dims, dtype)


def call(kernel, out, args, flops=0, nbytes=0, smem=(), scratch=(), vmem=14):
    specs = [
        pl.BlockSpec(memory_space=pltpu.SMEM if k in smem else pltpu.VMEM)
        for k in range(len(args))
    ]
    many = isinstance(out, (list, tuple))
    out_specs = [pl.BlockSpec(memory_space=pltpu.VMEM) for _ in (out if many else [out])]
    return pl.pallas_call(
        kernel,
        out_shape=out,
        in_specs=specs,
        out_specs=out_specs if many else out_specs[0],
        scratch_shapes=list(scratch),
        compiler_params=pltpu.CompilerParams(vmem_limit_bytes=vmem * 1024 * 1024),
        cost_estimate=pl.CostEstimate(flops=flops, bytes_accessed=nbytes, transcendentals=0),
    )(*args)


def normal_parts(x):
    centred = x - jnp.mean(x, axis=-1, keepdims=True)
    spread = jnp.mean(centred * centred, axis=-1, keepdims=True)
    scale = lax.rsqrt(spread + norm_eps)
    return centred * scale, scale


def place_of(ids_ref, slots_ref, half):
    return ids_ref[half : half + 1, :] * CAP + slots_ref[half : half + 1, :]


def slot_table(pos):
    tokens = pos.shape[1]
    row = iota((PEERS * PAD, tokens), 0)
    want = (row // PAD) * GROUP + row % PAD
    return jnp.where((want == pos) & (row % PAD < GROUP), 1.0, 0.0).astype(bf16)


def dispatch_kernel(me_ref, ids_ref, slots_ref, tok_ref, gain_ref, out_ref):
    normed = normal_parts(tok_ref[...].astype(f32))[0] * gain_ref[...].reshape(1, -1)
    normed = normed.astype(bf16)
    tokens, width = normed.shape
    tokens = tokens // 2
    sent = kinds = None
    for half in range(2):
        pos = place_of(ids_ref, slots_ref, half)
        part = nn(slot_table(pos), normed[half * tokens : (half + 1) * tokens])
        row = iota((PEERS * PAD, tokens), 0)
        goes = (row % PAD == GROUP) & (pos // GROUP == row // PAD)
        goes = jnp.where(goes, 1.0, 0.0).astype(bf16)
        place = pos % GROUP
        column = (place // CAP) * 128 + me_ref[0] * CAP + place % CAP
        lane = iota((2 * 128, tokens), 0)
        kind = nt(goes, jnp.where(lane == column, 1.0 + half, 0.0).astype(bf16))
        sent = part if sent is None else sent + part
        kinds = kind if kinds is None else kinds + kind
    first = sent[:, : 2 * 128] + kinds
    out_ref[:, :, : 2 * 128] = first.astype(bf16).reshape(PEERS, PAD, 2 * 128)
    out_ref[:, :, 2 * 128 :] = sent[:, 2 * 128 :].astype(bf16).reshape(
        PEERS, PAD, width - 2 * 128
    )


def repack_table(rows, back):
    shape = (PEERS * PAD, rows) if back else (rows, PEERS * PAD)
    r = iota(shape, 1 if back else 0)
    m = iota(shape, 0 if back else 1)
    held, rest = r // HALF, r % HALF
    from_slot = (rest // CAP) * PAD + held * CAP + rest % CAP
    hit = (r < 2 * HALF) & (m == from_slot)
    if not back:
        hit = hit | ((r == 2 * HALF) & (m % PAD == GROUP))
    return jnp.where(hit, 1.0, 0.0).astype(bf16)


def repack_kernel(in_ref, first_ref, second_ref):
    width = in_ref.shape[2]
    rows = 2 * HALF + KIND_ROWS
    out = nn(repack_table(rows, False), in_ref[...].reshape(PEERS * PAD, width)).astype(bf16)
    first_ref[...] = out[:HALF]
    second_ref[...] = out[HALF:]


def forward_kernel(count, *refs):
    firsts, seconds = refs[:count], refs[count : 2 * count]
    w_in, pooled_ref, slope_ref, pool_ref = refs[2 * count :]
    c0 = math.sqrt(2.0 / math.pi)
    c1 = 0.044715
    for k in range(count):
        for held in range(HELD):
            rows = firsts[k][...] if held == 0 else seconds[k][:HALF, :]
            h = nn(rows, w_in[held])
            h2 = h * h
            t = jnp.tanh(c0 * h * (1.0 + c1 * h2))
            half = 0.5 * (1.0 + t)
            act = (h * half).astype(bf16)
            slope = half + 0.5 * h * (1.0 - t * t) * (c0 * (1.0 + 3.0 * c1 * h2))
            kinds = seconds[k][HALF : HALF + KIND_ROWS, held * 128 : held * 128 + 128]
            kinds = kinds.astype(f32)[:1, :HALF]
            q = iota((POOLED, HALF), 0)
            r = iota((POOLED, HALF), 1)
            hit = (q % PEERS == r // CAP) & (kinds == (q // PEERS + 1).astype(f32))
            pool = jnp.where(hit, 1.0, 0.0).astype(bf16)
            pooled_ref[k, held] = nn(pool, act).astype(bf16)
            slope_ref[k, held] = slope.astype(bf16)
            pool_ref[k, held] = pool


def forward(firsts, seconds, w_in):
    count = len(firsts)
    hidden = w_in.shape[2]
    width = w_in.shape[1]
    return call(
        functools.partial(forward_kernel, count),
        [
            shape_of(count, HELD, POOLED, hidden),
            shape_of(count, HELD, HALF, hidden),
            shape_of(count, HELD, POOLED, HALF),
        ],
        [*firsts, *seconds, w_in],
        flops=count * 2 * 2 * HALF * width * hidden,
        nbytes=w_in.size * 2 + count * 2 * HALF * (width + hidden) * 2,
    )


def block_of(refs, k):
    if k < 2:
        return refs[0].at[k]
    if k < 6:
        return refs[1].at[k - 2]
    return refs[k - 4].at[0]


AROUND = (0, 4, 6, 2)


def out_kernel(shift, *refs):
    pooled, w_out, out_ref = refs[:-2], refs[-2], refs[-1]
    total = None
    for held in range(HELD):
        rows = jnp.concatenate([block_of(pooled, k + shift)[held] for k in AROUND], axis=0)
        part = nn(rows, w_out[held])
        total = part if total is None else total + part
    out_ref[...] = total.astype(bf16).reshape(out_ref.shape)


def join_kernel(z_ref, own_ref, got_ref, out_ref):
    for ahead in range(4):
        to = lax.rem(z_ref[0] + ahead, 4)
        out_ref[to] = (own_ref[ahead].astype(f32) + got_ref[ahead].astype(f32)).astype(bf16)


def loss_kernel(z_ref, own_ref, other_ref, w_out, grad_ref, rows_ref, prod_ref, gi_ref, gt_ref):
    highest = lax.Precision.HIGHEST
    image = jnp.concatenate([own_ref[0], other_ref[0]], axis=0)
    text = jnp.concatenate([own_ref[1], other_ref[1]], axis=0)
    pairs, width = image.shape
    scale = PAIR_TOKENS / math.sqrt(width)
    logits = scale * nt(image, text, highest)

    def softmax(axis):
        top = jnp.exp(logits - jnp.max(logits, axis=axis, keepdims=True))
        return top / jnp.sum(top, axis=axis, keepdims=True)

    same = jnp.where(iota((pairs, pairs), 0) == iota((pairs, pairs), 1), 2.0, 0.0)
    grad_logits = objective_scale * (softmax(1) + softmax(0) - same)
    grad_image = (scale / PAIR_TOKENS) * lax.dot_general(
        grad_logits,
        text,
        (((1,), (0,)), ((), ())),
        precision=highest,
        preferred_element_type=f32,
    )
    grad_text = (scale / PAIR_TOKENS) * tn(grad_logits, image, highest)
    grad_ref[0] = grad_image
    grad_ref[1] = grad_text
    gi_ref[...] = grad_image.astype(bf16)
    gt_ref[...] = grad_text.astype(bf16)
    for at, k in enumerate(AROUND):
        for other in range(2):
            first = other * 4 * PEERS + lax.rem(z_ref[0] + at, 4) * PEERS
            span = pl.ds(pl.multiple_of(first, PEERS), PEERS)
            rows_ref[k + other, :PEERS, :] = gi_ref[span, :]
            rows_ref[k + other, PEERS:, :] = gt_ref[span, :]
    rows = rows_ref[...].reshape(8 * POOLED, width)
    for held in range(HELD):
        prod_ref[held] = nt(rows, w_out[held]).astype(bf16)


def backward_kernel(first, at, count, pool_ref, slope_ref, prod_ref, w_in, pre_ref, *outs):
    for k in range(count):
        for held in range(HELD):
            prod = prod_ref[held, (first + k) * POOLED : (first + k + 1) * POOLED, :]
            grad_act = tn(pool_ref[at + k, held], prod)
            pre = (grad_act * slope_ref[at + k, held].astype(f32)).astype(bf16)
            pre_ref[k, held] = pre
            outs[k][held * HALF : (held + 1) * HALF, :] = nt(pre, w_in[held]).astype(bf16)


def backward(first, at, count, made, prod, w_in):
    width, hidden = w_in.shape[1:]
    return call(
        functools.partial(backward_kernel, first, at, count),
        [shape_of(count, HELD, HALF, hidden)] + [shape_of(2 * HALF, width)] * count,
        [made[2], made[1], prod, w_in],
        flops=count * 2 * 2 * HALF * width * hidden,
        nbytes=w_in.size * 2 + count * 2 * HALF * (width + hidden) * 2,
    )


def grad_in_kernel(*refs):
    blocks, pres = refs[:16], refs[16:21]
    out_ref, x_ref, p_ref = refs[21:]
    held = pl.program_id(0)

    def fill(which):
        for k in range(8):
            span = slice(k * HALF, (k + 1) * HALF)
            x_ref[span, :] = blocks[8 * which + k][:HALF, :]
            p_ref[span, :] = (pres[k // 2].at[k % 2] if k < 6 else pres[k - 3].at[0])[which]

    for which in range(HELD):
        pl.when(held == which)(functools.partial(fill, which))
    out_ref[0] = tn(x_ref[...], p_ref[...])


def grad_in(firsts, seconds, pres, width, hidden):
    whole = pl.BlockSpec(memory_space=pltpu.VMEM)
    return pl.pallas_call(
        grad_in_kernel,
        grid=(HELD,),
        out_shape=shape_of(HELD, width, hidden, dtype=f32),
        in_specs=[whole] * 21,
        out_specs=pl.BlockSpec((1, width, hidden), lambda i: (i, 0, 0)),
        scratch_shapes=[
            pltpu.VMEM((8 * HALF, width), bf16),
            pltpu.VMEM((8 * HALF, hidden), bf16),
        ],
        compiler_params=pltpu.CompilerParams(vmem_limit_bytes=24 * 1024 * 1024),
        cost_estimate=pl.CostEstimate(
            flops=2 * 2 * 8 * HALF * width * hidden, bytes_accessed=17_000_000, transcendentals=0
        ),
    )(*firsts, *seconds, *pres)


def grad_out_kernel(*args):
    refs, rows_ref, out_ref = args[:-2], args[-2], args[-1]
    held = pl.program_id(0)
    width = rows_ref.shape[2]
    pooled = jnp.concatenate([block_of(refs, k)[held] for k in range(8)], axis=0)
    out_ref[0] = tn(pooled, rows_ref[...].reshape(8 * POOLED, width))


def grad_out(pooled, rows, width, hidden):
    whole = pl.BlockSpec(memory_space=pltpu.VMEM)
    return pl.pallas_call(
        grad_out_kernel,
        grid=(HELD,),
        out_shape=shape_of(HELD, hidden, width, dtype=f32),
        in_specs=[whole] * 5,
        out_specs=pl.BlockSpec((1, hidden, width), lambda i: (i, 0, 0)),
        compiler_params=pltpu.CompilerParams(vmem_limit_bytes=18 * 1024 * 1024),
        cost_estimate=pl.CostEstimate(
            flops=2 * 2 * 8 * POOLED * width * hidden, bytes_accessed=9_000_000, transcendentals=0
        ),
    )(*pooled, rows)


def settle_kernel(own_ref, got_ref, la_ref, lb_ref, ra_ref, rb_ref, out_ref):
    width = own_ref.shape[1]
    total = own_ref[...].astype(f32) + got_ref[...].astype(f32)
    first = total[:HALF] + la_ref[...].astype(f32) + ra_ref[...].astype(f32)
    second = total[HALF:] + lb_ref[...].astype(f32) + rb_ref[...].astype(f32)
    table = repack_table(2 * HALF, True)
    rows = jnp.concatenate([first.astype(bf16), second.astype(bf16)], axis=0)
    out_ref[...] = nn(table, rows).astype(bf16).reshape(PEERS, PAD, width)


def tail_kernel(ids_ref, slots_ref, tok_ref, gain_ref, grad_ref, back_ref, out_ref):
    width = tok_ref.shape[1]
    tokens = tok_ref.shape[0] // 2
    gain = gain_ref[...].reshape(1, -1)
    back = back_ref[...].reshape(PEERS * PAD, width)
    for half in range(2):
        span = slice(half * tokens, (half + 1) * tokens)
        grad_normed = tn(slot_table(place_of(ids_ref, slots_ref, half)), back)
        unit, scale = normal_parts(tok_ref[span, :].astype(f32))
        grad = grad_normed * gain
        grad = scale * (
            grad
            - jnp.mean(grad, axis=-1, keepdims=True)
            - unit * jnp.mean(grad * unit, axis=-1, keepdims=True)
        )
        out_ref[span, :] = (grad_ref[half : half + 1, :] + grad).astype(bf16)


PAIR_TOKENS = 64


def body(tokens, expert_ids, slots, ln_gain, w_in, w_out):
    width, hidden = w_in.shape[1:]
    row_count = tokens.shape[1] * tokens.shape[2]
    flat = tokens.reshape(row_count, width)
    ids, places = expert_ids[0], slots[0]
    data = lax.axis_index("dp")
    group = lax.axis_index("expert")
    z = (data // 2).reshape(1)
    everyone = ("dp", "expert")
    cores = [[d * PEERS + e for d in range(c, 8, 2) for e in range(PEERS)] for c in range(2)]

    def up(x):
        return lax.ppermute(x, "dp", [(i, (i + 2) % 8) for i in range(8)])

    def down(x):
        return lax.ppermute(x, "dp", [(i, (i + 6) % 8) for i in range(8)])

    def swap(x):
        return lax.ppermute(x, "dp", [(i, i ^ 1) for i in range(8)])

    def after(x, *tokens):
        return lax.optimization_barrier((x, *tokens))[0]

    def exchange(x):
        return lax.all_to_all(x, "expert", split_axis=0, concat_axis=0, tiled=True)

    def spread(x):
        return lax.all_to_all(
            x, everyone, split_axis=0, concat_axis=0, tiled=True, axis_index_groups=cores
        )

    sent = call(
        dispatch_kernel,
        shape_of(PEERS, PAD, width),
        [group.reshape(1), ids, places, flat, ln_gain],
        smem=(0,),
    )
    first, second = call(
        repack_kernel,
        [shape_of(HALF, width), shape_of(HALF + KIND_ROWS, width)],
        [exchange(sent)],
    )

    a, b = [None] * 8, [None] * 8
    a[0], b[0] = first, second
    a[2] = up(first)
    b[4] = down(second)
    a[1], b[1] = swap(first), swap(second)
    b[2] = up(after(second, a[1]))
    a[4] = down(after(first, b[1]))
    near = forward(a[0:2], b[0:2], w_in)
    a[2], b[4] = after(a[2], near[0]), after(b[4], near[0])
    a[6] = up(a[2])
    b[6] = down(b[4])
    for k in (2, 4):
        a[k + 1] = swap(a[k])
        b[k + 1] = swap(b[k])
    mid = forward(a[2:6], b[2:6], w_in)
    a[6], b[6] = after(a[6], mid[0]), after(b[6], mid[0])
    a[7], b[7] = swap(a[6]), swap(b[6])
    far = forward(a[6:7], b[6:7], w_in)
    a[7] = after(a[7], far[0])
    last = forward(a[7:8], b[7:8], w_in)
    made = [near, mid, far, last]
    pooled = [m[0] for m in made]
    slope = [m[1] for m in made]
    pool = [m[2] for m in made]

    def product(shift, w_out):
        return call(
            functools.partial(out_kernel, shift),
            shape_of(4, POOLED, width),
            [*pooled, w_out],
            flops=2 * 4 * POOLED * width * hidden * HELD,
            nbytes=w_out.size * 2,
        )

    other = product(1, w_out)
    got = swap(other)
    own = product(0, after(w_out, other))
    joined = call(
        join_kernel, shape_of(4, POOLED, width), [z, own, after(got, own)], smem=(0,)
    )
    joined = joined.reshape(4, 2, PEERS, width).transpose(0, 2, 1, 3).reshape(-1, 2, width)
    parts = spread(joined)
    emb = jnp.sum(parts.astype(f32), axis=0) + jnp.sum(
        flat.reshape(2, PAIR_TOKENS, width).astype(f32), axis=1
    )
    emb = spread(jnp.broadcast_to((emb / PAIR_TOKENS)[None], (4 * PEERS, 2, width)))
    emb = emb.transpose(1, 0, 2)
    emb_other = swap(emb)
    grad_pooled, rows, prod = call(
        loss_kernel,
        [
            shape_of(2, 8 * PEERS, width, dtype=f32),
            shape_of(8, POOLED, width),
            shape_of(HELD, 8 * POOLED, hidden),
        ],
        [z, emb, emb_other, w_out],
        smem=(0,),
        scratch=[pltpu.VMEM((8 * PEERS, width), bf16), pltpu.VMEM((8 * PEERS, width), bf16)],
        flops=2 * 8 * POOLED * width * hidden * HELD,
        nbytes=w_out.size * 2,
    )
    grad_own = lax.dynamic_index_in_dim(
        grad_pooled, (data // 2) * PEERS + group, axis=1, keepdims=False
    )

    def plus(x, y):
        return (x.astype(f32) + y.astype(f32)).astype(bf16)

    pre7, p7 = backward(7, 0, 1, last, prod, w_in)
    s7 = swap(p7)
    pre6, p6 = backward(6, 0, 1, far, after(prod, p7), w_in)
    pre4, p4, p5 = backward(4, 2, 2, mid, after(prod, p6), w_in)
    s5 = swap(p5)
    r6 = plus(p6, after(s7, p4))
    from_below = up(r6[:HALF])
    from_above = down(r6[HALF:])
    pre2, p2, p3 = backward(2, 0, 2, mid, after(prod, r6), w_in)
    s3 = swap(p3)
    r4 = plus(p4, after(s5, p2))
    low_b = up(r4[HALF:])
    pre0, p0, p1 = backward(0, 0, 2, near, after(prod, r4), w_in)
    s1 = swap(p1)
    r2 = plus(p2, after(s3, p0))
    high_a = down(r2[:HALF])
    low_a = up(plus(r4[:HALF], from_below))
    high_b = down(plus(r2[HALF:], from_above))
    grad_w_in = grad_in(
        a, b, [after(pre0, r2), pre2, pre4, pre6, pre7], width, hidden
    )
    settled = call(
        settle_kernel,
        shape_of(PEERS, PAD, width),
        [after(p0, grad_w_in), s1, low_a, low_b, high_a, high_b],
    )
    back = exchange(settled)
    grad_w_out = grad_out(pooled, after(rows, settled), width, hidden)
    grad_flat = call(
        tail_kernel, shape_of(row_count, width), [ids, places, flat, ln_gain, grad_own, after(back, grad_w_out)]
    )
    return (grad_flat.reshape(tokens.shape), grad_w_in, grad_w_out)


def solution(mesh):
    placed = (
        P(("dp", "expert"), None, None, None),
        P(("dp", "expert"), None, None),
        P(("dp", "expert"), None, None),
        P(),
        P("expert", None, "dp"),
        P("expert", "dp", None),
    )
    return jax.shard_map(
        body,
        mesh=mesh,
        in_specs=placed,
        out_specs=(
            P(("dp", "expert"), None, None, None),
            P("expert", None, "dp"),
            P("expert", "dp", None),
        ),
        check_vma=False,
    )
```

```python
import functools
import math

import jax
import jax.numpy as jnp
from jax import lax
from jax.experimental import pallas as pl
from jax.experimental.pallas import tpu as pltpu
from jax.sharding import PartitionSpec as P

norm_eps = 1e-06
objective_scale = 32.0
bf16 = jnp.bfloat16
f32 = jnp.float32
i32 = jnp.int32

CAP = 6
HELD = 2
GROUP = HELD * CAP
PEERS = 16
PLANES = 4
HALF = PEERS * CAP
ROWS = 2 * HALF + 16
POOLED = 2 * PEERS
LANES = 128
QUAD = 4 * GROUP
REST = 32
MESSAGE = 2 * QUAD + REST
PAIR_TOKENS = 64


def nn(a, b):
    return lax.dot_general(a, b, (((1,), (0,)), ((), ())), preferred_element_type=f32)


def nt(a, b, precision=None):
    return lax.dot_general(
        a, b, (((1,), (1,)), ((), ())), precision=precision, preferred_element_type=f32
    )


def tn(a, b, precision=None):
    return lax.dot_general(
        a, b, (((0,), (0,)), ((), ())), precision=precision, preferred_element_type=f32
    )


def iota(shape, dim):
    return lax.broadcasted_iota(i32, shape, dim)


def shape_of(*dims, dtype=bf16):
    return jax.ShapeDtypeStruct(dims, dtype)


def call(kernel, out, args, flops=0, nbytes=0, smem=(), scratch=(), vmem=14):
    specs = [
        pl.BlockSpec(memory_space=pltpu.SMEM if k in smem else pltpu.VMEM)
        for k in range(len(args))
    ]
    many = isinstance(out, (list, tuple))
    out_specs = [pl.BlockSpec(memory_space=pltpu.VMEM) for _ in (out if many else [out])]
    return pl.pallas_call(
        kernel,
        out_shape=out,
        in_specs=specs,
        out_specs=out_specs if many else out_specs[0],
        scratch_shapes=list(scratch),
        compiler_params=pltpu.CompilerParams(vmem_limit_bytes=vmem * 1024 * 1024),
        cost_estimate=pl.CostEstimate(flops=flops, bytes_accessed=nbytes, transcendentals=0),
    )(*args)


def normal_parts(x):
    centred = x - jnp.mean(x, axis=-1, keepdims=True)
    spread = jnp.mean(centred * centred, axis=-1, keepdims=True)
    scale = lax.rsqrt(spread + norm_eps)
    return centred * scale, scale


def places(ids_ref, slots_ref):
    pos = ids_ref[...] * CAP + slots_ref[...]
    return jnp.concatenate([pos[:1], pos[1:]], axis=1)


def one_hot(hit):
    return jnp.where(hit, 1.0, 0.0).astype(bf16)


def slot_table(pos, span, at):
    tokens = pos.shape[1]
    row = iota((PEERS * span, tokens), 0)
    inner = row % span - at
    return one_hot(((row // span) * GROUP + inner == pos) & (inner >= 0) & (inner < GROUP))


def dispatch_kernel(me_ref, ids_ref, slots_ref, tok_ref, gain_ref, out_ref):
    pos = places(ids_ref, slots_ref)
    tokens = pos.shape[1]
    normed = normal_parts(tok_ref[...].astype(f32))[0] * gain_ref[...].reshape(1, -1)
    normed = normed.astype(bf16)

    def column(j):
        return normed[:, j * LANES : (j + 1) * LANES]

    quads = None
    for at in range(4):
        both = jnp.concatenate([column(at), column(at + 4)], axis=1)
        part = nn(slot_table(pos, QUAD, at * GROUP), both)
        quads = part if quads is None else quads + part
    row = iota((PEERS * REST, tokens), 0)
    held = row % REST - 2 * GROUP
    goes = one_hot((pos // GROUP == row // REST) & ((pos % GROUP) // CAP == held))
    kind = jnp.where(iota((LANES, tokens), 1) < tokens // 2, 1.0, 2.0)
    lane = iota((LANES, tokens), 0)
    rest = nt(goes, jnp.where(lane == me_ref[0] * CAP + pos % CAP, kind, 0.0).astype(bf16))
    for at in range(2):
        rest = rest + nn(slot_table(pos, REST, at * GROUP), column(8 + at))
    first = quads[:, :LANES].astype(bf16).reshape(PEERS, QUAD, LANES)
    second = quads[:, LANES:].astype(bf16).reshape(PEERS, QUAD, LANES)
    rest = rest.astype(bf16).reshape(PEERS, REST, LANES)
    for plane in range(PLANES):
        to = slice(plane * PEERS, (plane + 1) * PEERS)
        out_ref[to, :QUAD, :] = first
        out_ref[to, QUAD : 2 * QUAD, :] = second
        out_ref[to, 2 * QUAD :, :] = rest


def row_table(span, at, back):
    shape = (PEERS * span, 2 * HALF) if back else (2 * HALF, PEERS * span)
    r = iota(shape, 1 if back else 0)
    inner = r % HALF
    want = (inner // CAP) * span + at + (r // HALF) * CAP + inner % CAP
    return one_hot(iota(shape, 0 if back else 1) == want)


def repack_kernel(in_ref, out_ref):
    quad = [row_table(QUAD, at * GROUP, False) for at in range(4)]
    rest = [row_table(REST, at * GROUP, False) for at in range(2)]
    row = iota((16, PEERS * REST), 0)
    kinds = one_hot(iota((16, PEERS * REST), 1) % REST - 2 * GROUP == row)
    kinds = jnp.where(row < HELD, kinds, jnp.zeros_like(kinds))
    for plane in range(PLANES):
        of = slice(plane * PEERS, (plane + 1) * PEERS)
        first = in_ref[of, :QUAD, :].reshape(PEERS * QUAD, LANES)
        second = in_ref[of, QUAD : 2 * QUAD, :].reshape(PEERS * QUAD, LANES)
        both = jnp.concatenate([first, second], axis=1)
        for at in range(4):
            got = nn(quad[at], both).astype(bf16)
            out_ref[plane, : 2 * HALF, at * LANES : (at + 1) * LANES] = got[:, :LANES]
            out_ref[plane, : 2 * HALF, (at + 4) * LANES : (at + 5) * LANES] = got[:, LANES:]
        last = in_ref[of, 2 * QUAD :, :].reshape(PEERS * REST, LANES)
        for at in range(2):
            got = nn(rest[at], last).astype(bf16)
            out_ref[plane, : 2 * HALF, (at + 8) * LANES : (at + 9) * LANES] = got
        out_ref[plane, 2 * HALF :, :LANES] = nn(kinds, last).astype(bf16)
        width = out_ref.shape[2]
        out_ref[plane, 2 * HALF :, LANES:] = jnp.zeros((16, width - LANES), bf16)


def forward_kernel(x_ref, w_in, pooled_ref, slope_ref, pool_ref):
    c0 = math.sqrt(2.0 / math.pi)
    c1 = c0 * 0.044715
    hidden = w_in.shape[2]
    for plane in range(PLANES):
        kinds = x_ref[plane, 2 * HALF :, :LANES].astype(f32)
        for held in range(HELD):
            rows = x_ref[plane, held * HALF : (held + 1) * HALF, :]
            q = iota((POOLED, HALF), 0)
            r = iota((POOLED, HALF), 1)
            kind = kinds[held : held + 1, :HALF]
            pool = one_hot((q % PEERS == r // CAP) & (kind == (q // PEERS + 1).astype(f32)))
            pool_ref[plane, held] = pool
            for at in range(0, hidden, 256):
                to = slice(at, min(at + 256, hidden))
                h = nn(rows, w_in[held, :, to])
                h2 = h * h
                t = jnp.tanh(h * (c0 + c1 * h2))
                half = 0.5 + 0.5 * t
                act = h * half
                slope = half + act * (1.0 - t) * (c0 + 3.0 * c1 * h2)
                pooled_ref[plane, held, :, to] = nn(pool, act.astype(bf16)).astype(bf16)
                slope_ref[plane, held, :, to] = slope.astype(bf16)


def forward(x, w_in):
    width, hidden = w_in.shape[1:]
    return call(
        forward_kernel,
        [
            shape_of(PLANES, HELD, POOLED, hidden),
            shape_of(PLANES, HELD, HALF, hidden),
            shape_of(PLANES, HELD, POOLED, HALF),
        ],
        [x, w_in],
        flops=PLANES * 2 * 2 * HALF * width * hidden,
        nbytes=w_in.size * 2 + PLANES * 2 * HALF * (width + hidden) * 2,
    )


def out_kernel(pooled_ref, w_out, out_ref):
    total = None
    for held in range(HELD):
        rows = jnp.concatenate([pooled_ref[k, held] for k in range(PLANES)], axis=0)
        part = nn(rows, w_out[held])
        total = part if total is None else total + part
    out_ref[...] = total.astype(bf16).reshape(out_ref.shape)


def loss_kernel(own_ref, other_ref, w_out, grad_ref, rows_ref, prod_ref):
    highest = lax.Precision.HIGHEST
    image = jnp.concatenate([own_ref[0], other_ref[0]], axis=0)
    text = jnp.concatenate([own_ref[1], other_ref[1]], axis=0)
    pairs, width = image.shape
    scale = PAIR_TOKENS / math.sqrt(width)
    logits = scale * nt(image, text, highest)

    def softmax(axis):
        top = jnp.exp(logits - jnp.max(logits, axis=axis, keepdims=True))
        return top / jnp.sum(top, axis=axis, keepdims=True)

    same = jnp.where(iota((pairs, pairs), 0) == iota((pairs, pairs), 1), 2.0, 0.0)
    grad_logits = objective_scale * (softmax(1) + softmax(0) - same)
    grad_image = (scale / PAIR_TOKENS) * lax.dot_general(
        grad_logits,
        text,
        (((1,), (0,)), ((), ())),
        precision=highest,
        preferred_element_type=f32,
    )
    grad_text = (scale / PAIR_TOKENS) * tn(grad_logits, image, highest)
    grad_ref[0] = grad_image
    grad_ref[1] = grad_text
    for core in range(2):
        for plane in range(PLANES):
            first = (core * PLANES + plane) * PEERS
            span = slice(first, first + PEERS)
            rows_ref[core, plane, :PEERS, :] = grad_image[span].astype(bf16)
            rows_ref[core, plane, PEERS:, :] = grad_text[span].astype(bf16)
    for core in range(2):
        rows = rows_ref[core].reshape(PLANES * POOLED, width)
        for held in range(HELD):
            prod_ref[core, held] = nt(rows, w_out[held]).astype(bf16)


def backward_kernel(core, pool_ref, slope_ref, prod_ref, w_in, pre_ref, out_ref):
    for held in range(HELD):
        for plane in range(PLANES):
            prod = prod_ref[core, held, plane * POOLED : (plane + 1) * POOLED, :]
            grad_act = tn(pool_ref[plane, held], prod)
            pre = (grad_act * slope_ref[plane, held].astype(f32)).astype(bf16)
            pre_ref[plane, held] = pre
        pre = pre_ref[:, held].reshape(PLANES * HALF, -1)
        part = nt(pre, w_in[held]).astype(bf16)
        for plane in range(PLANES):
            span = slice(plane * HALF, (plane + 1) * HALF)
            out_ref[plane, held * HALF : (held + 1) * HALF, :] = part[span]


def backward(core, made, prod, w_in):
    width, hidden = w_in.shape[1:]
    return call(
        functools.partial(backward_kernel, core),
        [shape_of(PLANES, HELD, HALF, hidden), shape_of(PLANES, 2 * HALF, width)],
        [made[2], made[1], prod, w_in],
        flops=PLANES * 2 * 2 * HALF * width * hidden,
        nbytes=w_in.size * 2 + PLANES * 2 * HALF * (width + hidden) * 2,
    )


def unpack_kernel(own_ref, got_ref, out_ref):
    quad = [row_table(QUAD, at * GROUP, True) for at in range(4)]
    rest = [row_table(REST, at * GROUP, True) for at in range(2)]
    for plane in range(PLANES):
        of = slice(plane * PEERS, (plane + 1) * PEERS)
        rows = (own_ref[plane].astype(f32) + got_ref[plane].astype(f32)).astype(bf16)

        def column(j):
            return rows[:, j * LANES : (j + 1) * LANES]

        total = None
        for at in range(4):
            both = jnp.concatenate([column(at), column(at + 4)], axis=1)
            part = nn(quad[at], both)
            total = part if total is None else total + part
        total = total.astype(bf16)
        out_ref[of, :QUAD, :] = total[:, :LANES].reshape(PEERS, QUAD, LANES)
        out_ref[of, QUAD : 2 * QUAD, :] = total[:, LANES:].reshape(PEERS, QUAD, LANES)
        last = nn(rest[0], column(8)) + nn(rest[1], column(9))
        out_ref[of, 2 * QUAD :, :] = last.astype(bf16).reshape(PEERS, REST, LANES)


def grad_in_kernel(own_ref, other_ref, own_pre, other_pre, out_ref, x_ref, p_ref):
    held = pl.program_id(0)

    def fill(which):
        for core, (x, pre) in enumerate(((own_ref, own_pre), (other_ref, other_pre))):
            for plane in range(PLANES):
                first = (core * PLANES + plane) * HALF
                x_ref[first : first + HALF, :] = x[plane, which * HALF : (which + 1) * HALF, :]
                p_ref[first : first + HALF, :] = pre[plane, which]

    for which in range(HELD):
        pl.when(held == which)(functools.partial(fill, which))
    out_ref[0] = tn(x_ref[...], p_ref[...])


def grad_in(own, other, own_pre, other_pre, width, hidden):
    whole = pl.BlockSpec(memory_space=pltpu.VMEM)
    return pl.pallas_call(
        grad_in_kernel,
        grid=(HELD,),
        out_shape=shape_of(HELD, width, hidden, dtype=f32),
        in_specs=[whole] * 4,
        out_specs=pl.BlockSpec((1, width, hidden), lambda i: (i, 0, 0)),
        scratch_shapes=[
            pltpu.VMEM((8 * HALF, width), bf16),
            pltpu.VMEM((8 * HALF, hidden), bf16),
        ],
        compiler_params=pltpu.CompilerParams(vmem_limit_bytes=26 * 1024 * 1024),
        cost_estimate=pl.CostEstimate(
            flops=2 * 2 * 8 * HALF * width * hidden, bytes_accessed=17_000_000, transcendentals=0
        ),
    )(own, other, own_pre, other_pre)


def grad_out_kernel(own_ref, other_ref, rows_ref, out_ref):
    held = pl.program_id(0)
    width = rows_ref.shape[3]
    pooled = [ref[k, held] for ref in (own_ref, other_ref) for k in range(PLANES)]
    rows = rows_ref[...].reshape(8 * POOLED, width)
    out_ref[0] = tn(jnp.concatenate(pooled, axis=0), rows)


def grad_out(own, other, rows, width, hidden):
    whole = pl.BlockSpec(memory_space=pltpu.VMEM)
    return pl.pallas_call(
        grad_out_kernel,
        grid=(HELD,),
        out_shape=shape_of(HELD, hidden, width, dtype=f32),
        in_specs=[whole] * 3,
        out_specs=pl.BlockSpec((1, hidden, width), lambda i: (i, 0, 0)),
        compiler_params=pltpu.CompilerParams(vmem_limit_bytes=18 * 1024 * 1024),
        cost_estimate=pl.CostEstimate(
            flops=2 * 2 * 8 * POOLED * width * hidden, bytes_accessed=9_000_000, transcendentals=0
        ),
    )(own, other, rows)


def tail_kernel(ids_ref, slots_ref, tok_ref, gain_ref, grad_ref, back_ref, out_ref, sum_ref):
    tokens = tok_ref.shape[0]
    pos = places(ids_ref, slots_ref)
    for peer in range(0, PEERS, 4):
        total = None
        for plane in range(PLANES):
            first = plane * PEERS + peer
            part = back_ref[first : first + 4].astype(f32)
            total = part if total is None else total + part
        sum_ref[peer : peer + 4] = total.astype(bf16)
    first = sum_ref[:, :QUAD, :].reshape(PEERS * QUAD, LANES)
    second = sum_ref[:, QUAD : 2 * QUAD, :].reshape(PEERS * QUAD, LANES)
    both = jnp.concatenate([first, second], axis=1)
    quads = [tn(slot_table(pos, QUAD, at * GROUP), both) for at in range(4)]
    last = sum_ref[:, 2 * QUAD :, :].reshape(PEERS * REST, LANES)
    ends = [tn(slot_table(pos, REST, at * GROUP), last) for at in range(2)]
    grad = jnp.concatenate(
        [g[:, :LANES] for g in quads] + [g[:, LANES:] for g in quads] + ends, axis=1
    )
    unit, scale = normal_parts(tok_ref[...].astype(f32))
    grad = grad * gain_ref[...].reshape(1, -1)
    grad = scale * (
        grad
        - jnp.mean(grad, axis=-1, keepdims=True)
        - unit * jnp.mean(grad * unit, axis=-1, keepdims=True)
    )
    for half in range(2):
        span = slice(half * (tokens // 2), (half + 1) * (tokens // 2))
        out_ref[span, :] = (grad_ref[half : half + 1, :] + grad[span]).astype(bf16)


def body(tokens, expert_ids, slots, ln_gain, w_in, w_out):
    width, hidden = w_in.shape[1:]
    row_count = tokens.shape[1] * tokens.shape[2]
    flat = tokens.reshape(row_count, width)
    ids, slot = expert_ids[0], slots[0]
    data = lax.axis_index("dp")
    group = lax.axis_index("expert")
    everyone = ("dp", "expert")
    chips = PLANES * PEERS
    cores = [[d * PEERS + e for d in range(c, 8, 2) for e in range(PEERS)] for c in range(2)]

    def swap(x):
        return lax.ppermute(x, "dp", [(i, i ^ 1) for i in range(8)])

    def after(x, *tokens):
        return lax.optimization_barrier((x, *tokens))[0]

    def spread(x):
        return lax.all_to_all(
            x, everyone, split_axis=0, concat_axis=0, tiled=True, axis_index_groups=cores
        )

    sent = call(
        dispatch_kernel,
        shape_of(chips, MESSAGE, LANES),
        [group.reshape(1), ids, slot, flat, ln_gain],
        smem=(0,),
    )
    x_own = call(repack_kernel, shape_of(PLANES, ROWS, width), [spread(sent)])
    x_other = swap(x_own)
    made_own = forward(x_own, w_in)

    def product(made, w_out):
        return call(
            out_kernel,
            shape_of(PLANES, POOLED, width),
            [made[0], w_out],
            flops=2 * 4 * POOLED * width * hidden * HELD,
            nbytes=w_out.size * 2,
        )

    own = product(made_own, w_out)
    made_other = forward(after(x_other, own), w_in)
    got = swap(product(made_other, w_out))
    joined = (own.astype(f32) + got.astype(f32)).astype(bf16)
    joined = joined.reshape(PLANES, 2, PEERS, width).transpose(0, 2, 1, 3)
    parts = spread(joined.reshape(chips, 2, width))
    emb = jnp.sum(parts.astype(f32), axis=0) + jnp.sum(
        flat.reshape(2, PAIR_TOKENS, width).astype(f32), axis=1
    )
    emb = spread(jnp.broadcast_to((emb / PAIR_TOKENS)[None], (chips, 2, width)))
    emb = emb.transpose(1, 0, 2)
    grad_pooled, rows, prod = call(
        loss_kernel,
        [
            shape_of(2, 2 * chips, width, dtype=f32),
            shape_of(2, PLANES, POOLED, width),
            shape_of(2, HELD, PLANES * POOLED, hidden),
        ],
        [emb, swap(emb), w_out],
        flops=2 * 8 * POOLED * width * hidden * HELD,
        nbytes=w_out.size * 2,
    )
    grad_own = lax.dynamic_index_in_dim(
        grad_pooled, (data // 2) * PEERS + group, axis=1, keepdims=False
    )
    pre_other, p_other = backward(1, made_other, prod, w_in)
    p_got = swap(p_other)
    pre_own, p_own = backward(0, made_own, after(prod, p_other), w_in)
    packed = call(unpack_kernel, shape_of(chips, MESSAGE, LANES), [p_own, p_got])
    back = spread(packed)
    grad_w_in = grad_in(x_own, x_other, after(pre_own, packed), pre_other, width, hidden)
    grad_w_out = grad_out(
        made_own[0], made_other[0], after(rows, packed), width, hidden
    )
    grad_flat = call(
        tail_kernel,
        shape_of(row_count, width),
        [ids, slot, flat, ln_gain, grad_own, after(back, grad_w_in, grad_w_out)],
        scratch=[pltpu.VMEM((PEERS, MESSAGE, LANES), bf16)],
    )
    return (grad_flat.reshape(tokens.shape), grad_w_in, grad_w_out)


def solution(mesh):
    placed = (
        P(("dp", "expert"), None, None, None),
        P(("dp", "expert"), None, None),
        P(("dp", "expert"), None, None),
        P(),
        P("expert", None, "dp"),
        P("expert", "dp", None),
    )
    return jax.shard_map(
        body,
        mesh=mesh,
        in_specs=placed,
        out_specs=(
            P(("dp", "expert"), None, None, None),
            P("expert", None, "dp"),
            P("expert", "dp", None),
        ),
        check_vma=False,
    )
```

```python
import functools
import math

import jax
import jax.numpy as jnp
from jax import lax
from jax.experimental import pallas as pl
from jax.experimental.pallas import tpu as pltpu
from jax.sharding import PartitionSpec as P

norm_eps = 1e-06
objective_scale = 32.0
bf16 = jnp.bfloat16
f32 = jnp.float32
i32 = jnp.int32

CAP = 6
HELD = 2
GROUP = HELD * CAP
PAD = 16
PEERS = 16
HALF = PEERS * CAP
KIND_ROWS = 16
POOLED = 2 * PEERS
PAIR_TOKENS = 64
LANES = 128
AROUND = (0, 4, 6, 2)


def nn(a, b):
    return lax.dot_general(a, b, (((1,), (0,)), ((), ())), preferred_element_type=f32)


def nt(a, b, precision=None):
    return lax.dot_general(
        a, b, (((1,), (1,)), ((), ())), precision=precision, preferred_element_type=f32
    )


def tn(a, b, precision=None):
    return lax.dot_general(
        a, b, (((0,), (0,)), ((), ())), precision=precision, preferred_element_type=f32
    )


def iota(shape, dim):
    return lax.broadcasted_iota(i32, shape, dim)


def shape_of(*dims, dtype=bf16):
    return jax.ShapeDtypeStruct(dims, dtype)


def one_hot(hit):
    return jnp.where(hit, 1.0, 0.0).astype(bf16)


def call(kernel, out, args, smem=(), hbm=(), scratch=(), vmem=14, cost=None):
    def space(k):
        return pltpu.SMEM if k in smem else pltpu.HBM if k in hbm else pltpu.VMEM

    many = isinstance(out, (list, tuple))
    out_specs = [pl.BlockSpec(memory_space=pltpu.VMEM) for _ in (out if many else [out])]
    return pl.pallas_call(
        kernel,
        out_shape=out,
        in_specs=[pl.BlockSpec(memory_space=space(k)) for k in range(len(args))],
        out_specs=out_specs if many else out_specs[0],
        scratch_shapes=list(scratch),
        compiler_params=pltpu.CompilerParams(vmem_limit_bytes=vmem * 1024 * 1024),
        cost_estimate=cost,
    )(*args)


def normal_parts(x):
    centred = x - jnp.mean(x, axis=-1, keepdims=True)
    spread = jnp.mean(centred * centred, axis=-1, keepdims=True)
    scale = lax.rsqrt(spread + norm_eps)
    return centred * scale, scale


def places(ids_ref, slots_ref):
    pos = ids_ref[...] * CAP + slots_ref[...]
    return jnp.concatenate([pos[:1], pos[1:]], axis=1)


def slot_table(pos):
    tokens = pos.shape[1]
    row = iota((PEERS * PAD, tokens), 0)
    want = (row // PAD) * GROUP + row % PAD
    return one_hot((want == pos) & (row % PAD < GROUP))


def fetch(sources, refs, sems):
    copies = [pltpu.make_async_copy(a, b, sems.at[k]) for k, (a, b) in enumerate(zip(sources, refs))]
    for copy in copies:
        copy.start()
    return copies


def input_scratch(tokens, width):
    return [
        pltpu.VMEM((2, tokens // 2), i32),
        pltpu.VMEM((2, tokens // 2), i32),
        pltpu.VMEM((tokens, width), bf16),
        pltpu.VMEM((width,), f32),
        pltpu.SemaphoreType.DMA((4,)),
    ]


def dispatch_kernel(ids, slots, toks, gain, out_ref, sum_ref, ids_ref, slots_ref, tok_ref, gain_ref, sems):
    copies = fetch((ids, slots, toks, gain), (ids_ref, slots_ref, tok_ref, gain_ref), sems)
    for copy in copies:
        copy.wait()
    pos = places(ids_ref, slots_ref)
    tokens = pos.shape[1]
    x = tok_ref[...].astype(f32)
    normed = normal_parts(x)[0] * gain_ref[...].reshape(1, -1)
    normed = normed.astype(bf16)
    sent = nn(slot_table(pos), normed)
    row = iota((PEERS * PAD, tokens), 0)
    goes = one_hot((row % PAD == GROUP) & (pos // GROUP == row // PAD))
    place = pos % GROUP
    column = (place // CAP) * 128 + lax.axis_index("expert") * CAP + place % CAP
    lane = iota((2 * 128, tokens), 0)
    kind = jnp.where(iota((2 * 128, tokens), 1) < tokens // 2, 1.0, 2.0)
    kinds = nt(goes, jnp.where(lane == column, kind, 0.0).astype(bf16))
    width = sent.shape[1]
    first = sent[:, : 2 * 128] + kinds
    out_ref[:, :, : 2 * 128] = first.astype(bf16).reshape(PEERS, PAD, 2 * 128)
    out_ref[:, :, 2 * 128 :] = sent[:, 2 * 128 :].astype(bf16).reshape(
        PEERS, PAD, width - 2 * 128
    )
    sum_ref[0:1, :] = jnp.sum(x[: tokens // 2], axis=0, keepdims=True)
    sum_ref[1:2, :] = jnp.sum(x[tokens // 2 :], axis=0, keepdims=True)


def repack_table(rows, back):
    shape = (PEERS * PAD, rows) if back else (rows, PEERS * PAD)
    r = iota(shape, 1 if back else 0)
    m = iota(shape, 0 if back else 1)
    held, rest = r // HALF, r % HALF
    from_slot = (rest // CAP) * PAD + held * CAP + rest % CAP
    hit = (r < 2 * HALF) & (m == from_slot)
    if not back:
        hit = hit | ((r == 2 * HALF) & (m % PAD == GROUP))
    return one_hot(hit)


def repack_kernel(in_ref, first_ref, second_ref):
    width = in_ref.shape[2]
    rows = 2 * HALF + KIND_ROWS
    out = nn(repack_table(rows, False), in_ref[...].reshape(PEERS * PAD, width)).astype(bf16)
    first_ref[...] = out[:HALF]
    second_ref[...] = out[HALF:]


def pool_table(seconds, held, wide_ref):
    count = len(seconds)
    wide_ref[...] = jnp.zeros_like(wide_ref)
    q = iota((POOLED, LANES), 0)
    r = iota((POOLED, LANES), 1)
    for k in range(count):
        kinds = seconds[k][HALF : HALF + KIND_ROWS, held * LANES : (held + 1) * LANES]
        kinds = kinds.astype(f32)[:1]
        hit = (q % PEERS == r // CAP) & (kinds == (q // PEERS + 1).astype(f32)) & (r < HALF)
        wide_ref[k * POOLED : (k + 1) * POOLED, k * LANES : (k + 1) * LANES] = one_hot(hit)


def forward_kernel(count, *refs):
    halves = refs[:count], refs[count : 2 * count]
    w_in, pooled_ref, slope_ref, wide_ref, act_ref = refs[2 * count :]
    c0 = math.sqrt(2.0 / math.pi)
    c1 = c0 * 0.044715
    hidden = w_in.shape[2]
    for held in range(HELD):
        pool_table(halves[1], held, wide_ref)
        rows = jnp.concatenate([ref[:HALF, :] for ref in halves[held]], axis=0)
        for at in range(0, hidden, 256):
            to = slice(at, min(at + 256, hidden))
            full = nn(rows, w_in[held, :, to])
            for k in range(count):
                h = full[k * HALF : (k + 1) * HALF]
                h2 = h * h
                t = jnp.tanh(h * (c0 + c1 * h2))
                half = 0.5 + 0.5 * t
                act = h * half
                slope = half + act * (1.0 - t) * (c0 + 3.0 * c1 * h2)
                slope_ref[k, held, :, to] = slope.astype(bf16)
                act_ref[k * LANES : k * LANES + HALF, to] = act.astype(bf16)
        for k in range(count):
            act_ref[k * LANES + HALF : (k + 1) * LANES, :] = jnp.zeros(
                (LANES - HALF, hidden), bf16
            )
        pooled = nn(wide_ref[...], act_ref[...]).astype(bf16)
        for k in range(count):
            pooled_ref[k, held] = pooled[k * POOLED : (k + 1) * POOLED]


def forward(firsts, seconds, w_in):
    count = len(firsts)
    hidden = w_in.shape[2]
    return call(
        functools.partial(forward_kernel, count),
        [
            shape_of(count, HELD, POOLED, hidden),
            shape_of(count, HELD, HALF, hidden),
        ],
        [*firsts, *seconds, w_in],
        scratch=[
            pltpu.VMEM((count * POOLED, count * LANES), bf16),
            pltpu.VMEM((count * LANES, hidden), bf16),
        ],
    )


def part_of(parts, k):
    if k < 2:
        return parts[0], k
    if k < 6:
        return parts[1], k - 2
    return parts[2], k - 6


def out_kernel(shift, a_ref, b_ref, c_ref, w_out, out_ref):
    total = None
    for held in range(HELD):
        rows = []
        for k in AROUND:
            ref, at = part_of((a_ref, b_ref, c_ref), k + shift)
            rows.append(ref[at, held])
        part = nn(jnp.concatenate(rows, axis=0), w_out[held])
        total = part if total is None else total + part
    out_ref[...] = total.astype(bf16).reshape(out_ref.shape)


def join_kernel(own_ref, got_ref, out_ref):
    for ahead in range(4):
        to = lax.rem(lax.axis_index("dp") // 2 + ahead, 4)
        out_ref[to] = (own_ref[ahead].astype(f32) + got_ref[ahead].astype(f32)).astype(bf16)


def mean_kernel(part_ref, sum_ref, out_ref):
    total = sum_ref[...]
    for first in range(0, part_ref.shape[0], 8):
        total = total + jnp.sum(part_ref[first : first + 8].astype(f32), axis=0)
    out_ref[...] = jnp.broadcast_to((total * (1.0 / PAIR_TOKENS))[None], out_ref.shape)


def split(x):
    high = x.astype(bf16)
    return high, (x - high.astype(f32)).astype(bf16)


def loss_kernel(own_ref, other_ref, w_out, grad_ref, rows_ref, prod_ref, gi_ref, gt_ref):
    image = jnp.concatenate([own_ref[0], other_ref[0]], axis=0)
    text = jnp.concatenate([own_ref[1], other_ref[1]], axis=0)
    pairs, width = image.shape
    scale = PAIR_TOKENS / math.sqrt(width)
    logits = scale * nt(image, text, lax.Precision.HIGHEST)

    def softmax(axis):
        top = jnp.exp(logits - jnp.max(logits, axis=axis, keepdims=True))
        return top / jnp.sum(top, axis=axis, keepdims=True)

    same = jnp.where(iota((pairs, pairs), 0) == iota((pairs, pairs), 1), 2.0, 0.0)
    grad_logits = (objective_scale * scale / PAIR_TOKENS) * (softmax(1) + softmax(0) - same)

    def thrice(g, x):
        (g0, g1), (x0, x1) = split(g), split(x)
        return nn(g0, x0) + (nn(g0, x1) + nn(g1, x0))

    grad_image = thrice(grad_logits, text)
    grad_text = thrice(grad_logits.T, image)
    grad_ref[0] = grad_image
    grad_ref[1] = grad_text
    gi_ref[...] = grad_image.astype(bf16)
    gt_ref[...] = grad_text.astype(bf16)
    for at, k in enumerate(AROUND):
        for other in range(2):
            first = other * 4 * PEERS + lax.rem(lax.axis_index("dp") // 2 + at, 4) * PEERS
            span = pl.ds(pl.multiple_of(first, PEERS), PEERS)
            rows_ref[k + other, :PEERS, :] = gi_ref[span, :]
            rows_ref[k + other, PEERS:, :] = gt_ref[span, :]
    rows = rows_ref[...].reshape(8 * POOLED, width)
    for held in range(HELD):
        prod_ref[held] = nt(rows, w_out[held]).astype(bf16)


def backward_kernel(blocks, *refs):
    count = len(blocks)
    seconds, slopes = refs[:count], refs[count : 2 * count]
    prod_ref, w_in, pre_ref = refs[2 * count : 2 * count + 3]
    outs = refs[2 * count + 3 : 3 * count + 3]
    wide_ref, prods_ref = refs[3 * count + 3 :]
    for held in range(HELD):
        pool_table(seconds, held, wide_ref)
        for k, block in enumerate(blocks):
            prods_ref[k * POOLED : (k + 1) * POOLED, :] = prod_ref[
                held, block * POOLED : (block + 1) * POOLED, :
            ]
        grad_act = tn(wide_ref[...], prods_ref[...])
        for k, block in enumerate(blocks):
            slope = slopes[k][part_of((None,) * 3, block)[1], held].astype(f32)
            pre_ref[k, held] = (grad_act[k * LANES : k * LANES + HALF] * slope).astype(bf16)
        pre = jnp.concatenate([pre_ref[k, held] for k in range(count)], axis=0)
        part = nt(pre, w_in[held]).astype(bf16)
        for k in range(count):
            outs[k][held * HALF : (held + 1) * HALF, :] = part[k * HALF : (k + 1) * HALF]


def backward(blocks, seconds, made, prod, w_in):
    count = len(blocks)
    width, hidden = w_in.shape[1:]
    of = [part_of(made, block)[0] for block in blocks]
    return call(
        functools.partial(backward_kernel, blocks),
        [shape_of(count, HELD, HALF, hidden)] + [shape_of(2 * HALF, width)] * count,
        [*[seconds[block] for block in blocks], *[m[1] for m in of], prod, w_in],
        scratch=[
            pltpu.VMEM((count * POOLED, count * LANES), bf16),
            pltpu.VMEM((count * POOLED, hidden), bf16),
        ],
    )


PAIRED = {7: (0, 0), 5: (0, 1), 6: (1, 0), 4: (1, 1), 3: (2, 0), 1: (2, 1), 2: (3, 0), 0: (3, 1)}


def grad_in_kernel(*refs):
    blocks, pres = refs[:16], refs[16:20]
    out_ref, x_ref, p_ref = refs[20:]
    held = pl.program_id(0)

    def fill(which):
        for k in range(8):
            span = slice(k * HALF, (k + 1) * HALF)
            x_ref[span, :] = blocks[8 * which + k][:HALF, :]
            pair, at = PAIRED[k]
            p_ref[span, :] = pres[pair][at, which]

    for which in range(HELD):
        pl.when(held == which)(functools.partial(fill, which))
    out_ref[0] = tn(x_ref[...], p_ref[...])


def grad_in(firsts, seconds, pres, width, hidden):
    whole = pl.BlockSpec(memory_space=pltpu.VMEM)
    return pl.pallas_call(
        grad_in_kernel,
        grid=(HELD,),
        out_shape=shape_of(HELD, width, hidden, dtype=f32),
        in_specs=[whole] * 20,
        out_specs=pl.BlockSpec((1, width, hidden), lambda i: (i, 0, 0)),
        scratch_shapes=[
            pltpu.VMEM((8 * HALF, width), bf16),
            pltpu.VMEM((8 * HALF, hidden), bf16),
        ],
        compiler_params=pltpu.CompilerParams(vmem_limit_bytes=26 * 1024 * 1024),
    )(*firsts, *seconds, *pres)


def grad_out_kernel(a_ref, b_ref, c_ref, rows_ref, out_ref):
    held = pl.program_id(0)
    width = rows_ref.shape[2]
    pooled = []
    for k in range(8):
        ref, at = part_of((a_ref, b_ref, c_ref), k)
        pooled.append(ref[at, held])
    out_ref[0] = tn(jnp.concatenate(pooled, axis=0), rows_ref[...].reshape(8 * POOLED, width))


def grad_out(pooled, rows, width, hidden):
    whole = pl.BlockSpec(memory_space=pltpu.VMEM)
    return pl.pallas_call(
        grad_out_kernel,
        grid=(HELD,),
        out_shape=shape_of(HELD, hidden, width, dtype=f32),
        in_specs=[whole] * 4,
        out_specs=pl.BlockSpec((1, hidden, width), lambda i: (i, 0, 0)),
        compiler_params=pltpu.CompilerParams(vmem_limit_bytes=18 * 1024 * 1024),
    )(*pooled, rows)


def plus_kernel(own_ref, got_ref, first_ref, second_ref):
    total = (own_ref[...].astype(f32) + got_ref[...].astype(f32)).astype(bf16)
    first_ref[...] = total[:HALF]
    second_ref[...] = total[HALF:]


def settle_kernel(own_ref, got_ref, la_ref, lb_ref, ra_ref, rb_ref, out_ref):
    width = own_ref.shape[1]
    total = own_ref[...].astype(f32) + got_ref[...].astype(f32)
    first = total[:HALF] + la_ref[...].astype(f32) + ra_ref[...].astype(f32)
    second = total[HALF:] + lb_ref[...].astype(f32) + rb_ref[...].astype(f32)
    table = repack_table(2 * HALF, True)
    rows = jnp.concatenate([first.astype(bf16), second.astype(bf16)], axis=0)
    out_ref[...] = nn(table, rows).astype(bf16).reshape(PEERS, PAD, width)


def tail_kernel(ids, slots, toks, gain, grads, back_ref, out_ref, ids_ref, slots_ref, tok_ref, gain_ref, sems, near_ref, near_sem):
    copies = fetch((ids, slots, toks, gain), (ids_ref, slots_ref, tok_ref, gain_ref), sems)
    at = (lax.axis_index("dp") // 2) * PEERS + lax.axis_index("expert")
    first = pl.multiple_of(at // 8 * 8, 8)
    near = pltpu.make_async_copy(grads.at[:, pl.ds(first, 8), :], near_ref, near_sem)
    near.start()
    for copy in copies:
        copy.wait()
    near.wait()
    width = tok_ref.shape[1]
    tokens = tok_ref.shape[0]
    back = back_ref[...].reshape(PEERS * PAD, width)
    grad_normed = tn(slot_table(places(ids_ref, slots_ref)), back)
    unit, scale = normal_parts(tok_ref[...].astype(f32))
    grad = grad_normed * gain_ref[...].reshape(1, -1)
    grad = scale * (
        grad
        - jnp.mean(grad, axis=-1, keepdims=True)
        - unit * jnp.mean(grad * unit, axis=-1, keepdims=True)
    )
    for half in range(2):
        span = slice(half * (tokens // 2), (half + 1) * (tokens // 2))
        rows = near_ref[half]
        own = jnp.where(iota(rows.shape, 0) == at % 8, rows, 0.0)
        own = jnp.sum(own, axis=0, keepdims=True)
        out_ref[span, :] = (own + grad[span]).astype(bf16)


def body(tokens, expert_ids, slots, ln_gain, w_in, w_out):
    width, hidden = w_in.shape[1:]
    row_count = tokens.shape[1] * tokens.shape[2]
    flat = tokens.reshape(row_count, width)
    ids, slot = expert_ids[0], slots[0]
    everyone = ("dp", "expert")
    chips = 4 * PEERS
    cores = [[d * PEERS + e for d in range(c, 8, 2) for e in range(PEERS)] for c in range(2)]

    def up(x):
        return lax.ppermute(x, "dp", [(i, (i + 2) % 8) for i in range(8)])

    def down(x):
        return lax.ppermute(x, "dp", [(i, (i + 6) % 8) for i in range(8)])

    def swap(x):
        return lax.ppermute(x, "dp", [(i, i ^ 1) for i in range(8)])

    def after(x, *tokens):
        return lax.optimization_barrier((x, *tokens))[0]

    def exchange(x):
        return lax.all_to_all(x, "expert", split_axis=0, concat_axis=0, tiled=True)

    def spread(x):
        return lax.all_to_all(
            x, everyone, split_axis=0, concat_axis=0, tiled=True, axis_index_groups=cores
        )

    sent, token_sum = call(
        dispatch_kernel,
        [shape_of(PEERS, PAD, width), shape_of(2, width, dtype=f32)],
        [ids, slot, flat, ln_gain],
        hbm=(0, 1, 2, 3),
        scratch=input_scratch(row_count, width),
        vmem=60,
    )
    first, second = call(
        repack_kernel,
        [shape_of(HALF, width), shape_of(HALF + KIND_ROWS, width)],
        [exchange(sent)],
    )

    a, b = [None] * 8, [None] * 8
    a[0], b[0] = first, second
    a[2] = up(first)
    b[4] = down(second)
    a[1], b[1] = swap(first), swap(second)
    b[2] = up(after(second, a[1], b[1]))
    a[4] = down(after(first, a[1], b[1]))
    a[6] = up(a[2])
    b[6] = down(b[4])
    near = forward(a[0:2], b[0:2], w_in)
    a[3], b[5] = swap(after(a[2], near[0])), swap(after(b[4], near[0]))
    a[5], b[3] = swap(a[4]), swap(b[2])
    mid = forward(a[2:6], b[2:6], w_in)
    a[6], b[6] = after(a[6], mid[0]), after(b[6], mid[0])
    a[7], b[7] = swap(a[6]), swap(b[6])
    far = forward(a[6:8], b[6:8], w_in)
    made = [near, mid, far]
    pooled = [m[0] for m in made]

    def product(shift, w_out):
        return call(
            functools.partial(out_kernel, shift),
            shape_of(4, POOLED, width),
            [*pooled, w_out],
        )

    other = product(1, w_out)
    got = swap(other)
    own = product(0, after(w_out, other))
    joined = call(join_kernel, shape_of(4, POOLED, width), [own, after(got, own)])
    joined = joined.reshape(4, 2, PEERS, width).transpose(0, 2, 1, 3).reshape(chips, 2, width)
    emb = call(
        mean_kernel, shape_of(chips, 2, width, dtype=f32), [spread(joined), token_sum]
    )
    emb = spread(emb).transpose(1, 0, 2)
    grad_pooled, rows, prod = call(
        loss_kernel,
        [
            shape_of(2, 8 * PEERS, width, dtype=f32),
            shape_of(8, POOLED, width),
            shape_of(HELD, 8 * POOLED, hidden),
        ],
        [emb, swap(emb), w_out],
        scratch=[pltpu.VMEM((8 * PEERS, width), bf16), pltpu.VMEM((8 * PEERS, width), bf16)],
    )

    def plus(x, y):
        return call(plus_kernel, [shape_of(HALF, width), shape_of(HALF, width)], [x, y])

    pre75, p7, p5 = backward((7, 5), b, made, prod, w_in)
    s7, s5 = swap(p7), swap(p5)
    pre64, p6, p4 = backward((6, 4), b, made, after(prod, p7), w_in)
    r6a, r6b = plus(p6, s7)
    from_below, from_above = up(r6a), down(r6b)
    r4a, r4b = plus(p4, after(s5, r6a))
    low_b = up(r4b)
    pre31, p3, p1 = backward((3, 1), b, made, after(prod, r4a), w_in)
    s3, s1 = swap(p3), swap(p1)
    pre20, p2, p0 = backward((2, 0), b, made, after(prod, p3), w_in)
    r2a, r2b = plus(p2, s3)
    high_a = down(r2a)

    def add(x, y):
        return (x.astype(f32) + y.astype(f32)).astype(bf16)

    grad_w_out = grad_out(pooled, after(rows, r2a), width, hidden)
    low_a = up(add(r4a, after(from_below, grad_w_out)))
    high_b = down(add(r2b, after(from_above, grad_w_out)))
    grad_w_in = grad_in(
        a, b, [pre75, pre64, pre31, after(pre20, grad_w_out)], width, hidden
    )
    settled = call(
        settle_kernel,
        shape_of(PEERS, PAD, width),
        [after(p0, grad_w_in), s1, low_a, low_b, high_a, high_b],
    )
    grad_flat = call(
        tail_kernel,
        shape_of(row_count, width),
        [ids, slot, flat, ln_gain, grad_pooled, exchange(settled)],
        hbm=(0, 1, 2, 3, 4),
        scratch=input_scratch(row_count, width)
        + [pltpu.VMEM((2, 8, width), f32), pltpu.SemaphoreType.DMA],
    )
    return (grad_flat.reshape(tokens.shape), grad_w_in, grad_w_out)


def solution(mesh):
    placed = (
        P(("dp", "expert"), None, None, None),
        P(("dp", "expert"), None, None),
        P(("dp", "expert"), None, None),
        P(),
        P("expert", None, "dp"),
        P("expert", "dp", None),
    )
    return jax.shard_map(
        body,
        mesh=mesh,
        in_specs=placed,
        out_specs=(
            P(("dp", "expert"), None, None, None),
            P("expert", None, "dp"),
            P("expert", "dp", None),
        ),
        check_vma=False,
    )
```

```python
import functools
import math

import jax
import jax.numpy as jnp
from jax import lax
from jax.experimental import pallas as pl
from jax.experimental.pallas import tpu as pltpu
from jax.sharding import PartitionSpec as P

norm_eps = 1e-06
objective_scale = 32.0
bf16 = jnp.bfloat16
f32 = jnp.float32
i32 = jnp.int32

CAP = 6
HELD = 2
GROUP = HELD * CAP
PAD = 16
PEERS = 16
HALF = PEERS * CAP
KIND_ROWS = 8
POOLED = 2 * PEERS
PAIR_TOKENS = 64
LANES = 128
AROUND = (0, 4, 6, 2)


def nn(a, b):
    return lax.dot_general(a, b, (((1,), (0,)), ((), ())), preferred_element_type=f32)


def nt(a, b, precision=None):
    return lax.dot_general(
        a, b, (((1,), (1,)), ((), ())), precision=precision, preferred_element_type=f32
    )


def tn(a, b, precision=None):
    return lax.dot_general(
        a, b, (((0,), (0,)), ((), ())), precision=precision, preferred_element_type=f32
    )


def iota(shape, dim):
    return lax.broadcasted_iota(i32, shape, dim)


def shape_of(*dims, dtype=bf16):
    return jax.ShapeDtypeStruct(dims, dtype)


def one_hot(hit):
    return jnp.where(hit, 1.0, 0.0).astype(bf16)


FREE = pl.CostEstimate(flops=1, bytes_accessed=1, transcendentals=0)
DEAR = pl.CostEstimate(flops=10**11, bytes_accessed=10**8, transcendentals=0)


def call(kernel, out, args, smem=(), hbm=(), scratch=(), vmem=14, cost=FREE):
    def space(k):
        return pltpu.SMEM if k in smem else pltpu.HBM if k in hbm else pltpu.VMEM

    many = isinstance(out, (list, tuple))
    out_specs = [pl.BlockSpec(memory_space=pltpu.VMEM) for _ in (out if many else [out])]
    return pl.pallas_call(
        kernel,
        out_shape=out,
        in_specs=[pl.BlockSpec(memory_space=space(k)) for k in range(len(args))],
        out_specs=out_specs if many else out_specs[0],
        scratch_shapes=list(scratch),
        compiler_params=pltpu.CompilerParams(vmem_limit_bytes=vmem * 1024 * 1024),
        cost_estimate=cost,
    )(*args)


def normal_parts(x):
    centred = x - jnp.mean(x, axis=-1, keepdims=True)
    spread = jnp.mean(centred * centred, axis=-1, keepdims=True)
    scale = lax.rsqrt(spread + norm_eps)
    return centred * scale, scale


def places(ids_ref, slots_ref):
    pos = ids_ref[...] * CAP + slots_ref[...]
    return jnp.concatenate([pos[:1], pos[1:]], axis=1)


def slot_table(pos):
    tokens = pos.shape[1]
    row = iota((PEERS * PAD, tokens), 0)
    want = (row // PAD) * GROUP + row % PAD
    return one_hot((want == pos) & (row % PAD < GROUP))


def fetch(sources, refs, sems):
    copies = [pltpu.make_async_copy(a, b, sems.at[k]) for k, (a, b) in enumerate(zip(sources, refs))]
    for copy in copies:
        copy.start()
    return copies


def input_scratch(tokens, width):
    return [
        pltpu.VMEM((2, tokens // 2), i32),
        pltpu.VMEM((2, tokens // 2), i32),
        pltpu.VMEM((tokens, width), bf16),
        pltpu.VMEM((width,), f32),
        pltpu.SemaphoreType.DMA((4,)),
    ]


def dispatch_kernel(ids, slots, toks, gain, out_ref, sum_ref, ids_ref, slots_ref, tok_ref, gain_ref, sems):
    copies = fetch((ids, slots, toks, gain), (ids_ref, slots_ref, tok_ref, gain_ref), sems)
    copies[0].wait()
    copies[1].wait()
    pos = places(ids_ref, slots_ref)
    tokens, width = tok_ref.shape
    table = slot_table(pos)
    row = iota((PEERS * PAD, tokens), 0)
    goes = one_hot((row % PAD == GROUP) & (pos // GROUP == row // PAD))
    place = pos % GROUP
    column = (place // CAP) * LANES + lax.axis_index("expert") * CAP + place % CAP
    lane = iota((2 * LANES, tokens), 0)
    kind = jnp.where(iota((2 * LANES, tokens), 1) < tokens // 2, 1.0, 2.0)
    kinds = nt(goes, jnp.where(lane == column, kind, 0.0).astype(bf16))
    copies[2].wait()
    copies[3].wait()
    x = tok_ref[...].astype(f32)
    normed = normal_parts(x)[0] * gain_ref[...].reshape(1, -1)
    sent = nn(table, normed.astype(bf16))
    first = sent[:, : 2 * LANES] + kinds
    out_ref[:, :, : 2 * LANES] = first.astype(bf16).reshape(PEERS, PAD, 2 * LANES)
    out_ref[:, :, 2 * LANES :] = sent[:, 2 * LANES :].astype(bf16).reshape(
        PEERS, PAD, width - 2 * LANES
    )
    sum_ref[0:1, :] = jnp.sum(x[: tokens // 2], axis=0, keepdims=True)
    sum_ref[1:2, :] = jnp.sum(x[tokens // 2 :], axis=0, keepdims=True)


def repack_table(rows, back):
    shape = (PEERS * PAD, rows) if back else (rows, PEERS * PAD)
    r = iota(shape, 1 if back else 0)
    m = iota(shape, 0 if back else 1)
    held, rest = r // HALF, r % HALF
    from_slot = (rest // CAP) * PAD + held * CAP + rest % CAP
    hit = (r < 2 * HALF) & (m == from_slot)
    if not back:
        hit = hit | ((r == 2 * HALF) & (m % PAD == GROUP))
    return one_hot(hit)


def repack_kernel(in_ref, out_ref):
    width = in_ref.shape[2]
    table = repack_table(out_ref.shape[0], False)
    out_ref[...] = nn(table, in_ref[...].reshape(PEERS * PAD, width)).astype(bf16)


def pool_table(seconds, held, wide_ref):
    wide_ref[...] = jnp.zeros_like(wide_ref)
    q = iota((POOLED, LANES), 0)
    r = iota((POOLED, LANES), 1)
    for k, ref in enumerate(seconds):
        kinds = ref[2 * HALF : 2 * HALF + KIND_ROWS, held * LANES : (held + 1) * LANES]
        kinds = kinds.astype(f32)[:1]
        hit = (q % PEERS == r // CAP) & (kinds == (q // PEERS + 1).astype(f32)) & (r < HALF)
        wide_ref[k * POOLED : (k + 1) * POOLED, k * LANES : (k + 1) * LANES] = one_hot(hit)


def forward_kernel(*refs):
    blocks = refs[:-5]
    count = len(blocks)
    w_in, pooled_ref, slope_ref, wide_ref, act_ref = refs[-5:]
    c0 = math.sqrt(2.0 / math.pi)
    c1 = c0 * 0.044715
    hidden = w_in.shape[2]
    for held in range(HELD):
        pool_table(blocks, held, wide_ref)
        rows = [block[held * HALF : (held + 1) * HALF, :] for block in blocks]
        rows = jnp.concatenate(rows, axis=0)
        for at in range(0, hidden, 256):
            to = slice(at, min(at + 256, hidden))
            full = nn(rows, w_in[held, :, to])
            for k in range(count):
                h = full[k * HALF : (k + 1) * HALF]
                h2 = h * h
                t = jnp.tanh(h * (c0 + c1 * h2))
                half = 0.5 + 0.5 * t
                act = h * half
                slope = half + act * (1.0 - t) * (c0 + 3.0 * c1 * h2)
                slope_ref[k, held, :, to] = slope.astype(bf16)
                act_ref[k * LANES : k * LANES + HALF, to] = act.astype(bf16)
        for k in range(count):
            act_ref[k * LANES + HALF : (k + 1) * LANES, :] = jnp.zeros(
                (LANES - HALF, hidden), bf16
            )
        pooled = nn(wide_ref[...], act_ref[...]).astype(bf16)
        for k in range(count):
            pooled_ref[k, held] = pooled[k * POOLED : (k + 1) * POOLED]


def forward(arrays, w_in):
    count = len(arrays)
    hidden = w_in.shape[2]
    return call(
        forward_kernel,
        [
            shape_of(count, HELD, POOLED, hidden),
            shape_of(count, HELD, HALF, hidden),
        ],
        [*arrays, w_in],
        scratch=[
            pltpu.VMEM((count * POOLED, count * LANES), bf16),
            pltpu.VMEM((count * LANES, hidden), bf16),
        ],
    )


def pick_kernel(x2_ref, x4_ref, first_ref, second_ref):
    first_ref[...] = x2_ref[:HALF, :]
    second_ref[...] = x4_ref[HALF:, :]


def stack_kernel(first_ref, second_ref, out_ref):
    out_ref[:HALF, :] = first_ref[...]
    out_ref[HALF:, :] = second_ref[...]


PARTS = {0: (0, 0), 1: (1, 0), 2: (1, 1), 4: (1, 2), 3: (2, 0), 5: (2, 1), 6: (3, 0), 7: (3, 1)}


def part_of(parts, k):
    which, at = PARTS[k]
    return parts[which], at


def out_kernel(shift, *refs):
    parts, (w_out, out_ref) = refs[:4], refs[4:]
    total = None
    for held in range(HELD):
        rows = []
        for k in AROUND:
            ref, at = part_of(parts, k + shift)
            rows.append(ref[at, held])
        part = nn(jnp.concatenate(rows, axis=0), w_out[held])
        total = part if total is None else total + part
    out_ref[...] = total.astype(bf16).reshape(out_ref.shape)


def join_kernel(own_ref, got_ref, out_ref):
    for ahead in range(4):
        to = lax.rem(lax.axis_index("dp") // 2 + ahead, 4)
        out_ref[to] = (own_ref[ahead].astype(f32) + got_ref[ahead].astype(f32)).astype(bf16)


def mean_kernel(part_ref, sum_ref, out_ref):
    total = sum_ref[...]
    for first in range(0, part_ref.shape[0], 8):
        total = total + jnp.sum(part_ref[first : first + 8].astype(f32), axis=0)
    out_ref[...] = jnp.broadcast_to((total * (1.0 / PAIR_TOKENS))[None], out_ref.shape)


def split(x):
    high = x.astype(bf16)
    return high, (x - high.astype(f32)).astype(bf16)


def loss_kernel(own_ref, other_ref, w_out, grad_ref, rows_ref, prod_ref, gi_ref, gt_ref):
    image = jnp.concatenate([own_ref[0], other_ref[0]], axis=0)
    text = jnp.concatenate([own_ref[1], other_ref[1]], axis=0)
    pairs, width = image.shape
    scale = PAIR_TOKENS / math.sqrt(width)
    (i0, i1), (t0, t1) = split(image), split(text)
    logits = scale * (nt(i0, t0) + (nt(i0, t1) + nt(i1, t0)))

    def softmax(axis):
        top = jnp.exp(logits - jnp.max(logits, axis=axis, keepdims=True))
        return top / jnp.sum(top, axis=axis, keepdims=True)

    same = jnp.where(iota((pairs, pairs), 0) == iota((pairs, pairs), 1), 2.0, 0.0)
    grad_logits = (objective_scale * scale / PAIR_TOKENS) * (softmax(1) + softmax(0) - same)

    def thrice(g, x0, x1):
        g0, g1 = split(g)
        return nn(g0, x0) + (nn(g0, x1) + nn(g1, x0))

    grad_image = thrice(grad_logits, t0, t1)
    grad_text = thrice(grad_logits.T, i0, i1)
    grad_ref[0] = grad_image
    grad_ref[1] = grad_text
    gi_ref[...] = grad_image.astype(bf16)
    gt_ref[...] = grad_text.astype(bf16)
    for at, k in enumerate(AROUND):
        for other in range(2):
            first = other * 4 * PEERS + lax.rem(lax.axis_index("dp") // 2 + at, 4) * PEERS
            span = pl.ds(pl.multiple_of(first, PEERS), PEERS)
            rows_ref[k + other, :PEERS, :] = gi_ref[span, :]
            rows_ref[k + other, PEERS:, :] = gt_ref[span, :]
    rows = rows_ref[...].reshape(8 * POOLED, width)
    for held in range(HELD):
        prod_ref[held] = nt(rows, w_out[held]).astype(bf16)


def backward_kernel(blocks, *refs):
    count = len(blocks)
    seconds, slopes = refs[:count], refs[count : 2 * count]
    prod_ref, w_in, pre_ref = refs[2 * count : 2 * count + 3]
    outs, (wide_ref, prods_ref) = refs[2 * count + 3 : -2], refs[-2:]
    for held in range(HELD):
        pool_table(seconds, held, wide_ref)
        for k, block in enumerate(blocks):
            prods_ref[k * POOLED : (k + 1) * POOLED, :] = prod_ref[
                held, block * POOLED : (block + 1) * POOLED, :
            ]
        grad_act = tn(wide_ref[...], prods_ref[...])
        for k, block in enumerate(blocks):
            slope = slopes[k][PARTS[block][1], held].astype(f32)
            pre_ref[k, held] = (grad_act[k * LANES : k * LANES + HALF] * slope).astype(bf16)
        pre = jnp.concatenate([pre_ref[k, held] for k in range(count)], axis=0)
        part = nt(pre, w_in[held]).astype(bf16)
        for k in range(count):
            rows = part[k * HALF : (k + 1) * HALF]
            outs[k // 2][k % 2, held * HALF : (held + 1) * HALF, :] = rows


def backward(blocks, rows, made, prod, w_in):
    count = len(blocks)
    width, hidden = w_in.shape[1:]
    return call(
        functools.partial(backward_kernel, blocks),
        [shape_of(count, HELD, HALF, hidden)]
        + [shape_of(2, 2 * HALF, width)] * (count // 2),
        [
            *[rows[block] for block in blocks],
            *[made[PARTS[block][0]][1] for block in blocks],
            prod,
            w_in,
        ],
        scratch=[
            pltpu.VMEM((count * POOLED, count * LANES), bf16),
            pltpu.VMEM((count * POOLED, hidden), bf16),
        ],
    )


PAIRED = {7: (0, 0), 5: (0, 1), 6: (1, 0), 4: (1, 1), 3: (2, 0), 1: (2, 1), 2: (2, 2), 0: (2, 3)}


def grad_in_kernel(*refs):
    rows, pres = refs[:8], refs[8:11]
    out_ref, x_ref, p_ref = refs[11:]
    held = pl.program_id(0)

    def fill(which):
        for k in range(8):
            span = slice(k * HALF, (k + 1) * HALF)
            x_ref[span, :] = rows[k][which * HALF : (which + 1) * HALF, :]
            pair, at = PAIRED[k]
            p_ref[span, :] = pres[pair][at, which]

    for which in range(HELD):
        pl.when(held == which)(functools.partial(fill, which))
    out_ref[0] = tn(x_ref[...], p_ref[...])


def grad_in(rows, pres, width, hidden):
    whole = pl.BlockSpec(memory_space=pltpu.VMEM)
    return pl.pallas_call(
        grad_in_kernel,
        grid=(HELD,),
        out_shape=shape_of(HELD, width, hidden, dtype=f32),
        in_specs=[whole] * 11,
        out_specs=pl.BlockSpec((1, width, hidden), lambda i: (i, 0, 0)),
        scratch_shapes=[
            pltpu.VMEM((8 * HALF, width), bf16),
            pltpu.VMEM((8 * HALF, hidden), bf16),
        ],
        compiler_params=pltpu.CompilerParams(vmem_limit_bytes=26 * 1024 * 1024),
        cost_estimate=FREE,
    )(*rows, *pres)


def grad_out_kernel(*refs):
    parts, (rows_ref, out_ref) = refs[:4], refs[4:]
    held = pl.program_id(0)
    width = rows_ref.shape[2]
    pooled = []
    for k in range(8):
        ref, at = part_of(parts, k)
        pooled.append(ref[at, held])
    out_ref[0] = tn(jnp.concatenate(pooled, axis=0), rows_ref[...].reshape(8 * POOLED, width))


def grad_out(pooled, rows, width, hidden):
    whole = pl.BlockSpec(memory_space=pltpu.VMEM)
    return pl.pallas_call(
        grad_out_kernel,
        grid=(HELD,),
        out_shape=shape_of(HELD, hidden, width, dtype=f32),
        in_specs=[whole] * 5,
        out_specs=pl.BlockSpec((1, hidden, width), lambda i: (i, 0, 0)),
        compiler_params=pltpu.CompilerParams(vmem_limit_bytes=18 * 1024 * 1024),
        cost_estimate=FREE,
    )(*pooled, rows)


def plus_kernel(own_ref, got_ref, *outs):
    for k in range(len(outs) // 2):
        total = (own_ref[k].astype(f32) + got_ref[k].astype(f32)).astype(bf16)
        outs[2 * k][...] = total[:HALF]
        outs[2 * k + 1][...] = total[HALF:]


def add_kernel(x_ref, y_ref, out_ref):
    out_ref[...] = (x_ref[...].astype(f32) + y_ref[...].astype(f32)).astype(bf16)


def below_kernel(own_ref, got_ref, above_ref, first_ref, second_ref):
    total = own_ref[0].astype(f32) + got_ref[0].astype(f32)
    first_ref[...] = total[:HALF].astype(bf16)
    second_ref[...] = (total[HALF:] + above_ref[...].astype(f32)).astype(bf16)


def settle_kernel(own_ref, got_ref, la_ref, lb_ref, ha_ref, hb_ref, out_ref):
    width = own_ref.shape[2]
    total = own_ref[1].astype(f32) + got_ref[1].astype(f32)
    first = total[:HALF] + la_ref[...].astype(f32) + ha_ref[...].astype(f32)
    second = total[HALF:] + lb_ref[...].astype(f32) + hb_ref[...].astype(f32)
    rows = jnp.concatenate([first.astype(bf16), second.astype(bf16)], axis=0)
    out_ref[...] = nn(repack_table(2 * HALF, True), rows).astype(bf16).reshape(PEERS, PAD, width)


def tail_kernel(ids, slots, toks, gain, grads, back_ref, out_ref, ids_ref, slots_ref, tok_ref, gain_ref, sems, near_ref, near_sem):
    copies = fetch((ids, slots, toks, gain), (ids_ref, slots_ref, tok_ref, gain_ref), sems)
    at = (lax.axis_index("dp") // 2) * PEERS + lax.axis_index("expert")
    first = pl.multiple_of(at // 8 * 8, 8)
    near = pltpu.make_async_copy(grads.at[:, pl.ds(first, 8), :], near_ref, near_sem)
    near.start()
    for copy in copies:
        copy.wait()
    near.wait()
    width = tok_ref.shape[1]
    tokens = tok_ref.shape[0]
    back = back_ref[...].reshape(PEERS * PAD, width)
    grad_normed = tn(slot_table(places(ids_ref, slots_ref)), back)
    unit, scale = normal_parts(tok_ref[...].astype(f32))
    grad = grad_normed * gain_ref[...].reshape(1, -1)
    grad = scale * (
        grad
        - jnp.mean(grad, axis=-1, keepdims=True)
        - unit * jnp.mean(grad * unit, axis=-1, keepdims=True)
    )
    for half in range(2):
        span = slice(half * (tokens // 2), (half + 1) * (tokens // 2))
        rows = near_ref[half]
        own = jnp.where(iota(rows.shape, 0) == at % 8, rows, 0.0)
        own = jnp.sum(own, axis=0, keepdims=True)
        out_ref[span, :] = (own + grad[span]).astype(bf16)


def body(tokens, expert_ids, slots, ln_gain, w_in, w_out):
    width, hidden = w_in.shape[1:]
    row_count = tokens.shape[1] * tokens.shape[2]
    flat = tokens.reshape(row_count, width)
    ids, slot = expert_ids[0], slots[0]
    everyone = ("dp", "expert")
    chips = 4 * PEERS
    cores = [[d * PEERS + e for d in range(c, 8, 2) for e in range(PEERS)] for c in range(2)]

    def up(x):
        return lax.ppermute(x, "dp", [(i, (i + 2) % 8) for i in range(8)])

    def down(x):
        return lax.ppermute(x, "dp", [(i, (i + 6) % 8) for i in range(8)])

    def swap(x):
        return lax.ppermute(x, "dp", [(i, i ^ 1) for i in range(8)])

    def after(x, *tokens):
        return lax.optimization_barrier((x, *tokens))[0]

    def exchange(x):
        return lax.all_to_all(x, "expert", split_axis=0, concat_axis=0, tiled=True)

    def spread(x):
        return lax.all_to_all(
            x, everyone, split_axis=0, concat_axis=0, tiled=True, axis_index_groups=cores
        )

    sent, token_sum = call(
        dispatch_kernel,
        [shape_of(PEERS, PAD, width), shape_of(2, width, dtype=f32)],
        [ids, slot, flat, ln_gain],
        hbm=(0, 1, 2, 3),
        scratch=input_scratch(row_count, width),
        vmem=60,
    )
    rows_shape = shape_of(2 * HALF + KIND_ROWS, width)
    x0 = call(repack_kernel, rows_shape, [exchange(sent)])
    x2, x4, x1 = up(x0), down(x0), swap(x0)
    made = [forward([x0], w_in)]
    first, second = call(
        pick_kernel,
        [shape_of(HALF, width), shape_of(HALF + KIND_ROWS, width)],
        [after(x2, made[0][0]), x4],
    )
    a6, b6 = up(first), down(second)
    made.append(forward([x1, after(x2, first), x4], w_in))
    x3, x5 = swap(after(x2, made[1][0])), swap(after(x4, made[1][0]))
    x6 = call(stack_kernel, rows_shape, [after(a6, made[1][0]), b6])
    x7 = swap(x6)
    made.append(forward([after(x3, x6), x5], w_in))
    made.append(forward([x6, after(x7, made[2][0])], w_in))
    pooled = [m[0] for m in made]
    block_rows = [x0, x1, x2, x3, x4, x5, x6, x7]

    def product(shift, w_out):
        return call(
            functools.partial(out_kernel, shift),
            shape_of(4, POOLED, width),
            [*pooled, w_out],
        )

    other = product(1, w_out)
    got = swap(other)
    own = product(0, after(w_out, other))
    joined = call(join_kernel, shape_of(4, POOLED, width), [own, after(got, own)])
    joined = joined.reshape(4, 2, PEERS, width).transpose(0, 2, 1, 3).reshape(chips, 2, width)
    emb = call(
        mean_kernel, shape_of(chips, 2, width, dtype=f32), [spread(joined), token_sum]
    )
    emb = spread(emb).transpose(1, 0, 2)
    grad_pooled, rows, prod = call(
        loss_kernel,
        [
            shape_of(2, 8 * PEERS, width, dtype=f32),
            shape_of(8, POOLED, width),
            shape_of(HELD, 8 * POOLED, hidden),
        ],
        [emb, swap(emb), w_out],
        scratch=[pltpu.VMEM((8 * PEERS, width), bf16), pltpu.VMEM((8 * PEERS, width), bf16)],
    )

    pre75, p75 = backward((7, 5), block_rows, made, prod, w_in)
    s75 = swap(p75)
    pre64, p64 = backward((6, 4), block_rows, made, after(prod, p75), w_in)
    half = shape_of(HALF, width)
    r6a, r6b, r4a, r4b = call(plus_kernel, [half] * 4, [p64, s75])
    from_below, from_above = up(r6a), down(r6b)
    low_b = up(r4b)
    rest, p31, p20 = backward((3, 1, 2, 0), block_rows, made, after(prod, r6a), w_in)
    s31 = swap(p31)
    low_a = call(add_kernel, half, [after(r4a, p20), from_below], cost=DEAR)
    r2a, r2b = call(below_kernel, [half, half], [p20, after(s31, low_a), from_above])
    high_a, high_b = down(r2a), down(r2b)
    grad_w_out = grad_out(pooled, after(rows, r2a), width, hidden)
    grad_w_in = grad_in(
        block_rows, [pre75, pre64, after(rest, grad_w_out)], width, hidden
    )
    low_a = up(low_a)
    settled = call(
        settle_kernel,
        shape_of(PEERS, PAD, width),
        [after(p20, grad_w_in), s31, low_a, low_b, high_a, high_b],
    )
    grad_flat = call(
        tail_kernel,
        shape_of(row_count, width),
        [ids, slot, flat, ln_gain, grad_pooled, exchange(settled)],
        hbm=(0, 1, 2, 3, 4),
        scratch=input_scratch(row_count, width)
        + [pltpu.VMEM((2, 8, width), f32), pltpu.SemaphoreType.DMA],
    )
    return (grad_flat.reshape(tokens.shape), grad_w_in, grad_w_out)


def solution(mesh):
    placed = (
        P(("dp", "expert"), None, None, None),
        P(("dp", "expert"), None, None),
        P(("dp", "expert"), None, None),
        P(),
        P("expert", None, "dp"),
        P("expert", "dp", None),
    )
    return jax.shard_map(
        body,
        mesh=mesh,
        in_specs=placed,
        out_specs=(
            P(("dp", "expert"), None, None, None),
            P("expert", None, "dp"),
            P("expert", "dp", None),
        ),
        check_vma=False,
    )
```

```python
import functools
import math

import jax
import jax.numpy as jnp
from jax import lax
from jax.experimental import pallas as pl
from jax.experimental.pallas import tpu as pltpu
from jax.sharding import PartitionSpec as P

norm_eps = 1e-06
objective_scale = 32.0
bf16 = jnp.bfloat16
f32 = jnp.float32
i32 = jnp.int32

CAP = 6
HELD = 2
GROUP = HELD * CAP
PAD = 16
PEERS = 16
HALF = PEERS * CAP
KIND_ROWS = 8
POOLED = 2 * PEERS
PAIR_TOKENS = 64
LANES = 128
AROUND = (0, 4, 6, 2)


def nn(a, b):
    return lax.dot_general(a, b, (((1,), (0,)), ((), ())), preferred_element_type=f32)


def nt(a, b, precision=None):
    return lax.dot_general(
        a, b, (((1,), (1,)), ((), ())), precision=precision, preferred_element_type=f32
    )


def tn(a, b, precision=None):
    return lax.dot_general(
        a, b, (((0,), (0,)), ((), ())), precision=precision, preferred_element_type=f32
    )


def iota(shape, dim):
    return lax.broadcasted_iota(i32, shape, dim)


def shape_of(*dims, dtype=bf16):
    return jax.ShapeDtypeStruct(dims, dtype)


def one_hot(hit):
    return jnp.where(hit, 1.0, 0.0).astype(bf16)


FREE = pl.CostEstimate(flops=1, bytes_accessed=1, transcendentals=0)
DEAR = pl.CostEstimate(flops=10**11, bytes_accessed=10**8, transcendentals=0)


def call(kernel, out, args, smem=(), hbm=(), scratch=(), vmem=14, cost=FREE):
    def space(k):
        return pltpu.SMEM if k in smem else pltpu.HBM if k in hbm else pltpu.VMEM

    many = isinstance(out, (list, tuple))
    out_specs = [pl.BlockSpec(memory_space=pltpu.VMEM) for _ in (out if many else [out])]
    return pl.pallas_call(
        kernel,
        out_shape=out,
        in_specs=[pl.BlockSpec(memory_space=space(k)) for k in range(len(args))],
        out_specs=out_specs if many else out_specs[0],
        scratch_shapes=list(scratch),
        compiler_params=pltpu.CompilerParams(vmem_limit_bytes=vmem * 1024 * 1024),
        cost_estimate=cost,
    )(*args)


def normal_parts(x):
    centred = x - jnp.mean(x, axis=-1, keepdims=True)
    spread = jnp.mean(centred * centred, axis=-1, keepdims=True)
    scale = lax.rsqrt(spread + norm_eps)
    return centred * scale, scale


def places(ids_ref, slots_ref):
    pos = ids_ref[...] * CAP + slots_ref[...]
    return jnp.concatenate([pos[:1], pos[1:]], axis=1)


def slot_table(pos):
    tokens = pos.shape[1]
    row = iota((PEERS * PAD, tokens), 0)
    want = (row // PAD) * GROUP + row % PAD
    return one_hot((want == pos) & (row % PAD < GROUP))


def fetch(sources, refs, sems):
    copies = [pltpu.make_async_copy(a, b, sems.at[k]) for k, (a, b) in enumerate(zip(sources, refs))]
    for copy in copies:
        copy.start()
    return copies


def input_scratch(tokens, width):
    return [
        pltpu.VMEM((2, tokens // 2), i32),
        pltpu.VMEM((2, tokens // 2), i32),
        pltpu.VMEM((tokens, width), bf16),
        pltpu.VMEM((width,), f32),
        pltpu.SemaphoreType.DMA((4,)),
    ]


def dispatch_kernel(ids, slots, toks, gain, out_ref, sum_ref, ids_ref, slots_ref, tok_ref, gain_ref, sems):
    copies = fetch((ids, slots, toks, gain), (ids_ref, slots_ref, tok_ref, gain_ref), sems)
    copies[0].wait()
    copies[1].wait()
    pos = places(ids_ref, slots_ref)
    tokens, width = tok_ref.shape
    table = slot_table(pos)
    row = iota((PEERS * PAD, tokens), 0)
    goes = one_hot((row % PAD == GROUP) & (pos // GROUP == row // PAD))
    place = pos % GROUP
    column = (place // CAP) * LANES + lax.axis_index("expert") * CAP + place % CAP
    lane = iota((2 * LANES, tokens), 0)
    kind = jnp.where(iota((2 * LANES, tokens), 1) < tokens // 2, 1.0, 2.0)
    kinds = nt(goes, jnp.where(lane == column, kind, 0.0).astype(bf16))
    copies[2].wait()
    copies[3].wait()
    x = tok_ref[...].astype(f32)
    normed = normal_parts(x)[0] * gain_ref[...].reshape(1, -1)
    sent = nn(table, normed.astype(bf16))
    first = sent[:, : 2 * LANES] + kinds
    out_ref[:, :, : 2 * LANES] = first.astype(bf16).reshape(PEERS, PAD, 2 * LANES)
    out_ref[:, :, 2 * LANES :] = sent[:, 2 * LANES :].astype(bf16).reshape(
        PEERS, PAD, width - 2 * LANES
    )
    sum_ref[0:1, :] = jnp.sum(x[: tokens // 2], axis=0, keepdims=True)
    sum_ref[1:2, :] = jnp.sum(x[tokens // 2 :], axis=0, keepdims=True)


def repack_table(rows, back):
    shape = (PEERS * PAD, rows) if back else (rows, PEERS * PAD)
    r = iota(shape, 1 if back else 0)
    m = iota(shape, 0 if back else 1)
    held, rest = r // HALF, r % HALF
    from_slot = (rest // CAP) * PAD + held * CAP + rest % CAP
    hit = (r < 2 * HALF) & (m == from_slot)
    if not back:
        hit = hit | ((r == 2 * HALF) & (m % PAD == GROUP))
    return one_hot(hit)


def repack_kernel(in_ref, out_ref):
    width = in_ref.shape[2]
    table = repack_table(out_ref.shape[0], False)
    out_ref[...] = nn(table, in_ref[...].reshape(PEERS * PAD, width)).astype(bf16)


def pool_table(seconds, held, wide_ref):
    wide_ref[...] = jnp.zeros_like(wide_ref)
    q = iota((POOLED, LANES), 0)
    r = iota((POOLED, LANES), 1)
    for k, ref in enumerate(seconds):
        kinds = ref[2 * HALF : 2 * HALF + KIND_ROWS, held * LANES : (held + 1) * LANES]
        kinds = kinds.astype(f32)[:1]
        hit = (q % PEERS == r // CAP) & (kinds == (q // PEERS + 1).astype(f32)) & (r < HALF)
        wide_ref[k * POOLED : (k + 1) * POOLED, k * LANES : (k + 1) * LANES] = one_hot(hit)


def forward_kernel(*refs):
    blocks = refs[:-5]
    count = len(blocks)
    w_in, pooled_ref, slope_ref, wide_ref, act_ref = refs[-5:]
    c0 = math.sqrt(2.0 / math.pi)
    c1 = c0 * 0.044715
    hidden = w_in.shape[2]
    for held in range(HELD):
        pool_table(blocks, held, wide_ref)
        rows = [block[held * HALF : (held + 1) * HALF, :] for block in blocks]
        rows = jnp.concatenate(rows, axis=0)
        for at in range(0, hidden, 256):
            to = slice(at, min(at + 256, hidden))
            full = nn(rows, w_in[held, :, to])
            for k in range(count):
                h = full[k * HALF : (k + 1) * HALF]
                h2 = h * h
                t = jnp.tanh(h * (c0 + c1 * h2))
                half = 0.5 + 0.5 * t
                act = h * half
                slope = half + act * (1.0 - t) * (c0 + 3.0 * c1 * h2)
                slope_ref[k, held, :, to] = slope.astype(bf16)
                act_ref[k * LANES : k * LANES + HALF, to] = act.astype(bf16)
        for k in range(count):
            act_ref[k * LANES + HALF : (k + 1) * LANES, :] = jnp.zeros(
                (LANES - HALF, hidden), bf16
            )
        pooled = nn(wide_ref[...], act_ref[...]).astype(bf16)
        for k in range(count):
            pooled_ref[k, held] = pooled[k * POOLED : (k + 1) * POOLED]


def forward(arrays, w_in):
    count = len(arrays)
    hidden = w_in.shape[2]
    return call(
        forward_kernel,
        [
            shape_of(count, HELD, POOLED, hidden),
            shape_of(count, HELD, HALF, hidden),
        ],
        [*arrays, w_in],
        scratch=[
            pltpu.VMEM((count * POOLED, count * LANES), bf16),
            pltpu.VMEM((count * LANES, hidden), bf16),
        ],
    )


def pick_kernel(x2_ref, x4_ref, first_ref, second_ref):
    first_ref[...] = x2_ref[:HALF, :]
    second_ref[...] = x4_ref[HALF:, :]


def stack_kernel(first_ref, second_ref, out_ref):
    out_ref[:HALF, :] = first_ref[...]
    out_ref[HALF:, :] = second_ref[...]


PARTS = {0: (0, 0), 1: (1, 0), 2: (1, 1), 4: (1, 2), 3: (2, 0), 5: (2, 1), 6: (3, 0), 7: (3, 1)}


def part_of(parts, k):
    which, at = PARTS[k]
    return parts[which], at


def out_kernel(shift, *refs):
    parts, (w_out, out_ref) = refs[:4], refs[4:]
    total = None
    for held in range(HELD):
        rows = []
        for k in AROUND:
            ref, at = part_of(parts, k + shift)
            rows.append(ref[at, held])
        part = nn(jnp.concatenate(rows, axis=0), w_out[held])
        total = part if total is None else total + part
    out_ref[...] = total.astype(bf16).reshape(out_ref.shape)


def join_kernel(own_ref, got_ref, out_ref):
    for ahead in range(4):
        to = lax.rem(lax.axis_index("dp") // 2 + ahead, 4)
        out_ref[to] = (own_ref[ahead].astype(f32) + got_ref[ahead].astype(f32)).astype(bf16)


def mean_kernel(part_ref, sum_ref, out_ref):
    total = sum_ref[...]
    for first in range(0, part_ref.shape[0], 8):
        total = total + jnp.sum(part_ref[first : first + 8].astype(f32), axis=0)
    out_ref[...] = jnp.broadcast_to((total * (1.0 / PAIR_TOKENS))[None], out_ref.shape)


def split(x):
    high = x.astype(bf16)
    return high, (x - high.astype(f32)).astype(bf16)


def loss_kernel(own_ref, other_ref, w_out, grad_ref, rows_ref, prod_ref, gi_ref, gt_ref):
    image = jnp.concatenate([own_ref[0], other_ref[0]], axis=0)
    text = jnp.concatenate([own_ref[1], other_ref[1]], axis=0)
    pairs, width = image.shape
    scale = PAIR_TOKENS / math.sqrt(width)
    (i0, i1), (t0, t1) = split(image), split(text)
    logits = scale * (nt(i0, t0) + (nt(i0, t1) + nt(i1, t0)))

    def softmax(axis):
        top = jnp.exp(logits - jnp.max(logits, axis=axis, keepdims=True))
        return top / jnp.sum(top, axis=axis, keepdims=True)

    same = jnp.where(iota((pairs, pairs), 0) == iota((pairs, pairs), 1), 2.0, 0.0)
    grad_logits = (objective_scale * scale / PAIR_TOKENS) * (softmax(1) + softmax(0) - same)

    def thrice(g, x0, x1):
        g0, g1 = split(g)
        return nn(g0, x0) + (nn(g0, x1) + nn(g1, x0))

    grad_image = thrice(grad_logits, t0, t1)
    grad_text = thrice(grad_logits.T, i0, i1)
    grad_ref[0] = grad_image
    grad_ref[1] = grad_text
    gi_ref[...] = grad_image.astype(bf16)
    gt_ref[...] = grad_text.astype(bf16)
    for at, k in enumerate(AROUND):
        for other in range(2):
            first = other * 4 * PEERS + lax.rem(lax.axis_index("dp") // 2 + at, 4) * PEERS
            span = pl.ds(pl.multiple_of(first, PEERS), PEERS)
            rows_ref[k + other, :PEERS, :] = gi_ref[span, :]
            rows_ref[k + other, PEERS:, :] = gt_ref[span, :]
    rows = rows_ref[...].reshape(8 * POOLED, width)
    for held in range(HELD):
        prod_ref[held] = nt(rows, w_out[held]).astype(bf16)


def backward_kernel(blocks, *refs):
    count = len(blocks)
    seconds, slopes = refs[:count], refs[count : 2 * count]
    prod_ref, w_in, pre_ref = refs[2 * count : 2 * count + 3]
    outs, (wide_ref, prods_ref) = refs[2 * count + 3 : -2], refs[-2:]
    for held in range(HELD):
        pool_table(seconds, held, wide_ref)
        for k, block in enumerate(blocks):
            prods_ref[k * POOLED : (k + 1) * POOLED, :] = prod_ref[
                held, block * POOLED : (block + 1) * POOLED, :
            ]
        grad_act = tn(wide_ref[...], prods_ref[...])
        for k, block in enumerate(blocks):
            slope = slopes[k][PARTS[block][1], held].astype(f32)
            pre_ref[k, held] = (grad_act[k * LANES : k * LANES + HALF] * slope).astype(bf16)
        pre = jnp.concatenate([pre_ref[k, held] for k in range(count)], axis=0)
        part = nt(pre, w_in[held]).astype(bf16)
        for k in range(count):
            rows = part[k * HALF : (k + 1) * HALF]
            outs[k][held * HALF : (held + 1) * HALF, :] = rows


def backward(blocks, rows, made, prod, w_in):
    count = len(blocks)
    width, hidden = w_in.shape[1:]
    return call(
        functools.partial(backward_kernel, blocks),
        [shape_of(count, HELD, HALF, hidden)]
        + [shape_of(2 * HALF, width)] * count,
        [
            *[rows[block] for block in blocks],
            *[made[PARTS[block][0]][1] for block in blocks],
            prod,
            w_in,
        ],
        scratch=[
            pltpu.VMEM((count * POOLED, count * LANES), bf16),
            pltpu.VMEM((count * POOLED, hidden), bf16),
        ],
    )


PAIRED = {7: (0, 0), 6: (1, 0), 5: (1, 1), 4: (1, 2), 3: (2, 0), 1: (2, 1), 2: (2, 2), 0: (2, 3)}


def grad_in_kernel(*refs):
    rows, pres = refs[:8], refs[8:11]
    out_ref, x_ref, p_ref = refs[11:]
    held = pl.program_id(0)

    def fill(which):
        for k in range(8):
            span = slice(k * HALF, (k + 1) * HALF)
            x_ref[span, :] = rows[k][which * HALF : (which + 1) * HALF, :]
            pair, at = PAIRED[k]
            p_ref[span, :] = pres[pair][at, which]

    for which in range(HELD):
        pl.when(held == which)(functools.partial(fill, which))
    out_ref[0] = tn(x_ref[...], p_ref[...])


def grad_in(rows, pres, width, hidden):
    whole = pl.BlockSpec(memory_space=pltpu.VMEM)
    return pl.pallas_call(
        grad_in_kernel,
        grid=(HELD,),
        out_shape=shape_of(HELD, width, hidden, dtype=f32),
        in_specs=[whole] * 11,
        out_specs=pl.BlockSpec((1, width, hidden), lambda i: (i, 0, 0)),
        scratch_shapes=[
            pltpu.VMEM((8 * HALF, width), bf16),
            pltpu.VMEM((8 * HALF, hidden), bf16),
        ],
        compiler_params=pltpu.CompilerParams(vmem_limit_bytes=26 * 1024 * 1024),
        cost_estimate=FREE,
    )(*rows, *pres)


def grad_out_kernel(*refs):
    parts, (rows_ref, out_ref) = refs[:4], refs[4:]
    held = pl.program_id(0)
    width = rows_ref.shape[2]
    pooled = []
    for k in range(8):
        ref, at = part_of(parts, k)
        pooled.append(ref[at, held])
    out_ref[0] = tn(jnp.concatenate(pooled, axis=0), rows_ref[...].reshape(8 * POOLED, width))


def grad_out(pooled, rows, width, hidden):
    whole = pl.BlockSpec(memory_space=pltpu.VMEM)
    return pl.pallas_call(
        grad_out_kernel,
        grid=(HELD,),
        out_shape=shape_of(HELD, hidden, width, dtype=f32),
        in_specs=[whole] * 5,
        out_specs=pl.BlockSpec((1, hidden, width), lambda i: (i, 0, 0)),
        compiler_params=pltpu.CompilerParams(vmem_limit_bytes=18 * 1024 * 1024),
        cost_estimate=FREE,
    )(*pooled, rows)


def plus_kernel(own_ref, got_ref, first_ref, second_ref):
    total = (own_ref[...].astype(f32) + got_ref[...].astype(f32)).astype(bf16)
    first_ref[...] = total[:HALF]
    second_ref[...] = total[HALF:]


def add_kernel(x_ref, y_ref, out_ref):
    out_ref[...] = (x_ref[...].astype(f32) + y_ref[...].astype(f32)).astype(bf16)


def below_kernel(own_ref, got_ref, above_ref, first_ref, second_ref):
    total = own_ref[...].astype(f32) + got_ref[...].astype(f32)
    first_ref[...] = total[:HALF].astype(bf16)
    second_ref[...] = (total[HALF:] + above_ref[...].astype(f32)).astype(bf16)


def settle_kernel(own_ref, got_ref, la_ref, lb_ref, ha_ref, hb_ref, out_ref):
    width = own_ref.shape[1]
    total = own_ref[...].astype(f32) + got_ref[...].astype(f32)
    first = total[:HALF] + la_ref[...].astype(f32) + ha_ref[...].astype(f32)
    second = total[HALF:] + lb_ref[...].astype(f32) + hb_ref[...].astype(f32)
    rows = jnp.concatenate([first.astype(bf16), second.astype(bf16)], axis=0)
    out_ref[...] = nn(repack_table(2 * HALF, True), rows).astype(bf16).reshape(PEERS, PAD, width)


def tail_kernel(ids_ref, slots_ref, tok_ref, gain_ref, grads_ref, back_ref, out_ref):
    at = (lax.axis_index("dp") // 2) * PEERS + lax.axis_index("expert")
    near = pl.ds(pl.multiple_of(at // 8 * 8, 8), 8)
    width = tok_ref.shape[1]
    tokens = tok_ref.shape[0]
    back = back_ref[...].reshape(PEERS * PAD, width)
    grad_normed = tn(slot_table(places(ids_ref, slots_ref)), back)
    unit, scale = normal_parts(tok_ref[...].astype(f32))
    grad = grad_normed * gain_ref[...].reshape(1, -1)
    grad = scale * (
        grad
        - jnp.mean(grad, axis=-1, keepdims=True)
        - unit * jnp.mean(grad * unit, axis=-1, keepdims=True)
    )
    for half in range(2):
        span = slice(half * (tokens // 2), (half + 1) * (tokens // 2))
        rows = grads_ref[half, near, :]
        own = jnp.where(iota(rows.shape, 0) == at % 8, rows, 0.0)
        own = jnp.sum(own, axis=0, keepdims=True)
        out_ref[span, :] = (own + grad[span]).astype(bf16)


def body(tokens, expert_ids, slots, ln_gain, w_in, w_out):
    width, hidden = w_in.shape[1:]
    row_count = tokens.shape[1] * tokens.shape[2]
    flat = tokens.reshape(row_count, width)
    ids, slot = expert_ids[0], slots[0]
    everyone = ("dp", "expert")
    chips = 4 * PEERS
    cores = [[d * PEERS + e for d in range(c, 8, 2) for e in range(PEERS)] for c in range(2)]

    def up(x):
        return lax.ppermute(x, "dp", [(i, (i + 2) % 8) for i in range(8)])

    def down(x):
        return lax.ppermute(x, "dp", [(i, (i + 6) % 8) for i in range(8)])

    def swap(x):
        return lax.ppermute(x, "dp", [(i, i ^ 1) for i in range(8)])

    def after(x, *tokens):
        return lax.optimization_barrier((x, *tokens))[0]

    def exchange(x):
        return lax.all_to_all(x, "expert", split_axis=0, concat_axis=0, tiled=True)

    def spread(x):
        return lax.all_to_all(
            x, everyone, split_axis=0, concat_axis=0, tiled=True, axis_index_groups=cores
        )

    sent, token_sum = call(
        dispatch_kernel,
        [shape_of(PEERS, PAD, width), shape_of(2, width, dtype=f32)],
        [ids, slot, flat, ln_gain],
        hbm=(0, 1, 2, 3),
        scratch=input_scratch(row_count, width),
        vmem=60,
    )
    rows_shape = shape_of(2 * HALF + KIND_ROWS, width)
    x0 = call(repack_kernel, rows_shape, [exchange(sent)])
    x2, x4, x1 = up(x0), down(x0), swap(x0)
    made = [forward([x0], w_in)]
    first, second = call(
        pick_kernel,
        [shape_of(HALF, width), shape_of(HALF + KIND_ROWS, width)],
        [after(x2, made[0][0]), x4],
    )
    a6, b6 = up(first), down(second)
    made.append(forward([x1, after(x2, first), x4], w_in))
    x3, x5 = swap(after(x2, made[1][0])), swap(after(x4, made[1][0]))
    x6 = call(stack_kernel, rows_shape, [after(a6, made[1][0]), b6])
    x7 = swap(x6)
    made.append(forward([after(x3, x6), x5], w_in))
    made.append(forward([x6, after(x7, made[2][0])], w_in))
    pooled = [m[0] for m in made]
    block_rows = [x0, x1, x2, x3, x4, x5, x6, x7]

    def product(shift, w_out):
        return call(
            functools.partial(out_kernel, shift),
            shape_of(4, POOLED, width),
            [*pooled, w_out],
        )

    other = product(1, w_out)
    got = swap(other)
    own = product(0, after(w_out, other))
    joined = call(join_kernel, shape_of(4, POOLED, width), [own, after(got, own)])
    joined = joined.reshape(4, 2, PEERS, width).transpose(0, 2, 1, 3).reshape(chips, 2, width)
    emb = call(
        mean_kernel, shape_of(chips, 2, width, dtype=f32), [spread(joined), token_sum]
    )
    emb = spread(emb).transpose(1, 0, 2)
    grad_pooled, rows, prod = call(
        loss_kernel,
        [
            shape_of(2, 8 * PEERS, width, dtype=f32),
            shape_of(8, POOLED, width),
            shape_of(HELD, 8 * POOLED, hidden),
        ],
        [emb, swap(emb), w_out],
        scratch=[pltpu.VMEM((8 * PEERS, width), bf16), pltpu.VMEM((8 * PEERS, width), bf16)],
    )

    def plus(x, y):
        return call(plus_kernel, [shape_of(HALF, width)] * 2, [x, y])

    half = shape_of(HALF, width)
    pre7, p7 = backward((7,), block_rows, made, prod, w_in)
    s7 = swap(p7)
    pre654, p6, p5, p4 = backward((6, 5, 4), block_rows, made, after(prod, p7), w_in)
    s5 = swap(p5)
    r6a, r6b = plus(p6, s7)
    from_below, from_above = up(r6a), down(r6b)
    rest, p3, p1, p2, p0 = backward((3, 1, 2, 0), block_rows, made, after(prod, r6a), w_in)
    r4a, r4b = plus(p4, after(s5, p2))
    low_b = up(r4b)
    s3, s1 = swap(p3), swap(p1)
    low_a = call(add_kernel, half, [after(r4a, p0), from_below], cost=DEAR)
    r2a, r2b = call(below_kernel, [half, half], [p2, after(s3, low_a), from_above])
    high_a, high_b = down(r2a), down(r2b)
    grad_w_out = grad_out(pooled, after(rows, r2a), width, hidden)
    grad_w_in = grad_in(
        block_rows, [pre7, pre654, after(rest, grad_w_out)], width, hidden
    )
    low_a = up(low_a)
    settled = call(
        settle_kernel,
        shape_of(PEERS, PAD, width),
        [after(p0, grad_w_in), s1, low_a, low_b, high_a, high_b],
    )
    grad_flat = call(
        tail_kernel,
        shape_of(row_count, width),
        [ids, slot, flat, ln_gain, grad_pooled, exchange(settled)],
    )
    return (grad_flat.reshape(tokens.shape), grad_w_in, grad_w_out)


def solution(mesh):
    placed = (
        P(("dp", "expert"), None, None, None),
        P(("dp", "expert"), None, None),
        P(("dp", "expert"), None, None),
        P(),
        P("expert", None, "dp"),
        P("expert", "dp", None),
    )
    return jax.shard_map(
        body,
        mesh=mesh,
        in_specs=placed,
        out_specs=(
            P(("dp", "expert"), None, None, None),
            P("expert", None, "dp"),
            P("expert", "dp", None),
        ),
        check_vma=False,
    )
```

```python
import functools
import math

import jax
import jax.numpy as jnp
from jax import lax
from jax.experimental import pallas as pl
from jax.experimental.pallas import tpu as pltpu
from jax.sharding import PartitionSpec as P

norm_eps = 1e-06
objective_scale = 32.0
bf16 = jnp.bfloat16
f32 = jnp.float32
i32 = jnp.int32

CAP = 6
HELD = 2
GROUP = HELD * CAP
PAD = 16
PEERS = 16
HALF = PEERS * CAP
KIND_ROWS = 16
POOLED = 2 * PEERS
PAIR_TOKENS = 64
LANES = 128
AROUND = (0, 4, 6, 2)


def nn(a, b):
    return lax.dot_general(a, b, (((1,), (0,)), ((), ())), preferred_element_type=f32)


def nt(a, b, precision=None):
    return lax.dot_general(
        a, b, (((1,), (1,)), ((), ())), precision=precision, preferred_element_type=f32
    )


def tn(a, b, precision=None):
    return lax.dot_general(
        a, b, (((0,), (0,)), ((), ())), precision=precision, preferred_element_type=f32
    )


def iota(shape, dim):
    return lax.broadcasted_iota(i32, shape, dim)


def shape_of(*dims, dtype=bf16):
    return jax.ShapeDtypeStruct(dims, dtype)


def one_hot(hit):
    return jnp.where(hit, 1.0, 0.0).astype(bf16)


FREE = pl.CostEstimate(flops=1, bytes_accessed=1, transcendentals=0)
DEAR = pl.CostEstimate(flops=10**11, bytes_accessed=10**8, transcendentals=0)


def call(kernel, out, args, smem=(), hbm=(), scratch=(), vmem=14, cost=FREE):
    def space(k):
        return pltpu.SMEM if k in smem else pltpu.HBM if k in hbm else pltpu.VMEM

    many = isinstance(out, (list, tuple))
    out_specs = [pl.BlockSpec(memory_space=pltpu.VMEM) for _ in (out if many else [out])]
    return pl.pallas_call(
        kernel,
        out_shape=out,
        in_specs=[pl.BlockSpec(memory_space=space(k)) for k in range(len(args))],
        out_specs=out_specs if many else out_specs[0],
        scratch_shapes=list(scratch),
        compiler_params=pltpu.CompilerParams(vmem_limit_bytes=vmem * 1024 * 1024),
        cost_estimate=cost,
    )(*args)


def normal_parts(x):
    centred = x - jnp.mean(x, axis=-1, keepdims=True)
    spread = jnp.mean(centred * centred, axis=-1, keepdims=True)
    scale = lax.rsqrt(spread + norm_eps)
    return centred * scale, scale


def places(ids_ref, slots_ref):
    pos = ids_ref[...] * CAP + slots_ref[...]
    return jnp.concatenate([pos[:1], pos[1:]], axis=1)


def slot_table(pos):
    tokens = pos.shape[1]
    row = iota((PEERS * PAD, tokens), 0)
    want = (row // PAD) * GROUP + row % PAD
    return one_hot((want == pos) & (row % PAD < GROUP))


def fetch(sources, refs, sems):
    copies = [pltpu.make_async_copy(a, b, sems.at[k]) for k, (a, b) in enumerate(zip(sources, refs))]
    for copy in copies:
        copy.start()
    return copies


def input_scratch(tokens, width):
    return [
        pltpu.VMEM((2, tokens // 2), i32),
        pltpu.VMEM((2, tokens // 2), i32),
        pltpu.VMEM((tokens, width), bf16),
        pltpu.VMEM((width,), f32),
        pltpu.SemaphoreType.DMA((4,)),
    ]


def dispatch_kernel(ids, slots, toks, gain, out_ref, sum_ref, ids_ref, slots_ref, tok_ref, gain_ref, sems):
    copies = fetch((ids, slots, toks, gain), (ids_ref, slots_ref, tok_ref, gain_ref), sems)
    copies[0].wait()
    copies[1].wait()
    pos = places(ids_ref, slots_ref)
    tokens, width = tok_ref.shape
    table = slot_table(pos)
    row = iota((PEERS * PAD, tokens), 0)
    goes = one_hot((row % PAD == GROUP) & (pos // GROUP == row // PAD))
    place = pos % GROUP
    column = (place // CAP) * LANES + lax.axis_index("expert") * CAP + place % CAP
    lane = iota((2 * LANES, tokens), 0)
    kind = jnp.where(iota((2 * LANES, tokens), 1) < tokens // 2, 1.0, 2.0)
    kinds = nt(goes, jnp.where(lane == column, kind, 0.0).astype(bf16))
    copies[2].wait()
    copies[3].wait()
    x = tok_ref[...].astype(f32)
    normed = normal_parts(x)[0] * gain_ref[...].reshape(1, -1)
    sent = nn(table, normed.astype(bf16))
    first = sent[:, : 2 * LANES] + kinds
    out_ref[:, :, : 2 * LANES] = first.astype(bf16).reshape(PEERS, PAD, 2 * LANES)
    out_ref[:, :, 2 * LANES :] = sent[:, 2 * LANES :].astype(bf16).reshape(
        PEERS, PAD, width - 2 * LANES
    )
    sum_ref[0:1, :] = jnp.sum(x[: tokens // 2], axis=0, keepdims=True)
    sum_ref[1:2, :] = jnp.sum(x[tokens // 2 :], axis=0, keepdims=True)


def repack_table(rows, back):
    shape = (PEERS * PAD, rows) if back else (rows, PEERS * PAD)
    r = iota(shape, 1 if back else 0)
    m = iota(shape, 0 if back else 1)
    held, rest = r // HALF, r % HALF
    from_slot = (rest // CAP) * PAD + held * CAP + rest % CAP
    hit = (r < 2 * HALF) & (m == from_slot)
    if not back:
        hit = hit | ((r == 2 * HALF) & (m % PAD == GROUP))
    return one_hot(hit)


def repack_kernel(in_ref, out_ref):
    width = in_ref.shape[2]
    table = repack_table(out_ref.shape[0], False)
    out_ref[...] = nn(table, in_ref[...].reshape(PEERS * PAD, width)).astype(bf16)


def pool_table(seconds, held, wide_ref):
    wide_ref[...] = jnp.zeros_like(wide_ref)
    q = iota((POOLED, LANES), 0)
    r = iota((POOLED, LANES), 1)
    for k, ref in enumerate(seconds):
        kinds = ref[2 * HALF : 2 * HALF + KIND_ROWS, held * LANES : (held + 1) * LANES]
        kinds = kinds.astype(f32)[:1]
        hit = (q % PEERS == r // CAP) & (kinds == (q // PEERS + 1).astype(f32)) & (r < HALF)
        wide_ref[k * POOLED : (k + 1) * POOLED, k * LANES : (k + 1) * LANES] = one_hot(hit)


def forward_kernel(*refs):
    blocks = refs[:-5]
    count = len(blocks)
    w_in, pooled_ref, slope_ref, wide_ref, act_ref = refs[-5:]
    c0 = math.sqrt(2.0 / math.pi)
    c1 = c0 * 0.044715
    hidden = w_in.shape[2]
    for held in range(HELD):
        pool_table(blocks, held, wide_ref)
        rows = [block[held * HALF : (held + 1) * HALF, :] for block in blocks]
        rows = jnp.concatenate(rows, axis=0)
        for at in range(0, hidden, 640):
            to = slice(at, min(at + 640, hidden))
            full = nn(rows, w_in[held, :, to])
            for k in range(count):
                h = full[k * HALF : (k + 1) * HALF]
                h2 = h * h
                t = jnp.tanh(h * (c0 + c1 * h2))
                half = 0.5 + 0.5 * t
                act = h * half
                slope = half + act * (1.0 - t) * (c0 + 3.0 * c1 * h2)
                slope_ref[k, held, :, to] = slope.astype(bf16)
                act_ref[k * LANES : k * LANES + HALF, to] = act.astype(bf16)
        for k in range(count):
            act_ref[k * LANES + HALF : (k + 1) * LANES, :] = jnp.zeros(
                (LANES - HALF, hidden), bf16
            )
        pooled = nn(wide_ref[...], act_ref[...]).astype(bf16)
        for k in range(count):
            pooled_ref[k, held] = pooled[k * POOLED : (k + 1) * POOLED]


def forward(arrays, w_in):
    count = len(arrays)
    hidden = w_in.shape[2]
    return call(
        forward_kernel,
        [
            shape_of(count, HELD, POOLED, hidden),
            shape_of(count, HELD, HALF, hidden),
        ],
        [*arrays, w_in],
        scratch=[
            pltpu.VMEM((count * POOLED, count * LANES), bf16),
            pltpu.VMEM((count * LANES, hidden), bf16),
        ],
    )


def pick_kernel(x2_ref, x4_ref, first_ref, second_ref):
    first_ref[...] = x2_ref[:HALF, :]
    second_ref[...] = x4_ref[HALF:, :]


def stack_kernel(first_ref, second_ref, out_ref):
    out_ref[:HALF, :] = first_ref[...]
    out_ref[HALF:, :] = second_ref[...]


PARTS = {0: (0, 0), 1: (1, 0), 2: (1, 1), 4: (1, 2), 3: (2, 0), 5: (2, 1), 6: (3, 0), 7: (3, 1)}


def part_of(parts, k):
    which, at = PARTS[k]
    return parts[which], at


def out_kernel(shift, *refs):
    parts, (w_out, out_ref) = refs[:4], refs[4:]
    total = None
    for held in range(HELD):
        rows = []
        for k in AROUND:
            ref, at = part_of(parts, k + shift)
            rows.append(ref[at, held])
        part = nn(jnp.concatenate(rows, axis=0), w_out[held])
        total = part if total is None else total + part
    out_ref[...] = total.astype(bf16).reshape(out_ref.shape)


def join_kernel(own_ref, got_ref, out_ref):
    for ahead in range(4):
        to = lax.rem(lax.axis_index("dp") // 2 + ahead, 4)
        out_ref[to] = (own_ref[ahead].astype(f32) + got_ref[ahead].astype(f32)).astype(bf16)


def mean_kernel(part_ref, sum_ref, out_ref):
    total = sum_ref[...]
    for first in range(0, part_ref.shape[0], 8):
        total = total + jnp.sum(part_ref[first : first + 8].astype(f32), axis=0)
    out_ref[...] = jnp.broadcast_to((total * (1.0 / PAIR_TOKENS))[None], out_ref.shape)


def split(x):
    high = x.astype(bf16)
    return high, (x - high.astype(f32)).astype(bf16)


def loss_kernel(own_ref, other_ref, w_out, grad_ref, rows_ref, prod_ref, gi_ref, gt_ref):
    image = jnp.concatenate([own_ref[0], other_ref[0]], axis=0)
    text = jnp.concatenate([own_ref[1], other_ref[1]], axis=0)
    pairs, width = image.shape
    scale = PAIR_TOKENS / math.sqrt(width)
    (i0, i1), (t0, t1) = split(image), split(text)
    logits = scale * (nt(i0, t0) + (nt(i0, t1) + nt(i1, t0)))

    def softmax(axis):
        top = jnp.exp(logits - jnp.max(logits, axis=axis, keepdims=True))
        return top / jnp.sum(top, axis=axis, keepdims=True)

    same = jnp.where(iota((pairs, pairs), 0) == iota((pairs, pairs), 1), 2.0, 0.0)
    grad_logits = (objective_scale * scale / PAIR_TOKENS) * (softmax(1) + softmax(0) - same)

    def thrice(g, x0, x1):
        g0, g1 = split(g)
        return nn(g0, x0) + (nn(g0, x1) + nn(g1, x0))

    grad_image = thrice(grad_logits, t0, t1)
    grad_text = thrice(grad_logits.T, i0, i1)
    grad_ref[0] = grad_image
    grad_ref[1] = grad_text
    gi_ref[...] = grad_image.astype(bf16)
    gt_ref[...] = grad_text.astype(bf16)
    for at, k in enumerate(AROUND):
        for other in range(2):
            first = other * 4 * PEERS + lax.rem(lax.axis_index("dp") // 2 + at, 4) * PEERS
            span = pl.ds(pl.multiple_of(first, PEERS), PEERS)
            rows_ref[k + other, :PEERS, :] = gi_ref[span, :]
            rows_ref[k + other, PEERS:, :] = gt_ref[span, :]
    rows = rows_ref[...].reshape(8 * POOLED, width)
    for held in range(HELD):
        prod_ref[held] = nt(rows, w_out[held]).astype(bf16)


def backward_kernel(blocks, *refs):
    count = len(blocks)
    seconds, slopes = refs[:count], refs[count : 2 * count]
    prod_ref, w_in, pre_ref = refs[2 * count : 2 * count + 3]
    outs, (wide_ref, prods_ref) = refs[2 * count + 3 : -2], refs[-2:]
    for held in range(HELD):
        pool_table(seconds, held, wide_ref)
        for k, block in enumerate(blocks):
            prods_ref[k * POOLED : (k + 1) * POOLED, :] = prod_ref[
                held, block * POOLED : (block + 1) * POOLED, :
            ]
        grad_act = tn(wide_ref[...], prods_ref[...])
        for k, block in enumerate(blocks):
            slope = slopes[k][PARTS[block][1], held].astype(f32)
            pre_ref[k, held] = (grad_act[k * LANES : k * LANES + HALF] * slope).astype(bf16)
        pre = jnp.concatenate([pre_ref[k, held] for k in range(count)], axis=0)
        part = nt(pre, w_in[held]).astype(bf16)
        for k in range(count):
            rows = part[k * HALF : (k + 1) * HALF]
            outs[k][held * HALF : (held + 1) * HALF, :] = rows


def backward(blocks, rows, made, prod, w_in):
    count = len(blocks)
    width, hidden = w_in.shape[1:]
    return call(
        functools.partial(backward_kernel, blocks),
        [shape_of(count, HELD, HALF, hidden)]
        + [shape_of(2 * HALF, width)] * count,
        [
            *[rows[block] for block in blocks],
            *[made[PARTS[block][0]][1] for block in blocks],
            prod,
            w_in,
        ],
        scratch=[
            pltpu.VMEM((count * POOLED, count * LANES), bf16),
            pltpu.VMEM((count * POOLED, hidden), bf16),
        ],
    )


PAIRED = {7: (0, 0), 6: (1, 0), 5: (1, 1), 4: (1, 2), 3: (2, 0), 1: (2, 1), 2: (2, 2), 0: (2, 3)}


def grad_in_kernel(*refs):
    rows, pres = refs[:8], refs[8:11]
    out_ref, x_ref, p_ref = refs[11:]
    held = pl.program_id(0)

    def fill(which):
        for k in range(8):
            span = slice(k * HALF, (k + 1) * HALF)
            x_ref[span, :] = rows[k][which * HALF : (which + 1) * HALF, :]
            pair, at = PAIRED[k]
            p_ref[span, :] = pres[pair][at, which]

    for which in range(HELD):
        pl.when(held == which)(functools.partial(fill, which))
    out_ref[0] = tn(x_ref[...], p_ref[...])


def grad_in(rows, pres, width, hidden):
    whole = pl.BlockSpec(memory_space=pltpu.VMEM)
    return pl.pallas_call(
        grad_in_kernel,
        grid=(HELD,),
        out_shape=shape_of(HELD, width, hidden, dtype=f32),
        in_specs=[whole] * 11,
        out_specs=pl.BlockSpec((1, width, hidden), lambda i: (i, 0, 0)),
        scratch_shapes=[
            pltpu.VMEM((8 * HALF, width), bf16),
            pltpu.VMEM((8 * HALF, hidden), bf16),
        ],
        compiler_params=pltpu.CompilerParams(vmem_limit_bytes=26 * 1024 * 1024),
        cost_estimate=FREE,
    )(*rows, *pres)


def grad_out_kernel(*refs):
    parts, (rows_ref, out_ref) = refs[:4], refs[4:]
    held = pl.program_id(0)
    width = rows_ref.shape[2]
    pooled = []
    for k in range(8):
        ref, at = part_of(parts, k)
        pooled.append(ref[at, held])
    out_ref[0] = tn(jnp.concatenate(pooled, axis=0), rows_ref[...].reshape(8 * POOLED, width))


def grad_out(pooled, rows, width, hidden):
    whole = pl.BlockSpec(memory_space=pltpu.VMEM)
    return pl.pallas_call(
        grad_out_kernel,
        grid=(HELD,),
        out_shape=shape_of(HELD, hidden, width, dtype=f32),
        in_specs=[whole] * 5,
        out_specs=pl.BlockSpec((1, hidden, width), lambda i: (i, 0, 0)),
        compiler_params=pltpu.CompilerParams(vmem_limit_bytes=18 * 1024 * 1024),
        cost_estimate=FREE,
    )(*pooled, rows)


def plus_kernel(own_ref, got_ref, first_ref, second_ref):
    total = (own_ref[...].astype(f32) + got_ref[...].astype(f32)).astype(bf16)
    first_ref[...] = total[:HALF]
    second_ref[...] = total[HALF:]


def add_kernel(x_ref, y_ref, out_ref):
    out_ref[...] = (x_ref[...].astype(f32) + y_ref[...].astype(f32)).astype(bf16)


def below_kernel(own_ref, got_ref, above_ref, first_ref, second_ref):
    total = own_ref[...].astype(f32) + got_ref[...].astype(f32)
    first_ref[...] = total[:HALF].astype(bf16)
    second_ref[...] = (total[HALF:] + above_ref[...].astype(f32)).astype(bf16)


def settle_kernel(own_ref, got_ref, la_ref, lb_ref, ha_ref, hb_ref, out_ref):
    width = own_ref.shape[1]
    total = own_ref[...].astype(f32) + got_ref[...].astype(f32)
    first = total[:HALF] + la_ref[...].astype(f32) + ha_ref[...].astype(f32)
    second = total[HALF:] + lb_ref[...].astype(f32) + hb_ref[...].astype(f32)
    rows = jnp.concatenate([first.astype(bf16), second.astype(bf16)], axis=0)
    out_ref[...] = nn(repack_table(2 * HALF, True), rows).astype(bf16).reshape(PEERS, PAD, width)


def tail_kernel(ids_ref, slots_ref, tok_ref, gain_ref, grads_ref, back_ref, out_ref):
    at = (lax.axis_index("dp") // 2) * PEERS + lax.axis_index("expert")
    near = pl.ds(pl.multiple_of(at // 8 * 8, 8), 8)
    width = tok_ref.shape[1]
    tokens = tok_ref.shape[0]
    back = back_ref[...].reshape(PEERS * PAD, width)
    grad_normed = tn(slot_table(places(ids_ref, slots_ref)), back)
    unit, scale = normal_parts(tok_ref[...].astype(f32))
    grad = grad_normed * gain_ref[...].reshape(1, -1)
    grad = scale * (
        grad
        - jnp.mean(grad, axis=-1, keepdims=True)
        - unit * jnp.mean(grad * unit, axis=-1, keepdims=True)
    )
    for half in range(2):
        span = slice(half * (tokens // 2), (half + 1) * (tokens // 2))
        rows = grads_ref[half, near, :]
        own = jnp.where(iota(rows.shape, 0) == at % 8, rows, 0.0)
        own = jnp.sum(own, axis=0, keepdims=True)
        out_ref[span, :] = (own + grad[span]).astype(bf16)


def body(tokens, expert_ids, slots, ln_gain, w_in, w_out):
    width, hidden = w_in.shape[1:]
    row_count = tokens.shape[1] * tokens.shape[2]
    flat = tokens.reshape(row_count, width)
    ids, slot = expert_ids[0], slots[0]
    everyone = ("dp", "expert")
    chips = 4 * PEERS
    cores = [[d * PEERS + e for d in range(c, 8, 2) for e in range(PEERS)] for c in range(2)]

    def up(x):
        return lax.ppermute(x, "dp", [(i, (i + 2) % 8) for i in range(8)])

    def down(x):
        return lax.ppermute(x, "dp", [(i, (i + 6) % 8) for i in range(8)])

    def swap(x):
        return lax.ppermute(x, "dp", [(i, i ^ 1) for i in range(8)])

    def after(x, *tokens):
        return lax.optimization_barrier((x, *tokens))[0]

    def exchange(x):
        return lax.all_to_all(x, "expert", split_axis=0, concat_axis=0, tiled=True)

    def spread(x):
        return lax.all_to_all(
            x, everyone, split_axis=0, concat_axis=0, tiled=True, axis_index_groups=cores
        )

    sent, token_sum = call(
        dispatch_kernel,
        [shape_of(PEERS, PAD, width), shape_of(2, width, dtype=f32)],
        [ids, slot, flat, ln_gain],
        hbm=(0, 1, 2, 3),
        scratch=input_scratch(row_count, width),
        vmem=60,
    )
    rows_shape = shape_of(2 * HALF + KIND_ROWS, width)
    x0 = call(repack_kernel, rows_shape, [exchange(sent)])
    x2, x4, x1 = up(x0), down(x0), swap(x0)
    made = [forward([x0], w_in)]
    first, second = call(
        pick_kernel,
        [shape_of(HALF, width), shape_of(HALF + KIND_ROWS, width)],
        [after(x2, made[0][0]), x4],
    )
    a6, b6 = up(first), down(second)
    made.append(forward([x1, after(x2, first), x4], w_in))
    x3, x5 = swap(after(x2, made[1][0])), swap(after(x4, made[1][0]))
    x6 = call(stack_kernel, rows_shape, [after(a6, made[1][0]), b6])
    x7 = swap(x6)
    made.append(forward([after(x3, x6), x5], w_in))
    made.append(forward([x6, after(x7, made[2][0])], w_in))
    pooled = [m[0] for m in made]
    block_rows = [x0, x1, x2, x3, x4, x5, x6, x7]

    def product(shift, w_out):
        return call(
            functools.partial(out_kernel, shift),
            shape_of(4, POOLED, width),
            [*pooled, w_out],
        )

    other = product(1, w_out)
    got = swap(other)
    own = product(0, after(w_out, other))
    joined = call(join_kernel, shape_of(4, POOLED, width), [own, after(got, own)])
    joined = joined.reshape(4, 2, PEERS, width).transpose(0, 2, 1, 3).reshape(chips, 2, width)
    emb = call(
        mean_kernel, shape_of(chips, 2, width, dtype=f32), [spread(joined), token_sum]
    )
    emb = spread(emb).transpose(1, 0, 2)
    grad_pooled, rows, prod = call(
        loss_kernel,
        [
            shape_of(2, 8 * PEERS, width, dtype=f32),
            shape_of(8, POOLED, width),
            shape_of(HELD, 8 * POOLED, hidden),
        ],
        [emb, swap(emb), w_out],
        scratch=[pltpu.VMEM((8 * PEERS, width), bf16), pltpu.VMEM((8 * PEERS, width), bf16)],
    )

    def plus(x, y):
        return call(plus_kernel, [shape_of(HALF, width)] * 2, [x, y])

    half = shape_of(HALF, width)
    pre7, p7 = backward((7,), block_rows, made, prod, w_in)
    s7 = swap(p7)
    pre654, p6, p5, p4 = backward((6, 5, 4), block_rows, made, after(prod, p7), w_in)
    s5 = swap(p5)
    r6a, r6b = plus(p6, s7)
    from_below, from_above = up(r6a), down(r6b)
    rest, p3, p1, p2, p0 = backward((3, 1, 2, 0), block_rows, made, after(prod, r6a), w_in)
    r4a, r4b = plus(p4, after(s5, p2))
    low_b = up(r4b)
    s3, s1 = swap(p3), swap(p1)
    low_a = call(add_kernel, half, [after(r4a, p0), from_below], cost=DEAR)
    r2a, r2b = call(below_kernel, [half, half], [p2, after(s3, low_a), from_above])
    high_a, high_b = down(r2a), down(r2b)
    grad_w_out = grad_out(pooled, after(rows, r2a), width, hidden)
    grad_w_in = grad_in(
        block_rows, [pre7, pre654, after(rest, grad_w_out)], width, hidden
    )
    low_a = up(low_a)
    settled = call(
        settle_kernel,
        shape_of(PEERS, PAD, width),
        [after(p0, grad_w_in), s1, low_a, low_b, high_a, high_b],
    )
    grad_flat = call(
        tail_kernel,
        shape_of(row_count, width),
        [ids, slot, flat, ln_gain, grad_pooled, exchange(settled)],
    )
    return (grad_flat.reshape(tokens.shape), grad_w_in, grad_w_out)


def solution(mesh):
    placed = (
        P(("dp", "expert"), None, None, None),
        P(("dp", "expert"), None, None),
        P(("dp", "expert"), None, None),
        P(),
        P("expert", None, "dp"),
        P("expert", "dp", None),
    )
    return jax.shard_map(
        body,
        mesh=mesh,
        in_specs=placed,
        out_specs=(
            P(("dp", "expert"), None, None, None),
            P("expert", None, "dp"),
            P("expert", "dp", None),
        ),
        check_vma=False,
    )
```

```python
import functools
import math

import jax
import jax.numpy as jnp
from jax import lax
from jax.experimental import pallas as pl
from jax.experimental.pallas import tpu as pltpu
from jax.sharding import PartitionSpec as P

norm_eps = 1e-06
objective_scale = 32.0
bf16 = jnp.bfloat16
f32 = jnp.float32
i32 = jnp.int32

CAP = 6
HELD = 2
GROUP = HELD * CAP
PAD = 16
PEERS = 16
HALF = PEERS * CAP
KIND_ROWS = 16
POOLED = 2 * PEERS
PAIR_TOKENS = 64
LANES = 128
AROUND = (0, 4, 6, 2)


def nn(a, b):
    return lax.dot_general(a, b, (((1,), (0,)), ((), ())), preferred_element_type=f32)


def nt(a, b, precision=None):
    return lax.dot_general(
        a, b, (((1,), (1,)), ((), ())), precision=precision, preferred_element_type=f32
    )


def tn(a, b, precision=None):
    return lax.dot_general(
        a, b, (((0,), (0,)), ((), ())), precision=precision, preferred_element_type=f32
    )


def iota(shape, dim):
    return lax.broadcasted_iota(i32, shape, dim)


def shape_of(*dims, dtype=bf16):
    return jax.ShapeDtypeStruct(dims, dtype)


def one_hot(hit):
    return jnp.where(hit, 1.0, 0.0).astype(bf16)


FREE = pl.CostEstimate(flops=1, bytes_accessed=1, transcendentals=0)
DEAR = pl.CostEstimate(flops=10**11, bytes_accessed=10**8, transcendentals=0)


def call(kernel, out, args, smem=(), hbm=(), scratch=(), vmem=14, cost=FREE):
    def space(k):
        return pltpu.SMEM if k in smem else pltpu.HBM if k in hbm else pltpu.VMEM

    many = isinstance(out, (list, tuple))
    out_specs = [pl.BlockSpec(memory_space=pltpu.VMEM) for _ in (out if many else [out])]
    return pl.pallas_call(
        kernel,
        out_shape=out,
        in_specs=[pl.BlockSpec(memory_space=space(k)) for k in range(len(args))],
        out_specs=out_specs if many else out_specs[0],
        scratch_shapes=list(scratch),
        compiler_params=pltpu.CompilerParams(vmem_limit_bytes=vmem * 1024 * 1024),
        cost_estimate=cost,
    )(*args)


def normal_parts(x):
    centred = x - jnp.mean(x, axis=-1, keepdims=True)
    spread = jnp.mean(centred * centred, axis=-1, keepdims=True)
    scale = lax.rsqrt(spread + norm_eps)
    return centred * scale, scale


def places(ids_ref, slots_ref):
    pos = ids_ref[...] * CAP + slots_ref[...]
    return jnp.concatenate([pos[:1], pos[1:]], axis=1)


def slot_table(pos):
    tokens = pos.shape[1]
    row = iota((PEERS * PAD, tokens), 0)
    want = (row // PAD) * GROUP + row % PAD
    return one_hot((want == pos) & (row % PAD < GROUP))


def dispatch_kernel(ids_ref, slots_ref, tok_ref, gain_ref, out_ref, sum_ref):
    pos = places(ids_ref, slots_ref)
    tokens, width = tok_ref.shape
    table = slot_table(pos)
    row = iota((PEERS * PAD, tokens), 0)
    goes = one_hot((row % PAD == GROUP) & (pos // GROUP == row // PAD))
    place = pos % GROUP
    column = (place // CAP) * LANES + lax.axis_index("expert") * CAP + place % CAP
    lane = iota((2 * LANES, tokens), 0)
    kind = jnp.where(iota((2 * LANES, tokens), 1) < tokens // 2, 1.0, 2.0)
    kinds = nt(goes, jnp.where(lane == column, kind, 0.0).astype(bf16))
    x = tok_ref[...].astype(f32)
    normed = normal_parts(x)[0] * gain_ref[...].reshape(1, -1)
    sent = nn(table, normed.astype(bf16))
    first = sent[:, : 2 * LANES] + kinds
    out_ref[:, :, : 2 * LANES] = first.astype(bf16).reshape(PEERS, PAD, 2 * LANES)
    out_ref[:, :, 2 * LANES :] = sent[:, 2 * LANES :].astype(bf16).reshape(
        PEERS, PAD, width - 2 * LANES
    )
    sum_ref[0:1, :] = jnp.sum(x[: tokens // 2], axis=0, keepdims=True)
    sum_ref[1:2, :] = jnp.sum(x[tokens // 2 :], axis=0, keepdims=True)


def repack_table(rows, back):
    shape = (PEERS * PAD, rows) if back else (rows, PEERS * PAD)
    r = iota(shape, 1 if back else 0)
    m = iota(shape, 0 if back else 1)
    held, rest = r // HALF, r % HALF
    from_slot = (rest // CAP) * PAD + held * CAP + rest % CAP
    hit = (r < 2 * HALF) & (m == from_slot)
    if not back:
        hit = hit | ((r == 2 * HALF) & (m % PAD == GROUP))
    return one_hot(hit)


def repack_kernel(in_ref, out_ref):
    width = in_ref.shape[2]
    table = repack_table(out_ref.shape[0], False)
    out_ref[...] = nn(table, in_ref[...].reshape(PEERS * PAD, width)).astype(bf16)


def pool_table(seconds, held, wide_ref):
    wide_ref[...] = jnp.zeros_like(wide_ref)
    q = iota((POOLED, LANES), 0)
    r = iota((POOLED, LANES), 1)
    for k, ref in enumerate(seconds):
        kinds = ref[2 * HALF : 2 * HALF + KIND_ROWS, held * LANES : (held + 1) * LANES]
        kinds = kinds.astype(f32)[:1]
        hit = (q % PEERS == r // CAP) & (kinds == (q // PEERS + 1).astype(f32)) & (r < HALF)
        wide_ref[k * POOLED : (k + 1) * POOLED, k * LANES : (k + 1) * LANES] = one_hot(hit)


def forward_kernel(*refs):
    blocks = refs[:-5]
    count = len(blocks)
    w_in, pooled_ref, slope_ref, wide_ref, act_ref = refs[-5:]
    c0 = math.sqrt(2.0 / math.pi)
    c1 = c0 * 0.044715
    hidden = w_in.shape[2]
    for held in range(HELD):
        pool_table(blocks, held, wide_ref)
        rows = [block[held * HALF : (held + 1) * HALF, :] for block in blocks]
        rows = jnp.concatenate(rows, axis=0)
        for at in range(0, hidden, 640):
            to = slice(at, min(at + 640, hidden))
            full = nn(rows, w_in[held, :, to])
            for k in range(count):
                h = full[k * HALF : (k + 1) * HALF]
                h2 = h * h
                t = jnp.tanh(h * (c0 + c1 * h2))
                half = 0.5 + 0.5 * t
                act = h * half
                slope = half + act * (1.0 - t) * (c0 + 3.0 * c1 * h2)
                slope_ref[k, held, :, to] = slope.astype(bf16)
                act_ref[k * LANES : k * LANES + HALF, to] = act.astype(bf16)
        for k in range(count):
            act_ref[k * LANES + HALF : (k + 1) * LANES, :] = jnp.zeros(
                (LANES - HALF, hidden), bf16
            )
        pooled = nn(wide_ref[...], act_ref[...]).astype(bf16)
        for k in range(count):
            pooled_ref[k, held] = pooled[k * POOLED : (k + 1) * POOLED]


def forward(arrays, w_in):
    count = len(arrays)
    hidden = w_in.shape[2]
    return call(
        forward_kernel,
        [
            shape_of(count, HELD, POOLED, hidden),
            shape_of(count, HELD, HALF, hidden),
        ],
        [*arrays, w_in],
        scratch=[
            pltpu.VMEM((count * POOLED, count * LANES), bf16),
            pltpu.VMEM((count * LANES, hidden), bf16),
        ],
    )


def pick_kernel(x2_ref, x4_ref, first_ref, second_ref):
    first_ref[...] = x2_ref[:HALF, :]
    second_ref[...] = x4_ref[HALF:, :]


def stack_kernel(first_ref, second_ref, out_ref):
    out_ref[:HALF, :] = first_ref[...]
    out_ref[HALF:, :] = second_ref[...]


PARTS = {0: (0, 0), 1: (1, 0), 2: (1, 1), 4: (1, 2), 3: (2, 0), 5: (2, 1), 6: (3, 0), 7: (3, 1)}


def part_of(parts, k):
    which, at = PARTS[k]
    return parts[which], at


def out_kernel(shift, *refs):
    parts, (w_out, out_ref) = refs[:4], refs[4:]
    total = None
    for held in range(HELD):
        rows = []
        for k in AROUND:
            ref, at = part_of(parts, k + shift)
            rows.append(ref[at, held])
        part = nn(jnp.concatenate(rows, axis=0), w_out[held])
        total = part if total is None else total + part
    out_ref[...] = total.astype(bf16).reshape(out_ref.shape)


def join_kernel(own_ref, got_ref, out_ref):
    for ahead in range(4):
        to = lax.rem(lax.axis_index("dp") // 2 + ahead, 4)
        out_ref[to] = (own_ref[ahead].astype(f32) + got_ref[ahead].astype(f32)).astype(bf16)


def mean_kernel(part_ref, sum_ref, out_ref):
    total = sum_ref[...]
    for first in range(0, part_ref.shape[0], 8):
        total = total + jnp.sum(part_ref[first : first + 8].astype(f32), axis=0)
    out_ref[...] = jnp.broadcast_to((total * (1.0 / PAIR_TOKENS))[None], out_ref.shape)


def split(x):
    high = x.astype(bf16)
    return high, (x - high.astype(f32)).astype(bf16)


def loss_kernel(own_ref, other_ref, w_out, grad_ref, rows_ref, prod_ref, gi_ref, gt_ref):
    image = jnp.concatenate([own_ref[0], other_ref[0]], axis=0)
    text = jnp.concatenate([own_ref[1], other_ref[1]], axis=0)
    pairs, width = image.shape
    scale = PAIR_TOKENS / math.sqrt(width)
    (i0, i1), (t0, t1) = split(image), split(text)
    logits = scale * (nt(i0, t0) + (nt(i0, t1) + nt(i1, t0)))

    def softmax(axis):
        top = jnp.exp(logits - jnp.max(logits, axis=axis, keepdims=True))
        return top / jnp.sum(top, axis=axis, keepdims=True)

    same = jnp.where(iota((pairs, pairs), 0) == iota((pairs, pairs), 1), 2.0, 0.0)
    grad_logits = (objective_scale * scale / PAIR_TOKENS) * (softmax(1) + softmax(0) - same)

    def thrice(g, x0, x1):
        g0, g1 = split(g)
        return nn(g0, x0) + (nn(g0, x1) + nn(g1, x0))

    grad_image = thrice(grad_logits, t0, t1)
    grad_text = thrice(grad_logits.T, i0, i1)
    grad_ref[0] = grad_image
    grad_ref[1] = grad_text
    gi_ref[...] = grad_image.astype(bf16)
    gt_ref[...] = grad_text.astype(bf16)
    for at, k in enumerate(AROUND):
        for other in range(2):
            first = other * 4 * PEERS + lax.rem(lax.axis_index("dp") // 2 + at, 4) * PEERS
            span = pl.ds(pl.multiple_of(first, PEERS), PEERS)
            rows_ref[k + other, :PEERS, :] = gi_ref[span, :]
            rows_ref[k + other, PEERS:, :] = gt_ref[span, :]
    rows = rows_ref[...].reshape(8 * POOLED, width)
    for held in range(HELD):
        prod_ref[held] = nt(rows, w_out[held]).astype(bf16)


def backward_kernel(blocks, *refs):
    count = len(blocks)
    seconds, slopes = refs[:count], refs[count : 2 * count]
    prod_ref, w_in, pre_ref = refs[2 * count : 2 * count + 3]
    outs, (wide_ref, prods_ref) = refs[2 * count + 3 : -2], refs[-2:]
    for held in range(HELD):
        pool_table(seconds, held, wide_ref)
        for k, block in enumerate(blocks):
            prods_ref[k * POOLED : (k + 1) * POOLED, :] = prod_ref[
                held, block * POOLED : (block + 1) * POOLED, :
            ]
        grad_act = tn(wide_ref[...], prods_ref[...])
        for k, block in enumerate(blocks):
            slope = slopes[k][PARTS[block][1], held].astype(f32)
            pre_ref[k, held] = (grad_act[k * LANES : k * LANES + HALF] * slope).astype(bf16)
        pre = jnp.concatenate([pre_ref[k, held] for k in range(count)], axis=0)
        part = nt(pre, w_in[held]).astype(bf16)
        for k in range(count):
            rows = part[k * HALF : (k + 1) * HALF]
            outs[k][held * HALF : (held + 1) * HALF, :] = rows


def backward(blocks, rows, made, prod, w_in):
    count = len(blocks)
    width, hidden = w_in.shape[1:]
    return call(
        functools.partial(backward_kernel, blocks),
        [shape_of(count, HELD, HALF, hidden)]
        + [shape_of(2 * HALF, width)] * count,
        [
            *[rows[block] for block in blocks],
            *[made[PARTS[block][0]][1] for block in blocks],
            prod,
            w_in,
        ],
        scratch=[
            pltpu.VMEM((count * POOLED, count * LANES), bf16),
            pltpu.VMEM((count * POOLED, hidden), bf16),
        ],
    )


PAIRED = {7: (0, 0), 6: (1, 0), 5: (1, 1), 4: (1, 2), 3: (2, 0), 1: (2, 1), 2: (2, 2), 0: (2, 3)}


def grad_in_kernel(*refs):
    rows, pres = refs[:8], refs[8:11]
    out_ref, x_ref, p_ref = refs[11:]
    held = pl.program_id(0)

    def fill(which):
        for k in range(8):
            span = slice(k * HALF, (k + 1) * HALF)
            x_ref[span, :] = rows[k][which * HALF : (which + 1) * HALF, :]
            pair, at = PAIRED[k]
            p_ref[span, :] = pres[pair][at, which]

    for which in range(HELD):
        pl.when(held == which)(functools.partial(fill, which))
    out_ref[0] = tn(x_ref[...], p_ref[...])


def grad_in(rows, pres, width, hidden):
    whole = pl.BlockSpec(memory_space=pltpu.VMEM)
    return pl.pallas_call(
        grad_in_kernel,
        grid=(HELD,),
        out_shape=shape_of(HELD, width, hidden, dtype=f32),
        in_specs=[whole] * 11,
        out_specs=pl.BlockSpec((1, width, hidden), lambda i: (i, 0, 0)),
        scratch_shapes=[
            pltpu.VMEM((8 * HALF, width), bf16),
            pltpu.VMEM((8 * HALF, hidden), bf16),
        ],
        compiler_params=pltpu.CompilerParams(vmem_limit_bytes=26 * 1024 * 1024),
        cost_estimate=FREE,
    )(*rows, *pres)


def grad_out_kernel(*refs):
    parts, (rows_ref, out_ref) = refs[:4], refs[4:]
    held = pl.program_id(0)
    width = rows_ref.shape[2]
    pooled = []
    for k in range(8):
        ref, at = part_of(parts, k)
        pooled.append(ref[at, held])
    out_ref[0] = tn(jnp.concatenate(pooled, axis=0), rows_ref[...].reshape(8 * POOLED, width))


def grad_out(pooled, rows, width, hidden):
    whole = pl.BlockSpec(memory_space=pltpu.VMEM)
    return pl.pallas_call(
        grad_out_kernel,
        grid=(HELD,),
        out_shape=shape_of(HELD, hidden, width, dtype=f32),
        in_specs=[whole] * 5,
        out_specs=pl.BlockSpec((1, hidden, width), lambda i: (i, 0, 0)),
        compiler_params=pltpu.CompilerParams(vmem_limit_bytes=18 * 1024 * 1024),
        cost_estimate=FREE,
    )(*pooled, rows)


def plus_kernel(own_ref, got_ref, first_ref, second_ref):
    total = (own_ref[...].astype(f32) + got_ref[...].astype(f32)).astype(bf16)
    first_ref[...] = total[:HALF]
    second_ref[...] = total[HALF:]


def add_kernel(x_ref, y_ref, out_ref):
    out_ref[...] = (x_ref[...].astype(f32) + y_ref[...].astype(f32)).astype(bf16)


def below_kernel(own_ref, got_ref, above_ref, first_ref, second_ref):
    total = own_ref[...].astype(f32) + got_ref[...].astype(f32)
    first_ref[...] = total[:HALF].astype(bf16)
    second_ref[...] = (total[HALF:] + above_ref[...].astype(f32)).astype(bf16)


def settle_kernel(own_ref, got_ref, la_ref, lb_ref, ha_ref, hb_ref, out_ref):
    width = own_ref.shape[1]
    total = own_ref[...].astype(f32) + got_ref[...].astype(f32)
    first = total[:HALF] + la_ref[...].astype(f32) + ha_ref[...].astype(f32)
    second = total[HALF:] + lb_ref[...].astype(f32) + hb_ref[...].astype(f32)
    rows = jnp.concatenate([first.astype(bf16), second.astype(bf16)], axis=0)
    out_ref[...] = nn(repack_table(2 * HALF, True), rows).astype(bf16).reshape(PEERS, PAD, width)


def tail_kernel(ids_ref, slots_ref, tok_ref, gain_ref, grads_ref, back_ref, out_ref):
    at = (lax.axis_index("dp") // 2) * PEERS + lax.axis_index("expert")
    near = pl.ds(pl.multiple_of(at // 8 * 8, 8), 8)
    width = tok_ref.shape[1]
    tokens = tok_ref.shape[0]
    back = back_ref[...].reshape(PEERS * PAD, width)
    grad_normed = tn(slot_table(places(ids_ref, slots_ref)), back)
    unit, scale = normal_parts(tok_ref[...].astype(f32))
    grad = grad_normed * gain_ref[...].reshape(1, -1)
    grad = scale * (
        grad
        - jnp.mean(grad, axis=-1, keepdims=True)
        - unit * jnp.mean(grad * unit, axis=-1, keepdims=True)
    )
    for half in range(2):
        span = slice(half * (tokens // 2), (half + 1) * (tokens // 2))
        rows = grads_ref[half, near, :]
        own = jnp.where(iota(rows.shape, 0) == at % 8, rows, 0.0)
        own = jnp.sum(own, axis=0, keepdims=True)
        out_ref[span, :] = (own + grad[span]).astype(bf16)


def body(tokens, expert_ids, slots, ln_gain, w_in, w_out):
    width, hidden = w_in.shape[1:]
    row_count = tokens.shape[1] * tokens.shape[2]
    flat = tokens.reshape(row_count, width)
    ids, slot = expert_ids[0], slots[0]
    everyone = ("dp", "expert")
    chips = 4 * PEERS
    cores = [[d * PEERS + e for d in range(c, 8, 2) for e in range(PEERS)] for c in range(2)]

    def up(x):
        return lax.ppermute(x, "dp", [(i, (i + 2) % 8) for i in range(8)])

    def down(x):
        return lax.ppermute(x, "dp", [(i, (i + 6) % 8) for i in range(8)])

    def swap(x):
        return lax.ppermute(x, "dp", [(i, i ^ 1) for i in range(8)])

    def after(x, *tokens):
        return lax.optimization_barrier((x, *tokens))[0]

    def exchange(x):
        return lax.all_to_all(x, "expert", split_axis=0, concat_axis=0, tiled=True)

    def spread(x):
        return lax.all_to_all(
            x, everyone, split_axis=0, concat_axis=0, tiled=True, axis_index_groups=cores
        )

    sent, token_sum = call(
        dispatch_kernel,
        [shape_of(PEERS, PAD, width), shape_of(2, width, dtype=f32)],
        [ids, slot, flat, ln_gain],
        vmem=60,
    )
    rows_shape = shape_of(2 * HALF + KIND_ROWS, width)
    x0 = call(repack_kernel, rows_shape, [exchange(sent)])
    x2, x4, x1 = up(x0), down(x0), swap(x0)
    made = [forward([x0], w_in)]
    first, second = call(
        pick_kernel,
        [shape_of(HALF, width), shape_of(HALF + KIND_ROWS, width)],
        [after(x2, made[0][0]), x4],
    )
    a6, b6 = up(first), down(second)
    made.append(forward([x1, after(x2, first), x4], w_in))
    x3, x5 = swap(after(x2, made[1][0])), swap(after(x4, made[1][0]))
    x6 = call(stack_kernel, rows_shape, [after(a6, made[1][0]), b6])
    x7 = swap(x6)
    made.append(forward([after(x3, x6), x5], w_in))
    made.append(forward([x6, after(x7, made[2][0])], w_in))
    pooled = [m[0] for m in made]
    block_rows = [x0, x1, x2, x3, x4, x5, x6, x7]

    def product(shift, w_out):
        return call(
            functools.partial(out_kernel, shift),
            shape_of(4, POOLED, width),
            [*pooled, w_out],
        )

    other = product(1, w_out)
    got = swap(other)
    own = product(0, after(w_out, other))
    joined = call(join_kernel, shape_of(4, POOLED, width), [own, after(got, own)])
    joined = joined.reshape(4, 2, PEERS, width).transpose(0, 2, 1, 3).reshape(chips, 2, width)
    emb = call(
        mean_kernel, shape_of(chips, 2, width, dtype=f32), [spread(joined), token_sum]
    )
    emb = spread(emb).transpose(1, 0, 2)
    grad_pooled, rows, prod = call(
        loss_kernel,
        [
            shape_of(2, 8 * PEERS, width, dtype=f32),
            shape_of(8, POOLED, width),
            shape_of(HELD, 8 * POOLED, hidden),
        ],
        [emb, swap(emb), w_out],
        scratch=[pltpu.VMEM((8 * PEERS, width), bf16), pltpu.VMEM((8 * PEERS, width), bf16)],
    )

    def plus(x, y):
        return call(plus_kernel, [shape_of(HALF, width)] * 2, [x, y])

    half = shape_of(HALF, width)
    pre7, p7 = backward((7,), block_rows, made, prod, w_in)
    s7 = swap(p7)
    pre654, p6, p5, p4 = backward((6, 5, 4), block_rows, made, after(prod, p7), w_in)
    s5 = swap(p5)
    r6a, r6b = plus(p6, s7)
    from_below, from_above = up(r6a), down(r6b)
    rest, p3, p1, p2, p0 = backward((3, 1, 2, 0), block_rows, made, after(prod, r6a), w_in)
    r4a, r4b = plus(p4, after(s5, p2))
    low_b = up(r4b)
    s3, s1 = swap(p3), swap(p1)
    low_a = call(add_kernel, half, [after(r4a, p0), from_below], cost=DEAR)
    r2a, r2b = call(below_kernel, [half, half], [p2, after(s3, low_a), from_above])
    high_a, high_b = down(r2a), down(r2b)
    grad_w_out = grad_out(pooled, after(rows, r2a), width, hidden)
    grad_w_in = grad_in(
        block_rows, [pre7, pre654, after(rest, grad_w_out)], width, hidden
    )
    low_a = up(low_a)
    settled = call(
        settle_kernel,
        shape_of(PEERS, PAD, width),
        [after(p0, grad_w_in), s1, low_a, low_b, high_a, high_b],
    )
    grad_flat = call(
        tail_kernel,
        shape_of(row_count, width),
        [ids, slot, flat, ln_gain, grad_pooled, exchange(settled)],
    )
    return (grad_flat.reshape(tokens.shape), grad_w_in, grad_w_out)


def solution(mesh):
    placed = (
        P(("dp", "expert"), None, None, None),
        P(("dp", "expert"), None, None),
        P(("dp", "expert"), None, None),
        P(),
        P("expert", None, "dp"),
        P("expert", "dp", None),
    )
    return jax.shard_map(
        body,
        mesh=mesh,
        in_specs=placed,
        out_specs=(
            P(("dp", "expert"), None, None, None),
            P("expert", None, "dp"),
            P("expert", "dp", None),
        ),
        check_vma=False,
    )
```

```python
import functools
import math

import jax
import jax.numpy as jnp
from jax import lax
from jax.experimental import pallas as pl
from jax.experimental.pallas import tpu as pltpu
from jax.sharding import PartitionSpec as P

norm_eps = 1e-06
objective_scale = 32.0
bf16 = jnp.bfloat16
f32 = jnp.float32
i32 = jnp.int32

CAP = 6
HELD = 2
GROUP = HELD * CAP
PAD = 16
PEERS = 16
HALF = PEERS * CAP
KIND_ROWS = 8
POOLED = 2 * PEERS
PAIR_TOKENS = 64
LANES = 128
AROUND = (0, 4, 6, 2)


def nn(a, b):
    return lax.dot_general(a, b, (((1,), (0,)), ((), ())), preferred_element_type=f32)


def nt(a, b, precision=None):
    return lax.dot_general(
        a, b, (((1,), (1,)), ((), ())), precision=precision, preferred_element_type=f32
    )


def tn(a, b, precision=None):
    return lax.dot_general(
        a, b, (((0,), (0,)), ((), ())), precision=precision, preferred_element_type=f32
    )


def iota(shape, dim):
    return lax.broadcasted_iota(i32, shape, dim)


def shape_of(*dims, dtype=bf16):
    return jax.ShapeDtypeStruct(dims, dtype)


def one_hot(hit):
    return jnp.where(hit, 1.0, 0.0).astype(bf16)


FREE = pl.CostEstimate(flops=1, bytes_accessed=1, transcendentals=0)
DEAR = pl.CostEstimate(flops=10**11, bytes_accessed=10**8, transcendentals=0)


def call(kernel, out, args, smem=(), hbm=(), scratch=(), vmem=14, cost=FREE):
    def space(k):
        return pltpu.SMEM if k in smem else pltpu.HBM if k in hbm else pltpu.VMEM

    many = isinstance(out, (list, tuple))
    out_specs = [pl.BlockSpec(memory_space=pltpu.VMEM) for _ in (out if many else [out])]
    return pl.pallas_call(
        kernel,
        out_shape=out,
        in_specs=[pl.BlockSpec(memory_space=space(k)) for k in range(len(args))],
        out_specs=out_specs if many else out_specs[0],
        scratch_shapes=list(scratch),
        compiler_params=pltpu.CompilerParams(vmem_limit_bytes=vmem * 1024 * 1024),
        cost_estimate=cost,
    )(*args)


def normal_parts(x):
    centred = x - jnp.mean(x, axis=-1, keepdims=True)
    spread = jnp.mean(centred * centred, axis=-1, keepdims=True)
    scale = lax.rsqrt(spread + norm_eps)
    return centred * scale, scale


def places(ids_ref, slots_ref):
    pos = ids_ref[...] * CAP + slots_ref[...]
    return jnp.concatenate([pos[:1], pos[1:]], axis=1)


def slot_table(pos):
    tokens = pos.shape[1]
    row = iota((PEERS * PAD, tokens), 0)
    want = (row // PAD) * GROUP + row % PAD
    return one_hot((want == pos) & (row % PAD < GROUP))


def fetch(sources, refs, sems):
    copies = [pltpu.make_async_copy(a, b, sems.at[k]) for k, (a, b) in enumerate(zip(sources, refs))]
    for copy in copies:
        copy.start()
    return copies


def input_scratch(tokens, width):
    return [
        pltpu.VMEM((2, tokens // 2), i32),
        pltpu.VMEM((2, tokens // 2), i32),
        pltpu.VMEM((tokens, width), bf16),
        pltpu.VMEM((width,), f32),
        pltpu.SemaphoreType.DMA((4,)),
    ]


def dispatch_kernel(ids, slots, toks, gain, out_ref, sum_ref, ids_ref, slots_ref, tok_ref, gain_ref, sems):
    copies = fetch((ids, slots, toks, gain), (ids_ref, slots_ref, tok_ref, gain_ref), sems)
    copies[0].wait()
    copies[1].wait()
    pos = places(ids_ref, slots_ref)
    tokens, width = tok_ref.shape
    table = slot_table(pos)
    row = iota((PEERS * PAD, tokens), 0)
    goes = one_hot((row % PAD == GROUP) & (pos // GROUP == row // PAD))
    place = pos % GROUP
    column = (place // CAP) * LANES + lax.axis_index("expert") * CAP + place % CAP
    lane = iota((2 * LANES, tokens), 0)
    kind = jnp.where(iota((2 * LANES, tokens), 1) < tokens // 2, 1.0, 2.0)
    kinds = nt(goes, jnp.where(lane == column, kind, 0.0).astype(bf16))
    copies[2].wait()
    copies[3].wait()
    x = tok_ref[...].astype(f32)
    normed = normal_parts(x)[0] * gain_ref[...].reshape(1, -1)
    sent = nn(table, normed.astype(bf16))
    first = sent[:, : 2 * LANES] + kinds
    out_ref[:, :, : 2 * LANES] = first.astype(bf16).reshape(PEERS, PAD, 2 * LANES)
    out_ref[:, :, 2 * LANES :] = sent[:, 2 * LANES :].astype(bf16).reshape(
        PEERS, PAD, width - 2 * LANES
    )
    sum_ref[0:1, :] = jnp.sum(x[: tokens // 2], axis=0, keepdims=True)
    sum_ref[1:2, :] = jnp.sum(x[tokens // 2 :], axis=0, keepdims=True)


def repack_table(rows, back):
    shape = (PEERS * PAD, rows) if back else (rows, PEERS * PAD)
    r = iota(shape, 1 if back else 0)
    m = iota(shape, 0 if back else 1)
    held, rest = r // HALF, r % HALF
    from_slot = (rest // CAP) * PAD + held * CAP + rest % CAP
    hit = (r < 2 * HALF) & (m == from_slot)
    if not back:
        hit = hit | ((r == 2 * HALF) & (m % PAD == GROUP))
    return one_hot(hit)


def repack_kernel(in_ref, out_ref):
    width = in_ref.shape[2]
    table = repack_table(out_ref.shape[0], False)
    out_ref[...] = nn(table, in_ref[...].reshape(PEERS * PAD, width)).astype(bf16)


def pool_table(seconds, held, wide_ref):
    wide_ref[...] = jnp.zeros_like(wide_ref)
    q = iota((POOLED, LANES), 0)
    r = iota((POOLED, LANES), 1)
    for k, ref in enumerate(seconds):
        kinds = ref[2 * HALF : 2 * HALF + KIND_ROWS, held * LANES : (held + 1) * LANES]
        kinds = kinds.astype(f32)[:1]
        hit = (q % PEERS == r // CAP) & (kinds == (q // PEERS + 1).astype(f32)) & (r < HALF)
        wide_ref[k * POOLED : (k + 1) * POOLED, k * LANES : (k + 1) * LANES] = one_hot(hit)


def forward_kernel(*refs):
    blocks = refs[:-5]
    count = len(blocks)
    w_in, pooled_ref, slope_ref, wide_ref, act_ref = refs[-5:]
    c0 = math.sqrt(2.0 / math.pi)
    c1 = c0 * 0.044715
    hidden = w_in.shape[2]
    for held in range(HELD):
        pool_table(blocks, held, wide_ref)
        rows = [block[held * HALF : (held + 1) * HALF, :] for block in blocks]
        rows = jnp.concatenate(rows, axis=0)
        for at in range(0, hidden, 640):
            to = slice(at, min(at + 640, hidden))
            full = nn(rows, w_in[held, :, to])
            for k in range(count):
                h = full[k * HALF : (k + 1) * HALF]
                h2 = h * h
                t = jnp.tanh(h * (c0 + c1 * h2))
                half = 0.5 + 0.5 * t
                act = h * half
                slope = half + act * (1.0 - t) * (c0 + 3.0 * c1 * h2)
                slope_ref[k, held, :, to] = slope.astype(bf16)
                act_ref[k * LANES : k * LANES + HALF, to] = act.astype(bf16)
        for k in range(count):
            act_ref[k * LANES + HALF : (k + 1) * LANES, :] = jnp.zeros(
                (LANES - HALF, hidden), bf16
            )
        pooled = nn(wide_ref[...], act_ref[...]).astype(bf16)
        for k in range(count):
            pooled_ref[k, held] = pooled[k * POOLED : (k + 1) * POOLED]


def forward(arrays, w_in):
    count = len(arrays)
    hidden = w_in.shape[2]
    return call(
        forward_kernel,
        [
            shape_of(count, HELD, POOLED, hidden),
            shape_of(count, HELD, HALF, hidden),
        ],
        [*arrays, w_in],
        scratch=[
            pltpu.VMEM((count * POOLED, count * LANES), bf16),
            pltpu.VMEM((count * LANES, hidden), bf16),
        ],
    )


def pick_kernel(x2_ref, x4_ref, first_ref, second_ref):
    first_ref[...] = x2_ref[:HALF, :]
    second_ref[...] = x4_ref[HALF:, :]


def stack_kernel(first_ref, second_ref, out_ref):
    out_ref[:HALF, :] = first_ref[...]
    out_ref[HALF:, :] = second_ref[...]


PARTS = {0: (0, 0), 1: (1, 0), 2: (1, 1), 4: (1, 2), 3: (2, 0), 5: (2, 1), 6: (3, 0), 7: (3, 1)}


def part_of(parts, k):
    which, at = PARTS[k]
    return parts[which], at


def out_kernel(shift, *refs):
    parts, (w_out, out_ref) = refs[:4], refs[4:]
    total = None
    for held in range(HELD):
        rows = []
        for k in AROUND:
            ref, at = part_of(parts, k + shift)
            rows.append(ref[at, held])
        part = nn(jnp.concatenate(rows, axis=0), w_out[held])
        total = part if total is None else total + part
    out_ref[...] = total.astype(bf16).reshape(out_ref.shape)


def join_kernel(own_ref, got_ref, out_ref):
    for ahead in range(4):
        to = lax.rem(lax.axis_index("dp") // 2 + ahead, 4)
        out_ref[to] = (own_ref[ahead].astype(f32) + got_ref[ahead].astype(f32)).astype(bf16)


def mean_kernel(part_ref, sum_ref, out_ref):
    total = sum_ref[...]
    for first in range(0, part_ref.shape[0], 8):
        total = total + jnp.sum(part_ref[first : first + 8].astype(f32), axis=0)
    out_ref[...] = jnp.broadcast_to((total * (1.0 / PAIR_TOKENS))[None], out_ref.shape)


def split(x):
    high = x.astype(bf16)
    return high, (x - high.astype(f32)).astype(bf16)


def loss_kernel(own_ref, other_ref, w_out, grad_ref, rows_ref, prod_ref, gi_ref, gt_ref):
    image = jnp.concatenate([own_ref[0], other_ref[0]], axis=0)
    text = jnp.concatenate([own_ref[1], other_ref[1]], axis=0)
    pairs, width = image.shape
    scale = PAIR_TOKENS / math.sqrt(width)
    (i0, i1), (t0, t1) = split(image), split(text)
    logits = scale * (nt(i0, t0) + (nt(i0, t1) + nt(i1, t0)))

    def softmax(axis):
        top = jnp.exp(logits - jnp.max(logits, axis=axis, keepdims=True))
        return top / jnp.sum(top, axis=axis, keepdims=True)

    same = jnp.where(iota((pairs, pairs), 0) == iota((pairs, pairs), 1), 2.0, 0.0)
    grad_logits = (objective_scale * scale / PAIR_TOKENS) * (softmax(1) + softmax(0) - same)

    def thrice(g, x0, x1):
        g0, g1 = split(g)
        return nn(g0, x0) + (nn(g0, x1) + nn(g1, x0))

    grad_image = thrice(grad_logits, t0, t1)
    grad_text = thrice(grad_logits.T, i0, i1)
    grad_ref[0] = grad_image
    grad_ref[1] = grad_text
    gi_ref[...] = grad_image.astype(bf16)
    gt_ref[...] = grad_text.astype(bf16)
    for at, k in enumerate(AROUND):
        for other in range(2):
            first = other * 4 * PEERS + lax.rem(lax.axis_index("dp") // 2 + at, 4) * PEERS
            span = pl.ds(pl.multiple_of(first, PEERS), PEERS)
            rows_ref[k + other, :PEERS, :] = gi_ref[span, :]
            rows_ref[k + other, PEERS:, :] = gt_ref[span, :]
    rows = rows_ref[...].reshape(8 * POOLED, width)
    for held in range(HELD):
        prod_ref[held] = nt(rows, w_out[held]).astype(bf16)


def backward_kernel(blocks, *refs):
    count = len(blocks)
    seconds, slopes = refs[:count], refs[count : 2 * count]
    prod_ref, w_in, pre_ref = refs[2 * count : 2 * count + 3]
    outs, (wide_ref, prods_ref) = refs[2 * count + 3 : -2], refs[-2:]
    for held in range(HELD):
        pool_table(seconds, held, wide_ref)
        for k, block in enumerate(blocks):
            prods_ref[k * POOLED : (k + 1) * POOLED, :] = prod_ref[
                held, block * POOLED : (block + 1) * POOLED, :
            ]
        grad_act = tn(wide_ref[...], prods_ref[...])
        for k, block in enumerate(blocks):
            slope = slopes[k][PARTS[block][1], held].astype(f32)
            pre_ref[k, held] = (grad_act[k * LANES : k * LANES + HALF] * slope).astype(bf16)
        pre = jnp.concatenate([pre_ref[k, held] for k in range(count)], axis=0)
        part = nt(pre, w_in[held]).astype(bf16)
        for k in range(count):
            rows = part[k * HALF : (k + 1) * HALF]
            outs[k][held * HALF : (held + 1) * HALF, :] = rows


def backward(blocks, rows, made, prod, w_in):
    count = len(blocks)
    width, hidden = w_in.shape[1:]
    return call(
        functools.partial(backward_kernel, blocks),
        [shape_of(count, HELD, HALF, hidden)]
        + [shape_of(2 * HALF, width)] * count,
        [
            *[rows[block] for block in blocks],
            *[made[PARTS[block][0]][1] for block in blocks],
            prod,
            w_in,
        ],
        scratch=[
            pltpu.VMEM((count * POOLED, count * LANES), bf16),
            pltpu.VMEM((count * POOLED, hidden), bf16),
        ],
    )


PAIRED = {7: (0, 0), 6: (1, 0), 5: (1, 1), 4: (1, 2), 3: (2, 0), 1: (2, 1), 2: (2, 2), 0: (2, 3)}


def grads_kernel(*refs):
    rows, pres, parts, grads = refs[:8], refs[8:11], refs[11:15], refs[15]
    in_ref, out_ref, x_ref, p_ref = refs[16:]
    step = pl.program_id(0)
    width = in_ref.shape[1]

    def inner(held):
        for k in range(8):
            span = slice(k * HALF, (k + 1) * HALF)
            x_ref[span, :] = rows[k][held * HALF : (held + 1) * HALF, :]
            pair, at = PAIRED[k]
            p_ref[span, :] = pres[pair][at, held]
        in_ref[0] = tn(x_ref[...], p_ref[...])

    def outer(held):
        pooled = []
        for k in range(8):
            ref, at = part_of(parts, k)
            pooled.append(ref[at, held])
        out_ref[0] = tn(jnp.concatenate(pooled, axis=0), grads[...].reshape(8 * POOLED, width))

    for held in range(HELD):
        pl.when(step == held)(functools.partial(inner, held))
        pl.when(step == HELD + held)(functools.partial(outer, held))


def weight_grads(rows, pres, pooled, grads, width, hidden):
    whole = pl.BlockSpec(memory_space=pltpu.VMEM)
    return pl.pallas_call(
        grads_kernel,
        grid=(2 * HELD,),
        out_shape=[
            shape_of(HELD, width, hidden, dtype=f32),
            shape_of(HELD, hidden, width, dtype=f32),
        ],
        in_specs=[whole] * 16,
        out_specs=[
            pl.BlockSpec((1, width, hidden), lambda i: (jnp.minimum(i, HELD - 1), 0, 0)),
            pl.BlockSpec((1, hidden, width), lambda i: (jnp.maximum(i - HELD, 0), 0, 0)),
        ],
        scratch_shapes=[
            pltpu.VMEM((8 * HALF, width), bf16),
            pltpu.VMEM((8 * HALF, hidden), bf16),
        ],
        compiler_params=pltpu.CompilerParams(vmem_limit_bytes=30 * 1024 * 1024),
        cost_estimate=FREE,
    )(*rows, *pres, *pooled, grads)


def plus_kernel(own_ref, got_ref, first_ref, second_ref):
    total = (own_ref[...].astype(f32) + got_ref[...].astype(f32)).astype(bf16)
    first_ref[...] = total[:HALF]
    second_ref[...] = total[HALF:]


def add_kernel(x_ref, y_ref, out_ref):
    out_ref[...] = (x_ref[...].astype(f32) + y_ref[...].astype(f32)).astype(bf16)


def below_kernel(own_ref, got_ref, above_ref, first_ref, second_ref):
    total = own_ref[...].astype(f32) + got_ref[...].astype(f32)
    first_ref[...] = total[:HALF].astype(bf16)
    second_ref[...] = (total[HALF:] + above_ref[...].astype(f32)).astype(bf16)


def settle_kernel(own_ref, got_ref, la_ref, lb_ref, ha_ref, hb_ref, out_ref):
    width = own_ref.shape[1]
    total = own_ref[...].astype(f32) + got_ref[...].astype(f32)
    first = total[:HALF] + la_ref[...].astype(f32) + ha_ref[...].astype(f32)
    second = total[HALF:] + lb_ref[...].astype(f32) + hb_ref[...].astype(f32)
    rows = jnp.concatenate([first.astype(bf16), second.astype(bf16)], axis=0)
    out_ref[...] = nn(repack_table(2 * HALF, True), rows).astype(bf16).reshape(PEERS, PAD, width)


def tail_kernel(ids_ref, slots_ref, tok_ref, gain_ref, grads_ref, back_ref, out_ref):
    at = (lax.axis_index("dp") // 2) * PEERS + lax.axis_index("expert")
    near = pl.ds(pl.multiple_of(at // 8 * 8, 8), 8)
    width = tok_ref.shape[1]
    tokens = tok_ref.shape[0]
    back = back_ref[...].reshape(PEERS * PAD, width)
    grad_normed = tn(slot_table(places(ids_ref, slots_ref)), back)
    unit, scale = normal_parts(tok_ref[...].astype(f32))
    grad = grad_normed * gain_ref[...].reshape(1, -1)
    grad = scale * (
        grad
        - jnp.mean(grad, axis=-1, keepdims=True)
        - unit * jnp.mean(grad * unit, axis=-1, keepdims=True)
    )
    for half in range(2):
        span = slice(half * (tokens // 2), (half + 1) * (tokens // 2))
        rows = grads_ref[half, near, :]
        own = jnp.where(iota(rows.shape, 0) == at % 8, rows, 0.0)
        own = jnp.sum(own, axis=0, keepdims=True)
        out_ref[span, :] = (own + grad[span]).astype(bf16)


def body(tokens, expert_ids, slots, ln_gain, w_in, w_out):
    width, hidden = w_in.shape[1:]
    row_count = tokens.shape[1] * tokens.shape[2]
    flat = tokens.reshape(row_count, width)
    ids, slot = expert_ids[0], slots[0]
    everyone = ("dp", "expert")
    chips = 4 * PEERS
    cores = [[d * PEERS + e for d in range(c, 8, 2) for e in range(PEERS)] for c in range(2)]

    def up(x):
        return lax.ppermute(x, "dp", [(i, (i + 2) % 8) for i in range(8)])

    def down(x):
        return lax.ppermute(x, "dp", [(i, (i + 6) % 8) for i in range(8)])

    def swap(x):
        return lax.ppermute(x, "dp", [(i, i ^ 1) for i in range(8)])

    def after(x, *tokens):
        return lax.optimization_barrier((x, *tokens))[0]

    def exchange(x):
        return lax.all_to_all(x, "expert", split_axis=0, concat_axis=0, tiled=True)

    def spread(x):
        return lax.all_to_all(
            x, everyone, split_axis=0, concat_axis=0, tiled=True, axis_index_groups=cores
        )

    sent, token_sum = call(
        dispatch_kernel,
        [shape_of(PEERS, PAD, width), shape_of(2, width, dtype=f32)],
        [ids, slot, flat, ln_gain],
        hbm=(0, 1, 2, 3),
        scratch=input_scratch(row_count, width),
        vmem=60,
    )
    rows_shape = shape_of(2 * HALF + KIND_ROWS, width)
    x0 = call(repack_kernel, rows_shape, [exchange(sent)])
    x2, x4, x1 = up(x0), down(x0), swap(x0)
    made = [forward([x0], w_in)]
    first, second = call(
        pick_kernel,
        [shape_of(HALF, width), shape_of(HALF + KIND_ROWS, width)],
        [after(x2, made[0][0]), x4],
    )
    a6, b6 = up(first), down(second)
    made.append(forward([x1, after(x2, first), x4], w_in))
    x3, x5 = swap(after(x2, made[1][0])), swap(after(x4, made[1][0]))
    x6 = call(stack_kernel, rows_shape, [after(a6, made[1][0]), b6])
    x7 = swap(x6)
    made.append(forward([after(x3, x6), x5], w_in))
    made.append(forward([x6, after(x7, made[2][0])], w_in))
    pooled = [m[0] for m in made]
    block_rows = [x0, x1, x2, x3, x4, x5, x6, x7]

    def product(shift, w_out):
        return call(
            functools.partial(out_kernel, shift),
            shape_of(4, POOLED, width),
            [*pooled, w_out],
        )

    other = product(1, w_out)
    got = swap(other)
    own = product(0, after(w_out, other))
    joined = call(join_kernel, shape_of(4, POOLED, width), [own, after(got, own)])
    joined = joined.reshape(4, 2, PEERS, width).transpose(0, 2, 1, 3).reshape(chips, 2, width)
    emb = call(
        mean_kernel, shape_of(chips, 2, width, dtype=f32), [spread(joined), token_sum]
    )
    emb = spread(emb).transpose(1, 0, 2)
    grad_pooled, rows, prod = call(
        loss_kernel,
        [
            shape_of(2, 8 * PEERS, width, dtype=f32),
            shape_of(8, POOLED, width),
            shape_of(HELD, 8 * POOLED, hidden),
        ],
        [emb, swap(emb), w_out],
        scratch=[pltpu.VMEM((8 * PEERS, width), bf16), pltpu.VMEM((8 * PEERS, width), bf16)],
    )

    def plus(x, y):
        return call(plus_kernel, [shape_of(HALF, width)] * 2, [x, y])

    half = shape_of(HALF, width)
    pre7, p7 = backward((7,), block_rows, made, prod, w_in)
    s7 = swap(p7)
    pre654, p6, p5, p4 = backward((6, 5, 4), block_rows, made, after(prod, p7), w_in)
    s5 = swap(p5)
    r6a, r6b = plus(p6, s7)
    from_below, from_above = up(r6a), down(r6b)
    rest, p3, p1, p2, p0 = backward((3, 1, 2, 0), block_rows, made, after(prod, r6a), w_in)
    r4a, r4b = plus(p4, after(s5, p2))
    low_b = up(r4b)
    s3, s1 = swap(p3), swap(p1)
    low_a = call(add_kernel, half, [after(r4a, p0), from_below], cost=DEAR)
    r2a, r2b = call(below_kernel, [half, half], [p2, after(s3, low_a), from_above])
    high_a, high_b = down(r2a), down(r2b)
    grad_w_in, grad_w_out = weight_grads(
        block_rows, [pre7, pre654, after(rest, r2a)], pooled, rows, width, hidden
    )
    low_a = up(low_a)
    settled = call(
        settle_kernel,
        shape_of(PEERS, PAD, width),
        [after(p0, grad_w_in), s1, low_a, low_b, high_a, high_b],
    )
    grad_flat = call(
        tail_kernel,
        shape_of(row_count, width),
        [ids, slot, flat, ln_gain, grad_pooled, exchange(settled)],
    )
    return (grad_flat.reshape(tokens.shape), grad_w_in, grad_w_out)


def solution(mesh):
    placed = (
        P(("dp", "expert"), None, None, None),
        P(("dp", "expert"), None, None),
        P(("dp", "expert"), None, None),
        P(),
        P("expert", None, "dp"),
        P("expert", "dp", None),
    )
    return jax.shard_map(
        body,
        mesh=mesh,
        in_specs=placed,
        out_specs=(
            P(("dp", "expert"), None, None, None),
            P("expert", None, "dp"),
            P("expert", "dp", None),
        ),
        check_vma=False,
    )
```

```python
import functools
import math

import jax
import jax.numpy as jnp
from jax import lax
from jax.experimental import pallas as pl
from jax.experimental.pallas import tpu as pltpu
from jax.sharding import PartitionSpec as P

norm_eps = 1e-06
objective_scale = 32.0
bf16 = jnp.bfloat16
f32 = jnp.float32
i32 = jnp.int32

CAP = 6
HELD = 2
GROUP = HELD * CAP
PAD = 16
PEERS = 16
HALF = PEERS * CAP
KIND_ROWS = 8
POOLED = 2 * PEERS
PAIR_TOKENS = 64
LANES = 128
AROUND = (0, 4, 6, 2)


def nn(a, b):
    return lax.dot_general(a, b, (((1,), (0,)), ((), ())), preferred_element_type=f32)


def nt(a, b, precision=None):
    return lax.dot_general(
        a, b, (((1,), (1,)), ((), ())), precision=precision, preferred_element_type=f32
    )


def tn(a, b, precision=None):
    return lax.dot_general(
        a, b, (((0,), (0,)), ((), ())), precision=precision, preferred_element_type=f32
    )


def iota(shape, dim):
    return lax.broadcasted_iota(i32, shape, dim)


def shape_of(*dims, dtype=bf16):
    return jax.ShapeDtypeStruct(dims, dtype)


def one_hot(hit):
    return jnp.where(hit, 1.0, 0.0).astype(bf16)


FREE = pl.CostEstimate(flops=1, bytes_accessed=1, transcendentals=0)
DEAR = pl.CostEstimate(flops=10**11, bytes_accessed=10**8, transcendentals=0)


def call(kernel, out, args, smem=(), hbm=(), scratch=(), vmem=14, cost=FREE):
    def space(k):
        return pltpu.SMEM if k in smem else pltpu.HBM if k in hbm else pltpu.VMEM

    many = isinstance(out, (list, tuple))
    out_specs = [pl.BlockSpec(memory_space=pltpu.VMEM) for _ in (out if many else [out])]
    return pl.pallas_call(
        kernel,
        out_shape=out,
        in_specs=[pl.BlockSpec(memory_space=space(k)) for k in range(len(args))],
        out_specs=out_specs if many else out_specs[0],
        scratch_shapes=list(scratch),
        compiler_params=pltpu.CompilerParams(vmem_limit_bytes=vmem * 1024 * 1024),
        cost_estimate=cost,
    )(*args)


def normal_parts(x):
    centred = x - jnp.mean(x, axis=-1, keepdims=True)
    spread = jnp.mean(centred * centred, axis=-1, keepdims=True)
    scale = lax.rsqrt(spread + norm_eps)
    return centred * scale, scale


def places(ids_ref, slots_ref):
    pos = ids_ref[...] * CAP + slots_ref[...]
    return jnp.concatenate([pos[:1], pos[1:]], axis=1)


def slot_table(pos):
    tokens = pos.shape[1]
    row = iota((PEERS * PAD, tokens), 0)
    want = (row // PAD) * GROUP + row % PAD
    return one_hot((want == pos) & (row % PAD < GROUP))


def fetch(sources, refs, sems):
    copies = [pltpu.make_async_copy(a, b, sems.at[k]) for k, (a, b) in enumerate(zip(sources, refs))]
    for copy in copies:
        copy.start()
    return copies


def input_scratch(tokens, width):
    return [
        pltpu.VMEM((2, tokens // 2), i32),
        pltpu.VMEM((2, tokens // 2), i32),
        pltpu.VMEM((tokens, width), bf16),
        pltpu.VMEM((width,), f32),
        pltpu.SemaphoreType.DMA((4,)),
    ]


def dispatch_kernel(ids, slots, toks, gain, out_ref, sum_ref, ids_ref, slots_ref, tok_ref, gain_ref, sems):
    copies = fetch((ids, slots, toks, gain), (ids_ref, slots_ref, tok_ref, gain_ref), sems)
    copies[0].wait()
    copies[1].wait()
    pos = places(ids_ref, slots_ref)
    tokens, width = tok_ref.shape
    table = slot_table(pos)
    row = iota((PEERS * PAD, tokens), 0)
    goes = one_hot((row % PAD == GROUP) & (pos // GROUP == row // PAD))
    place = pos % GROUP
    column = (place // CAP) * LANES + lax.axis_index("expert") * CAP + place % CAP
    lane = iota((2 * LANES, tokens), 0)
    kind = jnp.where(iota((2 * LANES, tokens), 1) < tokens // 2, 1.0, 2.0)
    kinds = nt(goes, jnp.where(lane == column, kind, 0.0).astype(bf16))
    copies[2].wait()
    copies[3].wait()
    x = tok_ref[...].astype(f32)
    normed = normal_parts(x)[0] * gain_ref[...].reshape(1, -1)
    sent = nn(table, normed.astype(bf16))
    first = sent[:, : 2 * LANES] + kinds
    out_ref[:, :, : 2 * LANES] = first.astype(bf16).reshape(PEERS, PAD, 2 * LANES)
    out_ref[:, :, 2 * LANES :] = sent[:, 2 * LANES :].astype(bf16).reshape(
        PEERS, PAD, width - 2 * LANES
    )
    sum_ref[0:1, :] = jnp.sum(x[: tokens // 2], axis=0, keepdims=True)
    sum_ref[1:2, :] = jnp.sum(x[tokens // 2 :], axis=0, keepdims=True)


def repack_table(rows, back):
    shape = (PEERS * PAD, rows) if back else (rows, PEERS * PAD)
    r = iota(shape, 1 if back else 0)
    m = iota(shape, 0 if back else 1)
    held, rest = r // HALF, r % HALF
    from_slot = (rest // CAP) * PAD + held * CAP + rest % CAP
    hit = (r < 2 * HALF) & (m == from_slot)
    if not back:
        hit = hit | ((r == 2 * HALF) & (m % PAD == GROUP))
    return one_hot(hit)


def repack_kernel(in_ref, out_ref):
    width = in_ref.shape[2]
    table = repack_table(out_ref.shape[0], False)
    out_ref[...] = nn(table, in_ref[...].reshape(PEERS * PAD, width)).astype(bf16)


def pool_table(seconds, held, wide_ref):
    wide_ref[...] = jnp.zeros_like(wide_ref)
    q = iota((POOLED, LANES), 0)
    r = iota((POOLED, LANES), 1)
    for k, ref in enumerate(seconds):
        kinds = ref[2 * HALF : 2 * HALF + KIND_ROWS, held * LANES : (held + 1) * LANES]
        kinds = kinds.astype(f32)[:1]
        hit = (q % PEERS == r // CAP) & (kinds == (q // PEERS + 1).astype(f32)) & (r < HALF)
        wide_ref[k * POOLED : (k + 1) * POOLED, k * LANES : (k + 1) * LANES] = one_hot(hit)


def forward_kernel(*refs):
    blocks = refs[:-5]
    count = len(blocks)
    w_in, pooled_ref, slope_ref, wide_ref, act_ref = refs[-5:]
    c0 = math.sqrt(2.0 / math.pi)
    c1 = c0 * 0.044715
    hidden = w_in.shape[2]
    for held in range(HELD):
        pool_table(blocks, held, wide_ref)
        rows = [block[held * HALF : (held + 1) * HALF, :] for block in blocks]
        rows = jnp.concatenate(rows, axis=0)
        for at in range(0, hidden, 640):
            to = slice(at, min(at + 640, hidden))
            full = nn(rows, w_in[held, :, to])
            for k in range(count):
                h = full[k * HALF : (k + 1) * HALF]
                h2 = h * h
                t = jnp.tanh(h * (c0 + c1 * h2))
                half = 0.5 + 0.5 * t
                act = h * half
                slope = half + act * (1.0 - t) * (c0 + 3.0 * c1 * h2)
                slope_ref[k, held, :, to] = slope.astype(bf16)
                act_ref[k * LANES : k * LANES + HALF, to] = act.astype(bf16)
        for k in range(count):
            act_ref[k * LANES + HALF : (k + 1) * LANES, :] = jnp.zeros(
                (LANES - HALF, hidden), bf16
            )
        pooled = nn(wide_ref[...], act_ref[...]).astype(bf16)
        for k in range(count):
            pooled_ref[k, held] = pooled[k * POOLED : (k + 1) * POOLED]


def forward(arrays, w_in):
    count = len(arrays)
    hidden = w_in.shape[2]
    return call(
        forward_kernel,
        [
            shape_of(count, HELD, POOLED, hidden),
            shape_of(count, HELD, HALF, hidden),
        ],
        [*arrays, w_in],
        scratch=[
            pltpu.VMEM((count * POOLED, count * LANES), bf16),
            pltpu.VMEM((count * LANES, hidden), bf16),
        ],
    )


def pick_kernel(x2_ref, x4_ref, first_ref, second_ref):
    first_ref[...] = x2_ref[:HALF, :]
    second_ref[...] = x4_ref[HALF:, :]


def stack_kernel(first_ref, second_ref, out_ref):
    out_ref[:HALF, :] = first_ref[...]
    out_ref[HALF:, :] = second_ref[...]


PARTS = {0: (0, 0), 1: (1, 0), 2: (1, 1), 4: (1, 2), 3: (2, 0), 5: (2, 1), 6: (3, 0), 7: (3, 1)}


def part_of(parts, k):
    which, at = PARTS[k]
    return parts[which], at


def out_kernel(shift, *refs):
    parts, (w_out, out_ref) = refs[:4], refs[4:]
    total = None
    for held in range(HELD):
        rows = []
        for k in AROUND:
            ref, at = part_of(parts, k + shift)
            rows.append(ref[at, held])
        part = nn(jnp.concatenate(rows, axis=0), w_out[held])
        total = part if total is None else total + part
    out_ref[...] = total.astype(bf16).reshape(out_ref.shape)


def join_kernel(own_ref, got_ref, out_ref):
    for ahead in range(4):
        to = lax.rem(lax.axis_index("dp") // 2 + ahead, 4)
        out_ref[to] = (own_ref[ahead].astype(f32) + got_ref[ahead].astype(f32)).astype(bf16)


def mean_kernel(part_ref, sum_ref, out_ref):
    total = sum_ref[...]
    for first in range(0, part_ref.shape[0], 8):
        total = total + jnp.sum(part_ref[first : first + 8].astype(f32), axis=0)
    out_ref[...] = jnp.broadcast_to((total * (1.0 / PAIR_TOKENS))[None], out_ref.shape)


def split(x):
    high = x.astype(bf16)
    return high, (x - high.astype(f32)).astype(bf16)


def loss_kernel(own_ref, other_ref, w_out, grad_ref, rows_ref, prod_ref, gi_ref, gt_ref):
    image = jnp.concatenate([own_ref[0], other_ref[0]], axis=0)
    text = jnp.concatenate([own_ref[1], other_ref[1]], axis=0)
    pairs, width = image.shape
    scale = PAIR_TOKENS / math.sqrt(width)
    (i0, i1), (t0, t1) = split(image), split(text)
    logits = scale * (nt(i0, t0) + (nt(i0, t1) + nt(i1, t0)))

    def softmax(axis):
        top = jnp.exp(logits - jnp.max(logits, axis=axis, keepdims=True))
        return top / jnp.sum(top, axis=axis, keepdims=True)

    same = jnp.where(iota((pairs, pairs), 0) == iota((pairs, pairs), 1), 2.0, 0.0)
    grad_logits = (objective_scale * scale / PAIR_TOKENS) * (softmax(1) + softmax(0) - same)

    def thrice(g, x0, x1):
        g0, g1 = split(g)
        return nn(g0, x0) + (nn(g0, x1) + nn(g1, x0))

    grad_image = thrice(grad_logits, t0, t1)
    grad_text = thrice(grad_logits.T, i0, i1)
    grad_ref[0] = grad_image
    grad_ref[1] = grad_text
    gi_ref[...] = grad_image.astype(bf16)
    gt_ref[...] = grad_text.astype(bf16)
    for at, k in enumerate(AROUND):
        for other in range(2):
            first = other * 4 * PEERS + lax.rem(lax.axis_index("dp") // 2 + at, 4) * PEERS
            span = pl.ds(pl.multiple_of(first, PEERS), PEERS)
            rows_ref[k + other, :PEERS, :] = gi_ref[span, :]
            rows_ref[k + other, PEERS:, :] = gt_ref[span, :]
    rows = rows_ref[...].reshape(8 * POOLED, width)
    for held in range(HELD):
        prod_ref[held] = nt(rows, w_out[held]).astype(bf16)


def backward_kernel(blocks, *refs):
    count = len(blocks)
    seconds, slopes = refs[:count], refs[count : 2 * count]
    prod_ref, w_in, pre_ref = refs[2 * count : 2 * count + 3]
    outs, (wide_ref, prods_ref) = refs[2 * count + 3 : -2], refs[-2:]
    for held in range(HELD):
        pool_table(seconds, held, wide_ref)
        for k, block in enumerate(blocks):
            prods_ref[k * POOLED : (k + 1) * POOLED, :] = prod_ref[
                held, block * POOLED : (block + 1) * POOLED, :
            ]
        grad_act = tn(wide_ref[...], prods_ref[...])
        for k, block in enumerate(blocks):
            slope = slopes[k][PARTS[block][1], held].astype(f32)
            pre_ref[k, held] = (grad_act[k * LANES : k * LANES + HALF] * slope).astype(bf16)
        pre = jnp.concatenate([pre_ref[k, held] for k in range(count)], axis=0)
        part = nt(pre, w_in[held]).astype(bf16)
        for k in range(count):
            rows = part[k * HALF : (k + 1) * HALF]
            outs[k][held * HALF : (held + 1) * HALF, :] = rows


def backward(blocks, rows, made, prod, w_in):
    count = len(blocks)
    width, hidden = w_in.shape[1:]
    return call(
        functools.partial(backward_kernel, blocks),
        [shape_of(count, HELD, HALF, hidden)]
        + [shape_of(2 * HALF, width)] * count,
        [
            *[rows[block] for block in blocks],
            *[made[PARTS[block][0]][1] for block in blocks],
            prod,
            w_in,
        ],
        scratch=[
            pltpu.VMEM((count * POOLED, count * LANES), bf16),
            pltpu.VMEM((count * POOLED, hidden), bf16),
        ],
    )


PAIRED = {7: (0, 0), 6: (1, 0), 5: (1, 1), 4: (1, 2), 3: (1, 3), 2: (2, 0), 1: (2, 1), 0: (2, 2)}


def grads_kernel(*refs):
    rows, pres, parts, grads = refs[:8], refs[8:11], refs[11:15], refs[15]
    in_ref, out_ref, x_ref, p_ref = refs[16:]
    step = pl.program_id(0)
    width = in_ref.shape[1]

    def inner(held):
        for k in range(8):
            span = slice(k * HALF, (k + 1) * HALF)
            x_ref[span, :] = rows[k][held * HALF : (held + 1) * HALF, :]
            pair, at = PAIRED[k]
            p_ref[span, :] = pres[pair][at, held]
        in_ref[0] = tn(x_ref[...], p_ref[...])

    def outer(held):
        pooled = []
        for k in range(8):
            ref, at = part_of(parts, k)
            pooled.append(ref[at, held])
        out_ref[0] = tn(jnp.concatenate(pooled, axis=0), grads[...].reshape(8 * POOLED, width))

    for held in range(HELD):
        pl.when(step == held)(functools.partial(inner, held))
        pl.when(step == HELD + held)(functools.partial(outer, held))


def weight_grads(rows, pres, pooled, grads, width, hidden):
    whole = pl.BlockSpec(memory_space=pltpu.VMEM)
    return pl.pallas_call(
        grads_kernel,
        grid=(2 * HELD,),
        out_shape=[
            shape_of(HELD, width, hidden, dtype=f32),
            shape_of(HELD, hidden, width, dtype=f32),
        ],
        in_specs=[whole] * 16,
        out_specs=[
            pl.BlockSpec((1, width, hidden), lambda i: (jnp.minimum(i, HELD - 1), 0, 0)),
            pl.BlockSpec((1, hidden, width), lambda i: (jnp.maximum(i - HELD, 0), 0, 0)),
        ],
        scratch_shapes=[
            pltpu.VMEM((8 * HALF, width), bf16),
            pltpu.VMEM((8 * HALF, hidden), bf16),
        ],
        compiler_params=pltpu.CompilerParams(vmem_limit_bytes=30 * 1024 * 1024),
        cost_estimate=FREE,
    )(*rows, *pres, *pooled, grads)


def plus_kernel(own_ref, got_ref, first_ref, second_ref):
    total = (own_ref[...].astype(f32) + got_ref[...].astype(f32)).astype(bf16)
    first_ref[...] = total[:HALF]
    second_ref[...] = total[HALF:]


def turn_kernel(above_ref, low_ref, below_ref, high_ref, up_ref, down_ref):
    up_ref[...] = (above_ref[...].astype(f32) + low_ref[...].astype(f32)).astype(bf16)
    down_ref[...] = (below_ref[...].astype(f32) + high_ref[...].astype(f32)).astype(bf16)


def settle_kernel(own_ref, got_ref, la_ref, lb_ref, ha_ref, hb_ref, out_ref):
    width = own_ref.shape[1]
    total = own_ref[...].astype(f32) + got_ref[...].astype(f32)
    first = total[:HALF] + la_ref[...].astype(f32) + ha_ref[...].astype(f32)
    second = total[HALF:] + lb_ref[...].astype(f32) + hb_ref[...].astype(f32)
    rows = jnp.concatenate([first.astype(bf16), second.astype(bf16)], axis=0)
    out_ref[...] = nn(repack_table(2 * HALF, True), rows).astype(bf16).reshape(PEERS, PAD, width)


def tail_kernel(ids_ref, slots_ref, tok_ref, gain_ref, grads_ref, back_ref, out_ref):
    at = (lax.axis_index("dp") // 2) * PEERS + lax.axis_index("expert")
    near = pl.ds(pl.multiple_of(at // 8 * 8, 8), 8)
    width = tok_ref.shape[1]
    tokens = tok_ref.shape[0]
    back = back_ref[...].reshape(PEERS * PAD, width)
    grad_normed = tn(slot_table(places(ids_ref, slots_ref)), back)
    unit, scale = normal_parts(tok_ref[...].astype(f32))
    grad = grad_normed * gain_ref[...].reshape(1, -1)
    grad = scale * (
        grad
        - jnp.mean(grad, axis=-1, keepdims=True)
        - unit * jnp.mean(grad * unit, axis=-1, keepdims=True)
    )
    for half in range(2):
        span = slice(half * (tokens // 2), (half + 1) * (tokens // 2))
        rows = grads_ref[half, near, :]
        own = jnp.where(iota(rows.shape, 0) == at % 8, rows, 0.0)
        own = jnp.sum(own, axis=0, keepdims=True)
        out_ref[span, :] = (own + grad[span]).astype(bf16)


def body(tokens, expert_ids, slots, ln_gain, w_in, w_out):
    width, hidden = w_in.shape[1:]
    row_count = tokens.shape[1] * tokens.shape[2]
    flat = tokens.reshape(row_count, width)
    ids, slot = expert_ids[0], slots[0]
    everyone = ("dp", "expert")
    chips = 4 * PEERS
    cores = [[d * PEERS + e for d in range(c, 8, 2) for e in range(PEERS)] for c in range(2)]

    def up(x):
        return lax.ppermute(x, "dp", [(i, (i + 2) % 8) for i in range(8)])

    def down(x):
        return lax.ppermute(x, "dp", [(i, (i + 6) % 8) for i in range(8)])

    def swap(x):
        return lax.ppermute(x, "dp", [(i, i ^ 1) for i in range(8)])

    def after(x, *tokens):
        return lax.optimization_barrier((x, *tokens))[0]

    def exchange(x):
        return lax.all_to_all(x, "expert", split_axis=0, concat_axis=0, tiled=True)

    def spread(x):
        return lax.all_to_all(
            x, everyone, split_axis=0, concat_axis=0, tiled=True, axis_index_groups=cores
        )

    sent, token_sum = call(
        dispatch_kernel,
        [shape_of(PEERS, PAD, width), shape_of(2, width, dtype=f32)],
        [ids, slot, flat, ln_gain],
        hbm=(0, 1, 2, 3),
        scratch=input_scratch(row_count, width),
        vmem=60,
    )
    rows_shape = shape_of(2 * HALF + KIND_ROWS, width)
    x0 = call(repack_kernel, rows_shape, [exchange(sent)])
    x2, x4, x1 = up(x0), down(x0), swap(x0)
    made = [forward([x0], w_in)]
    first, second = call(
        pick_kernel,
        [shape_of(HALF, width), shape_of(HALF + KIND_ROWS, width)],
        [after(x2, made[0][0]), x4],
    )
    a6, b6 = up(first), down(second)
    made.append(forward([x1, after(x2, first), x4], w_in))
    x3, x5 = swap(after(x2, made[1][0])), swap(after(x4, made[1][0]))
    x6 = call(stack_kernel, rows_shape, [after(a6, made[1][0]), b6])
    x7 = swap(x6)
    made.append(forward([after(x3, x6), x5], w_in))
    made.append(forward([x6, after(x7, made[2][0])], w_in))
    pooled = [m[0] for m in made]
    block_rows = [x0, x1, x2, x3, x4, x5, x6, x7]

    def product(shift, w_out):
        return call(
            functools.partial(out_kernel, shift),
            shape_of(4, POOLED, width),
            [*pooled, w_out],
        )

    other = product(1, w_out)
    got = swap(other)
    own = product(0, after(w_out, other))
    joined = call(join_kernel, shape_of(4, POOLED, width), [own, after(got, own)])
    joined = joined.reshape(4, 2, PEERS, width).transpose(0, 2, 1, 3).reshape(chips, 2, width)
    emb = call(
        mean_kernel, shape_of(chips, 2, width, dtype=f32), [spread(joined), token_sum]
    )
    emb = spread(emb).transpose(1, 0, 2)
    grad_pooled, rows, prod = call(
        loss_kernel,
        [
            shape_of(2, 8 * PEERS, width, dtype=f32),
            shape_of(8, POOLED, width),
            shape_of(HELD, 8 * POOLED, hidden),
        ],
        [emb, swap(emb), w_out],
        scratch=[pltpu.VMEM((8 * PEERS, width), bf16), pltpu.VMEM((8 * PEERS, width), bf16)],
    )

    def plus(x, y):
        return call(plus_kernel, [shape_of(HALF, width)] * 2, [x, y])

    half = shape_of(HALF, width)
    pre7, p7 = backward((7,), block_rows, made, prod, w_in)
    s7 = swap(p7)
    pre6543, p6, p5, p4, p3 = backward(
        (6, 5, 4, 3), block_rows, made, after(prod, p7), w_in
    )
    s5, s3 = swap(p5), swap(p3)
    r6a, r6b = plus(p6, s7)
    from_below, from_above = up(r6a), down(r6b)
    pre210, p2, p1, p0 = backward((2, 1, 0), block_rows, made, after(prod, r6a), w_in)
    s1 = swap(p1)
    r4a, r4b = plus(p4, after(s5, p2))
    r2a, r2b = plus(p2, s3)
    low_b, high_a = up(r4b), down(r2a)
    low_a, high_b = call(
        turn_kernel, [half, half], [r4a, from_below, r2b, from_above], cost=DEAR
    )
    grad_w_in, grad_w_out = weight_grads(
        block_rows, [pre7, pre6543, after(pre210, low_a)], pooled, rows, width, hidden
    )
    low_a, high_b = up(low_a), down(high_b)
    settled = call(
        settle_kernel,
        shape_of(PEERS, PAD, width),
        [after(p0, grad_w_in), s1, low_a, low_b, high_a, high_b],
    )
    grad_flat = call(
        tail_kernel,
        shape_of(row_count, width),
        [ids, slot, flat, ln_gain, grad_pooled, exchange(settled)],
    )
    return (grad_flat.reshape(tokens.shape), grad_w_in, grad_w_out)


def solution(mesh):
    placed = (
        P(("dp", "expert"), None, None, None),
        P(("dp", "expert"), None, None),
        P(("dp", "expert"), None, None),
        P(),
        P("expert", None, "dp"),
        P("expert", "dp", None),
    )
    return jax.shard_map(
        body,
        mesh=mesh,
        in_specs=placed,
        out_specs=(
            P(("dp", "expert"), None, None, None),
            P("expert", None, "dp"),
            P("expert", "dp", None),
        ),
        check_vma=False,
    )
```
